128 devices in a mesh: shard: 8 (over z_lo, y), ctx: 16 (over x, z_hi, core).
Axes of the slice: x: 4, y: 4, z: 4 (z_hi: 2, z_lo: 2; z = z_hi * 2 + z_lo), core: 2. Of those that a mesh axis runs over, the one named last changes fastest.
Arguments:
- tokens: bfloat16 [32768, 960], P(('shard', 'ctx')), may hold values from -6 to 6
- w_query: bfloat16 [960, 960], P('shard', 'ctx'), may hold values from -0.1875 to 0.1875
- w_key: bfloat16 [960, 320], P('shard', 'ctx'), may hold values from -0.1875 to 0.1875
- w_value: bfloat16 [960, 320], P('shard', 'ctx'), may hold values from -0.1875 to 0.1875
- w_out: bfloat16 [960, 960], P('shard', 'ctx'), may hold values from -1.5 to 1.5
- w_gate: bfloat16 [960, 2560], P('shard', 'ctx'), may hold values from -0.1875 to 0.1875
- w_up: bfloat16 [960, 2560], P('shard', 'ctx'), may hold values from -0.1875 to 0.1875
- w_down: bfloat16 [2560, 960], P('shard', 'ctx'), may hold values from -0.125 to 0.125
- attention_norm_gain: float32 [960], replicated, may hold values from 0.1 to 1.9
- feedforward_norm_gain: float32 [960], replicated, may hold values from 0.1 to 1.9
- span_order: int32 [8, 32], P('shard'), may hold values from 0 to 31, as said below
- positions: int32 [8, 4096], P('shard'), may hold values from 0 to 8191, as said below
- out_grad: bfloat16 [32768, 960], P(('shard', 'ctx')), may hold values from -6 to 6
Outputs:
- output: bfloat16 [32768, 960], P(('shard', 'ctx'))
- input_grad: bfloat16 [32768, 960], P(('shard', 'ctx'))
- grad_query: float32 [960, 960], P('shard', 'ctx')
- grad_key: float32 [960, 320], P('shard', 'ctx')
- grad_value: float32 [960, 320], P('shard', 'ctx')
- grad_out: float32 [960, 960], P('shard', 'ctx')
- grad_gate: float32 [960, 2560], P('shard', 'ctx')
- grad_up: float32 [960, 2560], P('shard', 'ctx')
- grad_down: float32 [2560, 960], P('shard', 'ctx')
- grad_norm_attn: float32 [960], replicated
- grad_norm_mlp: float32 [960], replicated
The draws below stay inside these ranges and needn't reach their ends.
Inputs may be any that keep to these rules, and one draw needn't show every extreme that they name: `span_order`: each row is a permutation of the 32 blocks of one sequence; ctx index c holds blocks row[2c] then row[2c + 1], and row[2c] + row[2c + 1] = 31. `positions`: each row starts at 0, rises strictly by 1 to 3 from one token to the next, and ends at 8191.
All inputs are finite; a program needn't handle non-finite values.
Results may differ from the reference program's by a relative error of at most 0.028.
Values may be sent and summed in bfloat16 or wider, within the bound.
No kernel may reach another device: no remote copies, remote signals or barrier semaphores. Data moves between devices by JAX's collectives and lax.ppermute only.
A program may use at most 256 MiB of HBM per device.

```python
import jax
import jax.numpy as jnp
from jax import lax

D = 960
HEADS = 15
KV_HEADS = 5
HEAD_DIM = 64
FF = 2560
TOK_DEV = 256
SPAN = 128
NCHUNK = 32
SEQ_LEN = 4096
SEQS = 8
TOKENS = 32768


def draw_span_order(key, part):
    key = jax.random.fold_in(key, 7)
    row_keys = jax.random.split(key, SEQS)

    def one_row(row_key):
        pair_key, flip_key = jax.random.split(row_key)
        pair = jax.random.permutation(pair_key, NCHUNK // 2)
        flip = jax.random.randint(flip_key, (NCHUNK // 2,), 0, 2)
        mirror = NCHUNK - 1 - pair
        first = jnp.where(flip == 1, mirror, pair)
        second = jnp.where(flip == 1, pair, mirror)
        return jnp.stack([first, second], axis=1).reshape(NCHUNK)
    return jax.vmap(one_row)(row_keys).astype(jnp.int32)


def draw_positions(key, part):
    key = jax.random.fold_in(key, 13)
    offsets = jax.random.randint(key, (SEQS, SEQ_LEN), 0, 2)
    column = jnp.arange(SEQ_LEN, dtype=jnp.int32)[None, :]
    offsets = jnp.where(column == 0, 0, offsets)
    offsets = jnp.where(column == SEQ_LEN - 1, 1, offsets)
    return (2 * column + offsets).astype(jnp.int32)


def level_of(own_key, extent, cuts, least, top_value):
    level = 1.0
    for axis_at, parts in cuts:
        steps = jax.random.uniform(jax.random.fold_in(jax.random.fold_in(own_key, 6), axis_at), (parts,), jnp.float32, least / len(cuts), top_value / len(cuts))
        level = level * jnp.repeat(jnp.exp(steps), extent[axis_at] // parts).reshape((-1,) + (1,) * (len(extent) - 1 - axis_at))
    return level


def centred(stream_key, extent, spread, most, shards=(), held_as=jnp.bfloat16):
    array = jax.random.normal(stream_key, extent, jnp.float32) * spread
    if len(shards) > 0:
        array = level_of(stream_key, extent, shards, -0.22, 0.18) * array
    return jnp.clip(array, min=-most, max=most).astype(held_as)


def setup_inputs(seed: int = 0) -> dict:
    arg_keys = jax.random.split(jax.random.key(seed), 14)
    tokens = centred(arg_keys[0], (TOKENS, D), 1.0, 6.0, ((0, 128),))
    w_query = centred(arg_keys[1], (D, D), D ** -0.5, 0.1875, ((0, 8), (1, 16)))
    w_key = centred(arg_keys[2], (D, KV_HEADS * HEAD_DIM), D ** -0.5, 0.1875, ((0, 8), (1, 16)))
    w_value = centred(arg_keys[3], (D, KV_HEADS * HEAD_DIM), D ** -0.5, 0.1875, ((0, 8), (1, 16)))
    w_out = centred(arg_keys[4], (D, D), (D // 64) ** -0.5, 1.5, ((0, 8), (1, 16)))
    w_gate = centred(arg_keys[5], (D, FF), D ** -0.5, 0.1875, ((0, 8), (1, 16)))
    w_up = centred(arg_keys[6], (D, FF), D ** -0.5, 0.1875, ((0, 8), (1, 16)))
    w_down = centred(arg_keys[7], (FF, D), FF ** -0.5, 0.125, ((0, 8), (1, 16)))
    attention_norm_gain = jnp.clip(1.0 + 0.18 * jax.random.normal(arg_keys[8], (D,), jnp.float32), 0.1, 1.9)
    feedforward_norm_gain = jnp.clip(1.0 + 0.18 * jax.random.normal(arg_keys[9], (D,), jnp.float32), 0.1, 1.9)
    span_order = draw_span_order(jax.random.fold_in(arg_keys[13], 71), 0)
    positions = draw_positions(jax.random.fold_in(arg_keys[13], 71), 0)
    out_grad = centred(arg_keys[12], (TOKENS, D), 1.0, 6.0, ((0, 128),))
    return dict(tokens=tokens, w_query=w_query, w_key=w_key, w_value=w_value, w_out=w_out, w_gate=w_gate, w_up=w_up, w_down=w_down, attention_norm_gain=attention_norm_gain, feedforward_norm_gain=feedforward_norm_gain, span_order=span_order, positions=positions, out_grad=out_grad)


EPS = 1e-05
ROPE_BASE = 100000.0

@jax.custom_vjp
def low(v):
    return lax.optimization_barrier(v.astype(jnp.bfloat16)).astype(jnp.float32)

@jax.custom_vjp
def low_back(v):
    return v

def low_keep(v):
    return (low(v), None)

def low_pass(kept, grad):
    return (grad,)

def back_keep(v):
    return (v, None)

def back_low(kept, grad):
    return (low(grad),)
low.defvjp(low_keep, low_pass)
low_back.defvjp(back_keep, back_low)

def highdot(left, right):
    return jnp.dot(left, right, precision=lax.Precision.HIGHEST, preferred_element_type=jnp.float32)

def rms_scale(value, gain):
    return value * lax.rsqrt(lax.optimization_barrier(jnp.mean(value * value, axis=-1, keepdims=True)) + EPS) * gain

def rotate(value, where_at):
    half_dim = value.shape[-1] // 2
    freq = jnp.power(ROPE_BASE, -jnp.arange(half_dim, dtype=jnp.float32) / half_dim)
    angle = where_at.astype(jnp.float32)[:, None] * freq[None, :]
    cosine = jnp.cos(angle)[:, None, :]
    sine = jnp.sin(angle)[:, None, :]
    first = value[..., :half_dim]
    second = value[..., half_dim:]
    return jnp.concatenate([first * cosine - second * sine, second * cosine + first * sine], axis=-1)

def attend_block(query_block, keys, values, query_index, key_index):
    count = query_block.shape[0]
    grouped = query_block.reshape(count, KV_HEADS, HEADS // KV_HEADS, HEAD_DIM)
    scale = HEAD_DIM ** (-0.5)
    scores = low_back(jnp.einsum('qgrd,kgd->qgrk', grouped, keys, precision=lax.Precision.HIGHEST) * scale)
    allowed = key_index[None, :] <= query_index[:, None]
    expo = jnp.where(allowed[:, None, None, :], jnp.exp(scores), 0.0)
    total = lax.optimization_barrier(jnp.sum(expo, axis=-1))
    numer = low_back(jnp.einsum('qgrk,kgd->qgrd', low(expo), values, precision=lax.Precision.HIGHEST))
    return (numer / total[..., None]).reshape(count, HEADS * HEAD_DIM)

def forward(layer_input_rows, wq, wk, wv, wo, wg, wu, wd, gain_attn, gain_mlp, place, index):
    count = layer_input_rows.shape[0]
    first_normed_rows = low(rms_scale(layer_input_rows, gain_attn))
    query = low_back(highdot(first_normed_rows, wq))
    key_lin = low_back(highdot(first_normed_rows, wk))
    value = low(low_back(highdot(first_normed_rows, wv)))
    query_rot = low(rotate(query.reshape(count, HEADS, HEAD_DIM), place))
    key_rot = low(rotate(key_lin.reshape(count, KV_HEADS, HEAD_DIM), place))
    key_seq = key_rot.reshape(SEQS, SEQ_LEN, KV_HEADS, HEAD_DIM)
    value_seq = value.reshape(SEQS, SEQ_LEN, KV_HEADS, HEAD_DIM)
    index_seq = index.reshape(SEQS, SEQ_LEN)
    block = min(512, SEQ_LEN)
    blocks = count // block

    def one_block(number):
        seq = number * block // SEQ_LEN
        query_block = lax.dynamic_slice_in_dim(query_rot, number * block, block, 0)
        query_index = lax.dynamic_slice_in_dim(index, number * block, block, 0)
        return attend_block(query_block, key_seq[seq], value_seq[seq], query_index, index_seq[seq])
    attended = lax.map(jax.checkpoint(one_block), jnp.arange(blocks, dtype=jnp.int32)).reshape(count, D)
    attended = low(low_back(attended))
    first_hidden_rows = layer_input_rows + low_back(highdot(attended, wo))
    second_normed_rows = low(rms_scale(first_hidden_rows, gain_mlp))
    gate = low_back(highdot(second_normed_rows, wg))
    upward = low_back(highdot(second_normed_rows, wu))
    active = low(jax.nn.silu(gate) * upward)
    return first_hidden_rows + highdot(active, wd)

def reference(tokens, w_query, w_key, w_value, w_out, w_gate, w_up, w_down, attention_norm_gain, feedforward_norm_gain, span_order, positions, out_grad):
    stored = jnp.arange(SEQ_LEN, dtype=jnp.int32)
    device = stored // TOK_DEV
    within = stored % TOK_DEV
    slot = 2 * device + within // SPAN
    spans = span_order[:, slot]
    index = (spans * SPAN + (within % SPAN)[None, :]).astype(jnp.int32)
    place = jnp.take_along_axis(positions, index, axis=1)
    index_flat = index.reshape(TOKENS)
    place_flat = place.reshape(TOKENS)
    floats = (tokens.astype(jnp.float32), w_query.astype(jnp.float32), w_key.astype(jnp.float32), w_value.astype(jnp.float32), w_out.astype(jnp.float32), w_gate.astype(jnp.float32), w_up.astype(jnp.float32), w_down.astype(jnp.float32), attention_norm_gain.astype(jnp.float32), feedforward_norm_gain.astype(jnp.float32))

    def run(*values):
        return forward(*values, place_flat, index_flat)
    result, pull = jax.vjp(run, *floats)
    grads = pull(out_grad.astype(jnp.float32))
    return (result.astype(jnp.bfloat16), grads[0].astype(jnp.bfloat16), grads[1], grads[2], grads[3], grads[4], grads[5], grads[6], grads[7], grads[8], grads[9])
```

```python
import jax
import jax.numpy as jnp
from jax import lax
from jax.experimental import pallas as pl
from jax.experimental.pallas import tpu as pltpu
from jax.sharding import Mesh
from jax.sharding import PartitionSpec as P

D = 960
HEADS = 15
KV_HEADS = 5
GROUP = 3
HEAD_DIM = 64
SPAN = 128
PAD = 1024

EPS = 1e-05
ROPE_BASE = 100000.0

BF = jnp.bfloat16
F32 = jnp.float32

PLANE = ("y", "x")
LINE = ("zh", "zl")
CHIPS = ("zl", "y", "x", "zh")
SEQ = ("x", "zh")
SWAP = [(0, 1), (1, 0)]


def pad_width(value):
    rows = value.shape[0]
    blocks = value.reshape(rows, 8, 120)
    return jnp.pad(blocks, ((0, 0), (0, 0), (0, 8))).reshape(rows, PAD)


def cut_width(value):
    rows = value.shape[0]
    return value.reshape(rows, 8, 128)[:, :, :120].reshape(rows, D)


def pad_lanes(value):
    return jnp.pad(value, ((0, 0), (0, 128 - value.shape[1])))


def other_core(value):
    return lax.ppermute(value, "c", SWAP)


def dot_last(left, right):
    return lax.dot_general(left, right, (((1,), (1,)), ((), ())), preferred_element_type=F32)


def dot_first(left, right):
    return lax.dot_general(left, right, (((0,), (0,)), ((), ())), preferred_element_type=F32)


def dot_plain(left, right):
    return jnp.dot(left, right, preferred_element_type=F32)


def key_rows_minus_query_lanes():
    row = lax.broadcasted_iota(jnp.int32, (SPAN, GROUP * SPAN), 0)
    lane = lax.broadcasted_iota(jnp.int32, (SPAN, GROUP * SPAN), 1)
    return row - lax.rem(lane, SPAN)


def second_tile(info, device):
    low = info[24 + device]
    mine = info[1]
    takes_low = low <= mine
    low_slot = info[8 + device]
    high_slot = 4 * device + 1 - low_slot
    slot = jnp.where(takes_low, low_slot, high_slot)
    half = jnp.where(takes_low, info[0], 1 - info[0])
    limit = jnp.where(low == mine, 0, SPAN)
    return slot, half, limit


def key_block(ref, slot):
    return ref[pl.ds(pl.multiple_of(slot * SPAN, SPAN), SPAN), :]


def attend_kernel(info, kv_ref, q_ref, out_ref, total_ref, query, numer, total):
    width = GROUP * SPAN
    query[...] = jnp.zeros_like(query)
    for half in range(2):
        query[half, :HEAD_DIM, :] = q_ref[0, half]
    numer[...] = jnp.zeros_like(numer)
    total[...] = jnp.zeros_like(total)
    diff = key_rows_minus_query_lanes()

    def add(half, keys, expo):
        numer[half] += dot_first(keys, expo.astype(BF))
        total[half] += jnp.sum(expo.reshape(expo.shape[0] // 8, 8, width), axis=0)

    def some(step, carry):
        high = 1 - info[0]
        keys = jnp.concatenate([key_block(kv_ref, info[8 + 4 * step + n]) for n in range(4)], axis=0)
        add(high, keys, jnp.exp(dot_plain(keys, query[high])))
        for n in range(4):
            slot, half, limit = second_tile(info, 4 * step + n)
            keys = key_block(kv_ref, slot)
            expo = jnp.exp(dot_plain(keys, query[half]))
            add(half, keys, jnp.where(diff <= limit, expo, 0.0))
        return carry

    lax.fori_loop(0, 4, some, 0)
    high = 1 - info[0]
    own = info[2]
    keys = key_block(kv_ref, 4 * own + 1 - info[8 + own])
    expo = jnp.exp(dot_plain(keys, query[high]))
    add(high, keys, jnp.where(diff <= 0, expo, 0.0))
    for half in range(2):
        summed = jnp.sum(total[half], axis=0, keepdims=True)
        total_ref[0, half] = summed
        out_ref[0, half] = numer[half, HEAD_DIM:, :] / summed


def attend(info, kv, query):
    width = GROUP * SPAN
    return pl.pallas_call(
        attend_kernel,
        grid_spec=pltpu.PrefetchScalarGridSpec(
            num_scalar_prefetch=1,
            grid=(KV_HEADS,),
            in_specs=[
                pl.BlockSpec((kv.shape[0], 2 * HEAD_DIM), lambda g, s: (0, g)),
                pl.BlockSpec((1, 2, HEAD_DIM, width), lambda g, s: (g, 0, 0, 0)),
            ],
            out_specs=[
                pl.BlockSpec((1, 2, HEAD_DIM, width), lambda g, s: (g, 0, 0, 0)),
                pl.BlockSpec((1, 2, 1, width), lambda g, s: (g, 0, 0, 0)),
            ],
            scratch_shapes=[
                pltpu.VMEM((2, 2 * HEAD_DIM, width), BF),
                pltpu.VMEM((2, 2 * HEAD_DIM, width), F32),
                pltpu.VMEM((2, 8, width), F32),
            ],
        ),
        out_shape=[
            jax.ShapeDtypeStruct((KV_HEADS, 2, HEAD_DIM, width), F32),
            jax.ShapeDtypeStruct((KV_HEADS, 2, 1, width), F32),
        ],
        compiler_params=pltpu.CompilerParams(vmem_limit_bytes=48 * 1024 * 1024),
        cost_estimate=pl.CostEstimate(flops=4 * 10**9, bytes_accessed=8 * 10**6, transcendentals=8 * 10**6),
    )(info, kv, query)


def attend_back_kernel(info, kv_ref, q_ref, dnum_ref, delta_ref, dq_ref, dkv_ref, wide, tall, dq, dkv):
    width = GROUP * SPAN
    for half in range(2):
        zero = jnp.zeros((HEAD_DIM, width), BF)
        both = jnp.concatenate(
            [
                jnp.concatenate([q_ref[0, half], zero], axis=1),
                jnp.concatenate([zero, dnum_ref[0, half]], axis=1),
            ],
            axis=0,
        )
        wide[half] = both
        tall[half] = both.T
    dq[...] = jnp.zeros_like(dq)
    dkv[...] = jnp.zeros_like(dkv)
    diff = key_rows_minus_query_lanes()

    def tile(half, slot, limit):
        keys = key_block(kv_ref, slot)
        scores = dot_plain(keys, wide[half])
        expo = jnp.exp(scores[:, :width])
        if limit is not None:
            expo = jnp.where(diff <= limit, expo, 0.0)
        grads = (expo * (scores[:, width:] - delta_ref[0, half])).astype(BF)
        pair = jnp.concatenate([grads, expo.astype(BF)], axis=1)
        at = pl.ds(pl.multiple_of(slot * SPAN, SPAN), SPAN)
        dkv[at, :] += dot_plain(pair, tall[half])
        dq[half] += dot_first(keys, grads)

    def some(step, carry):
        for n in range(2):
            device = 2 * step + n
            tile(1 - info[0], info[8 + device], None)
            slot, half, limit = second_tile(info, device)
            tile(half, slot, limit)
        return carry

    lax.fori_loop(0, 8, some, 0)
    own = info[2]
    tile(1 - info[0], 4 * own + 1 - info[8 + own], 0)
    for half in range(2):
        dq_ref[0, half] = dq[half, :HEAD_DIM, :] * (HEAD_DIM**-0.5)
    dkv_ref[...] = dkv[...].astype(BF)


def attend_back(info, kv, query, dnum, delta):
    width = GROUP * SPAN
    rows = kv.shape[0]
    head = pl.BlockSpec((1, 2, HEAD_DIM, width), lambda g, s: (g, 0, 0, 0))
    return pl.pallas_call(
        attend_back_kernel,
        grid_spec=pltpu.PrefetchScalarGridSpec(
            num_scalar_prefetch=1,
            grid=(KV_HEADS,),
            in_specs=[
                pl.BlockSpec((rows, 2 * HEAD_DIM), lambda g, s: (0, g)),
                head,
                head,
                pl.BlockSpec((1, 2, 1, width), lambda g, s: (g, 0, 0, 0)),
            ],
            out_specs=[head, pl.BlockSpec((rows, 2 * HEAD_DIM), lambda g, s: (0, g))],
            scratch_shapes=[
                pltpu.VMEM((2, 2 * HEAD_DIM, 2 * width), BF),
                pltpu.VMEM((2, 2 * width, 2 * HEAD_DIM), BF),
                pltpu.VMEM((2, 2 * HEAD_DIM, width), F32),
                pltpu.VMEM((rows, 2 * HEAD_DIM), F32),
            ],
        ),
        out_shape=[
            jax.ShapeDtypeStruct((KV_HEADS, 2, HEAD_DIM, width), F32),
            jax.ShapeDtypeStruct((rows, KV_HEADS * 2 * HEAD_DIM), BF),
        ],
        compiler_params=pltpu.CompilerParams(vmem_limit_bytes=48 * 1024 * 1024),
        cost_estimate=pl.CostEstimate(flops=10 * 10**9, bytes_accessed=12 * 10**6, transcendentals=8 * 10**6),
    )(info, kv, query, dnum, delta)


def by_half(value):
    split = value.reshape(KV_HEADS, GROUP, HEAD_DIM, 2, SPAN)
    return split.transpose(0, 3, 2, 1, 4).reshape(KV_HEADS, 2, HEAD_DIM, GROUP * SPAN)


def by_head(value):
    rows = value.shape[2]
    split = value.reshape(KV_HEADS, 2, rows, GROUP, SPAN)
    return split.transpose(0, 3, 2, 1, 4).reshape(HEADS, rows, 2 * SPAN)


def rotate(value, cosine, sine):
    first, second = value[:, :32], value[:, 32:]
    return jnp.concatenate([first * cosine - second * sine, second * cosine + first * sine], axis=1)


def unrotate(value, cosine, sine):
    first, second = value[:, :32], value[:, 32:]
    return jnp.concatenate([first * cosine + second * sine, second * cosine - first * sine], axis=1)


def norm_forward(value, gain):
    inverse = lax.rsqrt(jnp.sum(value * value, axis=-1, keepdims=True) / D + EPS)
    unit = value * inverse
    return unit, inverse, (unit * gain).astype(BF)


def norm_back(grad, unit, inverse, gain):
    scaled = grad * gain
    inner = jnp.sum(scaled * unit, axis=-1, keepdims=True) / D
    return inverse * (scaled - unit * inner), jnp.sum(grad * unit, axis=0)


def body(
    tokens,
    w_query,
    w_key,
    w_value,
    w_out,
    w_gate,
    w_up,
    w_down,
    attention_norm_gain,
    feedforward_norm_gain,
    span_order,
    positions,
    out_grad,
):
    rows = tokens.shape[0]
    core = lax.axis_index("c")
    me = lax.axis_index(("x", "zh", "c"))

    mixed = jnp.concatenate([w_down.reshape(2, 160, 60), w_out.reshape(2, 60, 60)], axis=1)
    mixed = lax.all_to_all(mixed, "c", 0, 0, tiled=True)
    mixed = jnp.concatenate([mixed[0], mixed[1]], axis=1)
    big = jnp.concatenate([w_gate.T, w_up.T, mixed], axis=0)
    big = jnp.pad(pad_lanes(big), ((0, 4), (0, 0)))
    big = lax.all_gather(big, LINE, axis=0, tiled=True)
    big = lax.all_gather(big, PLANE, axis=0, tiled=True).reshape(4, 4, 2, 2, 544, 128)

    small = pad_lanes(jnp.concatenate([w_query.T, w_key.T, w_value.T], axis=0))
    small = lax.all_to_all(jnp.broadcast_to(small, (64, 100, 128)), CHIPS, 0, 0, tiled=True)
    small = lax.all_to_all(jnp.broadcast_to(small, (2, 64, 100, 128)), "c", 0, 0, tiled=True)
    small = small.reshape(2, 2, 4, 4, 2, 100, 128).transpose(3, 4, 0, 5, 1, 2, 6)
    w_q = small[:, :, :, :60].reshape(D, PAD)
    w_k = small[:, :, :, 60:80].reshape(KV_HEADS, HEAD_DIM, PAD)
    w_v = small[:, :, :, 80:].reshape(KV_HEADS, HEAD_DIM, PAD)
    w_kv = jnp.concatenate([w_k, w_v], axis=1).reshape(2 * KV_HEADS * HEAD_DIM, PAD)
    w_qkv = jnp.concatenate([w_q, w_kv], axis=0)

    order = span_order[0]
    pairs = order.reshape(16, 2)
    low_half = (pairs[:, 0] > pairs[:, 1]).astype(jnp.int32)
    low_span = jnp.minimum(pairs[:, 0], pairs[:, 1])
    own_pair = lax.dynamic_slice_in_dim(order, 2 * me, 2)
    own_low_half = (own_pair[0] > own_pair[1]).astype(jnp.int32)
    head_info = jnp.stack([own_low_half, jnp.minimum(own_pair[0], own_pair[1]), me.astype(jnp.int32)])
    info = jnp.concatenate(
        [
            head_info,
            jnp.zeros((5,), jnp.int32),
            2 * jnp.arange(16, dtype=jnp.int32) + low_half,
            low_span,
        ]
    ).astype(jnp.int32)
    place = jnp.concatenate(
        [
            lax.dynamic_slice_in_dim(positions[0], own_pair[0] * SPAN, SPAN, 0),
            lax.dynamic_slice_in_dim(positions[0], own_pair[1] * SPAN, SPAN, 0),
        ]
    )
    half_dim = HEAD_DIM // 2
    freq = jnp.power(ROPE_BASE, -jnp.arange(half_dim, dtype=F32) / half_dim)
    angle = freq[:, None] * place.astype(F32)[None, :]
    cosine, sine = jnp.cos(angle), jnp.sin(angle)

    gain_one = pad_width(attention_norm_gain[None])
    gain_two = pad_width(feedforward_norm_gain[None])
    layer_input = pad_width(tokens).astype(F32)
    dy = pad_width(out_grad)
    dy_both = jnp.concatenate([dy, other_core(dy)], axis=0)

    unit_one, inverse_one, normed_one = norm_forward(layer_input, gain_one)
    qkv = dot_last(w_qkv, normed_one)
    query = rotate(qkv[:D].reshape(HEADS, HEAD_DIM, rows), cosine, sine).astype(BF)
    key_value = qkv[D:].reshape(KV_HEADS, 2, HEAD_DIM, rows)
    key = rotate(key_value[:, 0], cosine, sine).astype(BF)
    kv_local = jnp.stack([key, key_value[:, 1].astype(BF)], axis=1)
    kv_local = kv_local.reshape(2 * KV_HEADS * HEAD_DIM, rows).T
    query = by_half(query.reshape(D, rows) * BF(HEAD_DIM**-0.5))

    kv = lax.all_to_all(jnp.broadcast_to(kv_local, (8, rows, 640)), SEQ, 0, 0, tiled=True)
    kv = lax.all_to_all(jnp.broadcast_to(kv, (2, 8, rows, 640)), "c", 0, 0, tiled=True)
    kv = kv.transpose(1, 0, 2, 3).reshape(16 * rows, 640)

    attended, total = attend(info, kv, query)
    attended = by_head(attended)
    total = by_head(total)
    attended_low = attended.astype(BF).reshape(D, rows)

    w_gate_t = big[:, :, :, :, :160].transpose(1, 2, 4, 3, 0, 5).reshape(1280, PAD)
    w_up_t = big[:, :, :, :, 160:320].transpose(1, 2, 4, 3, 0, 5).reshape(1280, PAD)
    w_down_h = big[:, :, :, :, 320:480].transpose(3, 0, 4, 1, 2, 5).reshape(1280, PAD)
    w_out_h = big[:, :, :, :, 480:540].transpose(3, 0, 4, 1, 2, 5).reshape(8, 60, PAD)
    w_out_o = other_core(w_out_h)
    first = core == 0
    w_out_full = jnp.stack(
        [jnp.where(first, w_out_h, w_out_o), jnp.where(first, w_out_o, w_out_h)], axis=1
    ).reshape(D, PAD)

    hidden = layer_input + dot_first(attended_low, w_out_full)
    unit_two, inverse_two, normed_two = norm_forward(hidden, gain_two)
    normed_both = jnp.concatenate([normed_two, other_core(normed_two)], axis=0)
    gate = dot_last(normed_both, w_gate_t)
    upward = dot_last(normed_both, w_up_t)
    sigma = jax.nn.sigmoid(gate)
    silu_gate = gate * sigma
    active = (silu_gate * upward).astype(BF)
    dact = dot_last(dy_both, w_down_h)
    dgate = (dact * upward * sigma * (1.0 + gate * (1.0 - sigma))).astype(BF)
    dup = (dact * silu_gate).astype(BF)
    dn_two = dot_plain(dgate, w_gate_t) + dot_plain(dup, w_up_t)
    dn_two = dn_two[:rows] + other_core(dn_two[rows:].astype(BF)).astype(F32)
    fed = dot_plain(active, w_down_h)
    fed = fed[:rows] + other_core(fed[rows:].astype(BF)).astype(F32)
    result = cut_width((hidden + fed).astype(BF))

    back_two, gain_two_grad = norm_back(dn_two, unit_two, inverse_two, gain_two)
    dh = dy.astype(F32) + back_two
    dh_low = dh.astype(BF)
    dob = dot_last(w_out_full, dh_low).astype(BF).reshape(HEADS, HEAD_DIM, rows)
    dob = dob.astype(F32)
    dnum = (dob / total).astype(BF)
    delta = jnp.sum(dob * attended, axis=1, keepdims=True) / total
    delta = delta.reshape(KV_HEADS, GROUP, 1, 2, SPAN).transpose(0, 3, 2, 1, 4)
    delta = delta.reshape(KV_HEADS, 2, 1, GROUP * SPAN)

    g_gate = dot_first(dgate, normed_both).astype(BF).reshape(4, 2, 160, 2, 4, 128)
    g_up = dot_first(dup, normed_both).astype(BF).reshape(4, 2, 160, 2, 4, 128)
    g_down = dot_first(active, dy_both).astype(BF).reshape(2, 4, 160, 4, 2, 128)
    g_out = dot_plain(attended_low, dh_low).astype(BF).reshape(8, 2, 60, PAD)
    keep = lax.dynamic_index_in_dim(g_out, core, 1, keepdims=False)
    give = lax.dynamic_index_in_dim(g_out, 1 - core, 1, keepdims=False)
    g_out = (keep.astype(F32) + other_core(give).astype(F32)).astype(BF).reshape(2, 4, 60, 4, 2, 128)
    g_big = jnp.concatenate(
        [
            g_gate.transpose(4, 0, 1, 3, 2, 5),
            g_up.transpose(4, 0, 1, 3, 2, 5),
            g_down.transpose(1, 3, 4, 0, 2, 5),
            g_out.transpose(1, 3, 4, 0, 2, 5),
            jnp.zeros((4, 4, 2, 2, 4, 128), BF),
        ],
        axis=4,
    ).reshape(64 * 544, 128)
    g_big = lax.psum_scatter(g_big, PLANE, scatter_dimension=0, tiled=True)
    g_big = lax.psum_scatter(g_big, LINE, scatter_dimension=0, tiled=True)

    dq, dkv = attend_back(info, kv, query, by_half(dnum.reshape(D, rows)), delta)

    dkv = dkv.reshape(8, 2, rows, 640)
    keep = lax.dynamic_index_in_dim(dkv, core, 1, keepdims=False)
    give = lax.dynamic_index_in_dim(dkv, 1 - core, 1, keepdims=False)
    dkv = (keep.astype(F32) + other_core(give).astype(F32)).astype(BF)
    dkv = lax.all_to_all(dkv, SEQ, 0, 0, tiled=True)
    dkv = jnp.sum(dkv.astype(F32), axis=0).T.reshape(KV_HEADS, 2, HEAD_DIM, rows)

    dq_low = unrotate(by_head(dq), cosine, sine).astype(BF).reshape(D, rows)
    dk_low = unrotate(dkv[:, 0], cosine, sine).astype(BF)
    dkv_low = jnp.stack([dk_low, dkv[:, 1].astype(BF)], axis=1).reshape(640, rows)
    dqkv = jnp.concatenate([dq_low, dkv_low], axis=0)
    dn_one = dot_first(dqkv, w_qkv)
    back_one, gain_one_grad = norm_back(dn_one, unit_one, inverse_one, gain_one)
    input_grad = cut_width((dh + back_one).astype(BF))

    g_qkv = dot_plain(dqkv, normed_one).astype(BF)
    g_q = g_qkv[:D].reshape(8, 2, 60, PAD)
    g_kv = g_qkv[D:].reshape(KV_HEADS, 2, HEAD_DIM, PAD)
    g_k = g_kv[:, 0].reshape(8, 2, 20, PAD)
    g_v = g_kv[:, 1].reshape(8, 2, 20, PAD)
    g_small = jnp.concatenate([g_q, g_k, g_v], axis=2)
    keep = lax.dynamic_index_in_dim(g_small, core, 1, keepdims=False)
    give = lax.dynamic_index_in_dim(g_small, 1 - core, 1, keepdims=False)
    g_small = (keep.astype(F32) + other_core(give).astype(F32)).astype(BF)
    g_small = g_small.reshape(8, 100, 8, 128).transpose(2, 0, 1, 3).reshape(64, 100, 128)
    gains = jnp.stack([gain_one_grad, gain_two_grad])
    gains = gains + other_core(gains)
    gains_high = gains.astype(BF)
    gains_low = (gains - gains_high.astype(F32)).astype(BF)
    gains = jnp.concatenate([gains_high.reshape(16, 128), gains_low.reshape(16, 128)], axis=0)
    last = jnp.concatenate([g_small, jnp.broadcast_to(gains, (64, 32, 128))], axis=1)
    last = lax.all_to_all(last, CHIPS, 0, 0, tiled=True)
    last = jnp.sum(last.astype(F32), axis=0)
    gains = cut_width((last[100:116] + last[116:132]).reshape(2, PAD))

    g_big = g_big.astype(F32)
    mixed = g_big[320:540, :120].reshape(220, 2, 60).transpose(1, 0, 2)
    mixed = lax.all_to_all(mixed, "c", 0, 0, tiled=True)
    return (
        result,
        input_grad,
        last[:60, :120].T,
        last[60:80, :120].T,
        last[80:100, :120].T,
        mixed[:, 160:].reshape(120, 60),
        g_big[:160, :120].T,
        g_big[160:320, :120].T,
        mixed[:, :160].reshape(320, 60),
        gains[0],
        gains[1],
    )


def solution(mesh):
    fine = Mesh(mesh.devices.reshape(2, 4, 4, 2, 2), ("zl", "y", "x", "zh", "c"))
    shard, ctx = ("zl", "y"), ("x", "zh", "c")
    both = shard + ctx
    return jax.shard_map(
        body,
        mesh=fine,
        in_specs=(P(both, None),)
        + (P(shard, ctx),) * 7
        + (P(), P(), P(shard, None), P(shard, None), P(both, None)),
        out_specs=(P(both, None), P(both, None)) + (P(shard, ctx),) * 7 + (P(), P()),
        check_vma=False,
    )
```

```python
import jax
import jax.numpy as jnp
from jax import lax
from jax.experimental import pallas as pl
from jax.experimental.pallas import tpu as pltpu
from jax.sharding import Mesh
from jax.sharding import PartitionSpec as P

D = 960
HEADS = 15
KV_HEADS = 5
GROUP = 3
HEAD_DIM = 64
SPAN = 128
PAD = 1024

EPS = 1e-05
ROPE_BASE = 100000.0

BF = jnp.bfloat16
F32 = jnp.float32

PLANE = ("y", "x")
LINE = ("zh", "zl")
CHIPS = ("zl", "y", "x", "zh")
SEQ = ("x", "zh")
SWAP = [(0, 1), (1, 0)]


def pad_width(value):
    rows = value.shape[0]
    blocks = value.reshape(rows, 8, 120)
    return jnp.pad(blocks, ((0, 0), (0, 0), (0, 8))).reshape(rows, PAD)


def cut_width(value):
    rows = value.shape[0]
    return value.reshape(rows, 8, 128)[:, :, :120].reshape(rows, D)


def pad_lanes(value):
    return jnp.pad(value, ((0, 0), (0, 128 - value.shape[1])))


def other_core(value):
    return lax.ppermute(value, "c", SWAP)


def dot_last(left, right):
    return lax.dot_general(left, right, (((1,), (1,)), ((), ())), preferred_element_type=F32)


def dot_first(left, right):
    return lax.dot_general(left, right, (((0,), (0,)), ((), ())), preferred_element_type=F32)


def dot_plain(left, right):
    return jnp.dot(left, right, preferred_element_type=F32)


VMEM_LIMIT = 56 * 1024 * 1024
WIDTH = GROUP * SPAN
TILES = 4
STEP = TILES * SPAN
SEQ_LEN = 4096
FEED = 640


def sort_blocks(info, sources, target):
    def one(slot, carry):
        at = pl.ds(pl.multiple_of(slot * SPAN, SPAN), SPAN)
        for n, source in enumerate(sources):
            to = pl.ds(pl.multiple_of(info[8 + 16 * n + slot] * SPAN, SPAN), SPAN)
            target[to, :] = source[at, :]
        return carry

    lax.fori_loop(0, 16, one, 0)


def unsort_blocks(info, source, targets):
    def one(slot, carry):
        at = pl.ds(pl.multiple_of(slot * SPAN, SPAN), SPAN)
        for n, target in enumerate(targets):
            to = pl.ds(pl.multiple_of(info[8 + 16 * n + slot] * SPAN, SPAN), SPAN)
            target[at, :] = source[to, :].astype(target.dtype)
        return carry

    lax.fori_loop(0, 16, one, 0)


def causal_steps(info, tile):
    low_half, low = info[0], info[1]
    high = 31 - low
    low_last = lax.div(low, TILES)
    high_last = lax.div(high, TILES)

    def whole(step, carry):
        is_low = step < low_last
        tile(
            jnp.where(is_low, low_half, 1 - low_half),
            jnp.where(is_low, step, step - low_last),
            None,
        )
        return carry

    lax.fori_loop(0, 7, whole, 0)
    tile(low_half, low_last, (low - low_last * TILES) * SPAN)
    tile(1 - low_half, high_last, (high - high_last * TILES) * SPAN)


def key_rows_minus_query_lanes():
    row = lax.broadcasted_iota(jnp.int32, (STEP, WIDTH), 0)
    lane = lax.broadcasted_iota(jnp.int32, (STEP, WIDTH), 1)
    return row - lax.rem(lane, SPAN)


def key_step(ref, step):
    return ref[pl.ds(pl.multiple_of(step * STEP, STEP), STEP), :]


def attend_kernel(info, mine_ref, other_ref, q_ref, out_ref, total_ref, keys_in_order, query, numer, total):
    sort_blocks(info, (mine_ref, other_ref), keys_in_order)
    query[...] = jnp.zeros_like(query)
    for half in range(2):
        query[half, :HEAD_DIM, :] = q_ref[0, half]
    numer[...] = jnp.zeros_like(numer)
    total[...] = jnp.zeros_like(total)

    def tile(half, step, limit):
        keys = key_step(keys_in_order, step)
        expo = jnp.exp(dot_plain(keys, query[half]))
        if limit is not None:
            expo = jnp.where(key_rows_minus_query_lanes() <= limit, expo, 0.0)
        numer[half] += dot_plain(keys.T[HEAD_DIM:], expo.astype(BF))
        total[half] += jnp.sum(expo.reshape(STEP // 8, 8, WIDTH), axis=0)

    causal_steps(info, tile)
    for half in range(2):
        summed = jnp.sum(total[half], axis=0, keepdims=True)
        total_ref[0, half] = summed
        out_ref[0, half] = numer[half] / summed


HEAD_SPEC = pl.BlockSpec((1, 2, HEAD_DIM, WIDTH), lambda g, s: (g, 0, 0, 0))
ROW_SPEC = pl.BlockSpec((1, 2, 1, WIDTH), lambda g, s: (g, 0, 0, 0))
KV_SPEC = pl.BlockSpec((SEQ_LEN // 2, 2 * HEAD_DIM), lambda g, s: (0, g))
HEAD_F32 = jax.ShapeDtypeStruct((KV_HEADS, 2, HEAD_DIM, WIDTH), F32)


def attend(info, mine, other, query):
    return pl.pallas_call(
        attend_kernel,
        grid_spec=pltpu.PrefetchScalarGridSpec(
            num_scalar_prefetch=1,
            grid=(KV_HEADS,),
            in_specs=[KV_SPEC, KV_SPEC, HEAD_SPEC],
            out_specs=[HEAD_SPEC, ROW_SPEC],
            scratch_shapes=[
                pltpu.VMEM((SEQ_LEN, 2 * HEAD_DIM), BF),
                pltpu.VMEM((2, 2 * HEAD_DIM, WIDTH), BF),
                pltpu.VMEM((2, HEAD_DIM, WIDTH), F32),
                pltpu.VMEM((2, 8, WIDTH), F32),
            ],
        ),
        out_shape=[HEAD_F32, jax.ShapeDtypeStruct((KV_HEADS, 2, 1, WIDTH), F32)],
        compiler_params=pltpu.CompilerParams(vmem_limit_bytes=VMEM_LIMIT),
        cost_estimate=pl.CostEstimate(flops=4 * 10**9, bytes_accessed=8 * 10**6, transcendentals=8 * 10**6),
    )(info, mine, other, query)


def attend_back_kernel(
    info, mine_ref, other_ref, q_ref, dnum_ref, delta_ref, dq_ref, dmine_ref, dother_ref, keys_in_order, wide, tall, dq, dkv
):
    sort_blocks(info, (mine_ref, other_ref), keys_in_order)
    for half in range(2):
        zero = jnp.zeros((HEAD_DIM, WIDTH), BF)
        both = jnp.concatenate(
            [
                jnp.concatenate([q_ref[0, half], zero], axis=1),
                jnp.concatenate([zero, dnum_ref[0, half]], axis=1),
            ],
            axis=0,
        )
        wide[half] = both
        tall[half] = both.T
    dq[...] = jnp.zeros_like(dq)
    dkv[...] = jnp.zeros_like(dkv)

    def tile(half, step, limit):
        keys = key_step(keys_in_order, step)
        scores = dot_plain(keys, wide[half])
        expo = jnp.exp(scores[:, :WIDTH])
        if limit is not None:
            expo = jnp.where(key_rows_minus_query_lanes() <= limit, expo, 0.0)
        grads = (expo * (scores[:, WIDTH:] - delta_ref[0, half])).astype(BF)
        pair = jnp.concatenate([grads, expo.astype(BF)], axis=1)
        at = pl.ds(pl.multiple_of(step * STEP, STEP), STEP)
        dkv[at, :] += dot_plain(pair, tall[half])
        dq[half] += dot_plain(keys.T[:HEAD_DIM], grads)

    causal_steps(info, tile)
    for half in range(2):
        dq_ref[0, half] = dq[half] * (HEAD_DIM**-0.5)
    unsort_blocks(info, dkv, (dmine_ref, dother_ref))


def attend_back(info, mine, other, query, dnum, delta):
    return pl.pallas_call(
        attend_back_kernel,
        grid_spec=pltpu.PrefetchScalarGridSpec(
            num_scalar_prefetch=1,
            grid=(KV_HEADS,),
            in_specs=[KV_SPEC, KV_SPEC, HEAD_SPEC, HEAD_SPEC, ROW_SPEC],
            out_specs=[HEAD_SPEC, KV_SPEC, KV_SPEC],
            scratch_shapes=[
                pltpu.VMEM((SEQ_LEN, 2 * HEAD_DIM), BF),
                pltpu.VMEM((2, 2 * HEAD_DIM, 2 * WIDTH), BF),
                pltpu.VMEM((2, 2 * WIDTH, 2 * HEAD_DIM), BF),
                pltpu.VMEM((2, HEAD_DIM, WIDTH), F32),
                pltpu.VMEM((SEQ_LEN, 2 * HEAD_DIM), F32),
            ],
        ),
        out_shape=[HEAD_F32] + [jax.ShapeDtypeStruct(mine.shape, BF)] * 2,
        compiler_params=pltpu.CompilerParams(vmem_limit_bytes=VMEM_LIMIT),
        cost_estimate=pl.CostEstimate(flops=10 * 10**9, bytes_accessed=12 * 10**6, transcendentals=8 * 10**6),
    )(info, mine, other, query, dnum, delta)


PARTS = ((0, 60), (64, 20), (88, 20))
BLOCK = 112


def project_kernel(info, mine_ref, other_ref, normed_ref, cos_ref, sin_ref, w_ref, query_ref, kv_ref, q_rows, k_rows, v_rows, pair):
    step = pl.program_id(0)
    core = info[2]
    for at in range(8):
        lanes = slice(at * 128, at * 128 + 128)
        w_ref[0, core, :, lanes] = mine_ref[at // 4, at % 4, 0, 0]
        w_ref[0, 1 - core, :, lanes] = other_ref[at // 4, at % 4, 0, 0]
    made = dot_last(w_ref[0].reshape(2 * BLOCK, PAD), normed_ref[...])
    for (start, count), rows in zip(PARTS, (q_rows, k_rows, v_rows)):
        pair[0:count] = made[start : start + count]
        pair[count : 2 * count] = made[BLOCK + start : BLOCK + start + count]
        rows[pl.ds(pl.multiple_of(step * 2 * count, 8), 2 * count), :] = pair[0 : 2 * count]

    @pl.when(step == 7)
    def _():
        cosine, sine = cos_ref[...], sin_ref[...]

        def turned(rows, head):
            first = rows[head * 64 : head * 64 + 32]
            second = rows[head * 64 + 32 : head * 64 + 64]
            return jnp.concatenate([first * cosine - second * sine, second * cosine + first * sine], axis=0)

        for g in range(KV_HEADS):
            for r in range(GROUP):
                head = turned(q_rows, GROUP * g + r).astype(BF) * BF(HEAD_DIM**-0.5)
                for half in range(2):
                    query_ref[g, half, :, r * SPAN : (r + 1) * SPAN] = head[:, half * SPAN : (half + 1) * SPAN]
            both = jnp.concatenate([turned(k_rows, g), v_rows[g * 64 : g * 64 + 64]], axis=0)
            kv_ref[:, g * 128 : (g + 1) * 128] = both.T.astype(BF)


def whole_spec(*shape):
    return pl.BlockSpec(shape, lambda j, s: (0,) * len(shape))


SMALL_SPEC = pl.BlockSpec((2, 4, 1, 1, BLOCK, 128), lambda j, s: (0, 0, j // 2, j % 2, 0, 0))
W_SPEC = pl.BlockSpec((1, 2, BLOCK, PAD), lambda j, s: (j, 0, 0, 0))


def project(info, mine, other, normed, cosine, sine):
    rows = normed.shape[0]
    return pl.pallas_call(
        project_kernel,
        grid_spec=pltpu.PrefetchScalarGridSpec(
            num_scalar_prefetch=1,
            grid=(8,),
            in_specs=[SMALL_SPEC, SMALL_SPEC, whole_spec(rows, PAD), whole_spec(32, rows), whole_spec(32, rows)],
            out_specs=[W_SPEC, whole_spec(KV_HEADS, 2, HEAD_DIM, WIDTH), whole_spec(rows, 640)],
            scratch_shapes=[
                pltpu.VMEM((D, rows), F32),
                pltpu.VMEM((320, rows), F32),
                pltpu.VMEM((320, rows), F32),
                pltpu.VMEM((120, rows), F32),
            ],
        ),
        out_shape=[
            jax.ShapeDtypeStruct((8, 2, BLOCK, PAD), BF),
            jax.ShapeDtypeStruct((KV_HEADS, 2, HEAD_DIM, WIDTH), BF),
            jax.ShapeDtypeStruct((rows, 640), BF),
        ],
        compiler_params=pltpu.CompilerParams(vmem_limit_bytes=VMEM_LIMIT),
        cost_estimate=pl.CostEstimate(flops=10**9, bytes_accessed=8 * 10**6, transcendentals=0),
    )(info, mine, other, normed, cosine, sine)


def project_back_kernel(
    info, dq_ref, dkv_ref, normed_ref, cos_ref, sin_ref, w_ref, dn_ref, mine_ref, other_ref, q_rows, k_rows, v_rows, pair, blocks, grads
):
    step = pl.program_id(0)
    core = info[2]

    @pl.when(step == 0)
    def _():
        cosine, sine = cos_ref[...], sin_ref[...]

        def turned_back(value):
            first, second = value[:32], value[32:]
            return jnp.concatenate([first * cosine + second * sine, second * cosine - first * sine], axis=0)

        for g in range(KV_HEADS):
            for r in range(GROUP):
                lanes = slice(r * SPAN, (r + 1) * SPAN)
                head = jnp.concatenate([dq_ref[g, 0, :, lanes], dq_ref[g, 1, :, lanes]], axis=1)
                at = (GROUP * g + r) * 64
                q_rows[at : at + 64] = turned_back(head)
            both = dkv_ref[:, g * 128 : (g + 1) * 128].T
            k_rows[g * 64 : g * 64 + 64] = turned_back(both[:64])
            v_rows[g * 64 : g * 64 + 64] = both[64:]
        blocks[...] = jnp.zeros_like(blocks)
        dn_ref[...] = jnp.zeros_like(dn_ref)

    for (start, count), rows in zip(PARTS, (q_rows, k_rows, v_rows)):
        pair[0 : 2 * count] = rows[pl.ds(pl.multiple_of(step * 2 * count, 8), 2 * count), :]
        blocks[start : start + count] = pair[0:count]
        blocks[BLOCK + start : BLOCK + start + count] = pair[count : 2 * count]
    block = blocks[...].astype(BF)
    dn_ref[...] += dot_first(block, w_ref[0].reshape(2 * BLOCK, PAD))
    grads[...] = dot_plain(block, normed_ref[...]).astype(BF).reshape(2, BLOCK, PAD)
    for at in range(8):
        lanes = slice(at * 128, at * 128 + 128)
        mine_ref[at // 4, at % 4, 0, 0] = grads[core, :, lanes]
        other_ref[at // 4, at % 4, 0, 0] = grads[1 - core, :, lanes]


def project_back(info, dq, dkv, normed, cosine, sine, w_all):
    rows = normed.shape[0]
    small = jax.ShapeDtypeStruct((2, 4, 4, 2, BLOCK, 128), BF)
    return pl.pallas_call(
        project_back_kernel,
        grid_spec=pltpu.PrefetchScalarGridSpec(
            num_scalar_prefetch=1,
            grid=(8,),
            in_specs=[
                whole_spec(KV_HEADS, 2, HEAD_DIM, WIDTH),
                whole_spec(rows, 640),
                whole_spec(rows, PAD),
                whole_spec(32, rows),
                whole_spec(32, rows),
                W_SPEC,
            ],
            out_specs=[whole_spec(rows, PAD), SMALL_SPEC, SMALL_SPEC],
            scratch_shapes=[
                pltpu.VMEM((D, rows), F32),
                pltpu.VMEM((320, rows), F32),
                pltpu.VMEM((320, rows), F32),
                pltpu.VMEM((120, rows), F32),
                pltpu.VMEM((2 * BLOCK, rows), F32),
                pltpu.VMEM((2, BLOCK, PAD), BF),
            ],
        ),
        out_shape=[jax.ShapeDtypeStruct((rows, PAD), F32), small, small],
        compiler_params=pltpu.CompilerParams(vmem_limit_bytes=VMEM_LIMIT),
        cost_estimate=pl.CostEstimate(flops=2 * 10**9, bytes_accessed=10 * 10**6, transcendentals=0),
    )(info, dq, dkv, normed, cosine, sine, w_all)


def feed_kernel(
    gate_ref, up_ref, down_ref, n_mine, n_other, dy_mine, dy_other,
    fed_mine, fed_other, dn_mine, dn_other, grad_ref, normed, dy, wg, wu, wd, fed, dn
):
    step = pl.program_id(0)
    rows = n_mine.shape[0]

    @pl.when(step == 0)
    def _():
        normed[:rows] = n_mine[...]
        normed[rows:] = n_other[...]
        dy[:rows] = dy_mine[...]
        dy[rows:] = dy_other[...]
        fed[...] = jnp.zeros_like(fed)
        dn[...] = jnp.zeros_like(dn)

    for group in range(4):
        part = slice(group * 160, group * 160 + 160)
        for at in range(8):
            lanes = slice(at * 128, at * 128 + 128)
            wg[part, lanes] = gate_ref[at % 4, group // 2, group % 2, at // 4]
            wu[part, lanes] = up_ref[at % 4, group // 2, group % 2, at // 4]
            wd[part, lanes] = down_ref[group, at // 2, at % 2, 0]
    gate = dot_last(normed[...], wg[...])
    upward = dot_last(normed[...], wu[...])
    dact = dot_last(dy[...], wd[...])
    sigma = jax.nn.sigmoid(gate)
    silu_gate = gate * sigma
    active = (silu_gate * upward).astype(BF)
    dgate = (dact * upward * sigma * (1.0 + gate * (1.0 - sigma))).astype(BF)
    dup = (dact * silu_gate).astype(BF)
    fed[...] += dot_plain(active, wd[...])
    dn[...] += dot_plain(dgate, wg[...]) + dot_plain(dup, wu[...])
    g_gate = dot_first(dgate, normed[...]).astype(BF)
    g_up = dot_first(dup, normed[...]).astype(BF)
    g_down = dot_first(active, dy[...]).astype(BF)
    for group in range(4):
        part = slice(group * 160, group * 160 + 160)
        for at in range(8):
            lanes = slice(at * 128, at * 128 + 128)
            grad_ref[at % 4, 2 * step + group // 2, group % 2, at // 4, 0:160] = g_gate[part, lanes]
            grad_ref[at % 4, 2 * step + group // 2, group % 2, at // 4, 160:320] = g_up[part, lanes]
            grad_ref[group, at // 2, at % 2, step, 320:480] = g_down[part, lanes]

    @pl.when(step == 1)
    def _():
        fed_mine[...] = fed[:rows]
        fed_other[...] = fed[rows:].astype(BF)
        dn_mine[...] = dn[:rows]
        dn_other[...] = dn[rows:].astype(BF)


def feed(big, n_mine, n_other, dy_mine, dy_other):
    rows = n_mine.shape[0]
    by_plane = (4, 2, 2, 2, 160, 128)

    def flat(*shape):
        return pl.BlockSpec(shape, lambda k: (0,) * len(shape))

    return pl.pallas_call(
        feed_kernel,
        grid=(2,),
        in_specs=[
            pl.BlockSpec(by_plane, lambda k: (0, k, 0, 0, 0, 0)),
            pl.BlockSpec(by_plane, lambda k: (0, k, 0, 0, 1, 0)),
            pl.BlockSpec((4, 4, 2, 1, 160, 128), lambda k: (0, 0, 0, k, 2, 0)),
        ]
        + [flat(rows, PAD)] * 4,
        out_specs=[flat(rows, PAD)] * 4 + [flat(4, 4, 2, 2, 480, 128)],
        out_shape=[
            jax.ShapeDtypeStruct((rows, PAD), F32),
            jax.ShapeDtypeStruct((rows, PAD), BF),
            jax.ShapeDtypeStruct((rows, PAD), F32),
            jax.ShapeDtypeStruct((rows, PAD), BF),
            jax.ShapeDtypeStruct((4, 4, 2, 2, 480, 128), BF),
        ],
        scratch_shapes=[pltpu.VMEM((2 * rows, PAD), BF)] * 2
        + [pltpu.VMEM((FEED, PAD), BF)] * 3
        + [pltpu.VMEM((2 * rows, PAD), F32)] * 2,
        compiler_params=pltpu.CompilerParams(vmem_limit_bytes=VMEM_LIMIT),
        cost_estimate=pl.CostEstimate(flops=12 * 10**9, bytes_accessed=22 * 10**6, transcendentals=10**6),
    )(big, big, big, n_mine, n_other, dy_mine, dy_other)


def by_half(value):
    rows = value.shape[1]
    split = value.reshape(KV_HEADS, GROUP, rows, 2, SPAN)
    return split.transpose(0, 3, 2, 1, 4).reshape(KV_HEADS, 2, rows, WIDTH)


def by_head(value):
    rows = value.shape[2]
    split = value.reshape(KV_HEADS, 2, rows, GROUP, SPAN)
    return split.transpose(0, 3, 2, 1, 4).reshape(HEADS, rows, 2 * SPAN)


def pad_rows(value, count):
    return jnp.pad(value, ((0, count - value.shape[0]), (0, 0)))


def norm_forward(value, gain):
    inverse = lax.rsqrt(jnp.sum(value * value, axis=-1, keepdims=True) / D + EPS)
    unit = value * inverse
    return unit, inverse, (unit * gain).astype(BF)


def norm_back(grad, unit, inverse, gain):
    scaled = grad * gain
    inner = jnp.sum(scaled * unit, axis=-1, keepdims=True) / D
    return inverse * (scaled - unit * inner), jnp.sum(grad * unit, axis=0)


def body(
    tokens,
    w_query,
    w_key,
    w_value,
    w_out,
    w_gate,
    w_up,
    w_down,
    attention_norm_gain,
    feedforward_norm_gain,
    span_order,
    positions,
    out_grad,
):
    rows = tokens.shape[0]
    core = lax.axis_index("c")
    me = lax.axis_index(("x", "zh", "c"))

    small = jnp.concatenate([pad_rows(w_query.T, 64), pad_rows(w_key.T, 24), pad_rows(w_value.T, 24)], axis=0)
    small = lax.all_to_all(jnp.broadcast_to(pad_lanes(small), (64, BLOCK, 128)), CHIPS, 0, 0, tiled=True)
    small = small.reshape(2, 4, 4, 2, BLOCK, 128)

    mixed = jnp.concatenate([w_down.reshape(2, 160, 60), w_out.reshape(2, 60, 60)], axis=1)
    mixed = lax.all_to_all(mixed, "c", 0, 0, tiled=True)
    mixed = jnp.concatenate([mixed[0], mixed[1]], axis=1)
    big = jnp.concatenate([w_gate.T, w_up.T, mixed], axis=0)
    big = pad_rows(pad_lanes(big), 544)
    big = lax.all_to_all(jnp.broadcast_to(big, (4, 544, 128)), LINE, 0, 0, tiled=True)
    big = lax.all_gather(big, PLANE, axis=0, tiled=True).reshape(4, 4, 2, 2, 544, 128)

    order = span_order[0]
    own_pair = lax.dynamic_slice_in_dim(order, 2 * me, 2)
    own_low_half = (own_pair[0] > own_pair[1]).astype(jnp.int32)
    spans = order.reshape(8, 2, 2)
    info = jnp.concatenate(
        [
            jnp.stack([own_low_half, jnp.minimum(own_pair[0], own_pair[1]), core.astype(jnp.int32)]),
            jnp.zeros((5,), jnp.int32),
            lax.dynamic_index_in_dim(spans, core, 1, keepdims=False).reshape(16),
            lax.dynamic_index_in_dim(spans, 1 - core, 1, keepdims=False).reshape(16),
        ]
    ).astype(jnp.int32)
    place = jnp.concatenate(
        [
            lax.dynamic_slice_in_dim(positions[0], own_pair[0] * SPAN, SPAN, 0),
            lax.dynamic_slice_in_dim(positions[0], own_pair[1] * SPAN, SPAN, 0),
        ]
    )
    half_dim = HEAD_DIM // 2
    freq = jnp.power(ROPE_BASE, -jnp.arange(half_dim, dtype=F32) / half_dim)
    angle = freq[:, None] * place.astype(F32)[None, :]
    cosine, sine = jnp.cos(angle), jnp.sin(angle)

    gain_one = pad_width(attention_norm_gain[None])
    gain_two = pad_width(feedforward_norm_gain[None])
    layer_input = pad_width(tokens).astype(F32)
    dy = pad_width(out_grad)
    dy_other = other_core(dy)

    unit_one, inverse_one, normed_one = norm_forward(layer_input, gain_one)
    w_all, query, kv_local = project(info, small, other_core(small), normed_one, cosine, sine)

    kv = lax.all_to_all(jnp.broadcast_to(kv_local, (8, rows, 640)), SEQ, 0, 0, tiled=True)
    kv = kv.reshape(8 * rows, 640)
    kv_other = other_core(kv)

    attended, total = attend(info, kv, kv_other, query)
    attended = by_head(attended)
    total = by_head(total)
    attended_low = attended.astype(BF).reshape(16, 60, rows)
    attended_low = jnp.pad(attended_low, ((0, 0), (0, 4), (0, 0))).reshape(PAD, rows)

    w_out_h = big[:, :, :, :, 480:].transpose(3, 0, 4, 1, 2, 5).reshape(8, 64, PAD)
    w_out_o = other_core(w_out_h)
    first = core == 0
    w_out_full = jnp.stack(
        [jnp.where(first, w_out_h, w_out_o), jnp.where(first, w_out_o, w_out_h)], axis=1
    ).reshape(PAD, PAD)

    hidden = layer_input + dot_first(attended_low, w_out_full)
    unit_two, inverse_two, normed_two = norm_forward(hidden, gain_two)
    fed, fed_other, dn_two, dn_other, g_big = feed(big, normed_two, other_core(normed_two), dy, dy_other)
    dn_two = dn_two + other_core(dn_other).astype(F32)
    result = cut_width((hidden + (fed + other_core(fed_other).astype(F32))).astype(BF))

    back_two, gain_two_grad = norm_back(dn_two, unit_two, inverse_two, gain_two)
    dh = dy.astype(F32) + back_two
    dh_low = dh.astype(BF)
    dob = dot_last(w_out_full, dh_low).astype(BF).reshape(16, 64, rows)[:, :60]
    dob = dob.reshape(HEADS, HEAD_DIM, rows).astype(F32)
    dnum = (dob / total).astype(BF)
    delta = jnp.sum(dob * attended, axis=1, keepdims=True) / total

    g_big = lax.psum_scatter(g_big.reshape(64 * 480, 128), PLANE, scatter_dimension=0, tiled=True)
    g_big = lax.psum_scatter(g_big, LINE, scatter_dimension=0, tiled=True)

    g_out = dot_plain(attended_low, dh_low).astype(BF).reshape(8, 2, 64, PAD)
    keep = lax.dynamic_index_in_dim(g_out, core, 1, keepdims=False)
    give = lax.dynamic_index_in_dim(g_out, 1 - core, 1, keepdims=False)
    g_out = (keep.astype(F32) + other_core(give).astype(F32)).astype(BF)
    g_out = g_out.reshape(8, 64, 8, 128).transpose(0, 2, 1, 3).reshape(64, 64, 128)
    g_out = lax.all_to_all(g_out, CHIPS, 0, 0, tiled=True)
    g_out = jnp.sum(g_out.astype(F32), axis=0)

    dq, dkv, dkv_other = attend_back(info, kv, kv_other, query, by_half(dnum), by_half(delta))
    dkv = (dkv.astype(F32) + other_core(dkv_other).astype(F32)).astype(BF)
    dkv = lax.all_to_all(dkv.reshape(8, rows, 640), SEQ, 0, 0, tiled=True)
    dkv = jnp.sum(dkv.astype(F32), axis=0)

    dn_one, g_small, g_other = project_back(info, dq, dkv, normed_one, cosine, sine, w_all)
    back_one, gain_one_grad = norm_back(dn_one, unit_one, inverse_one, gain_one)
    input_grad = cut_width((dh + back_one).astype(BF))

    g_small = (g_small.astype(F32) + other_core(g_other).astype(F32)).astype(BF).reshape(64, BLOCK, 128)
    gains = jnp.stack([gain_one_grad, gain_two_grad])
    gains = gains + other_core(gains)
    gains_high = gains.astype(BF)
    gains_low = (gains - gains_high.astype(F32)).astype(BF)
    gains = jnp.concatenate([gains_high.reshape(16, 128), gains_low.reshape(16, 128)], axis=0)
    last = jnp.concatenate([g_small, jnp.broadcast_to(gains, (64, 32, 128))], axis=1)
    last = lax.all_to_all(last, CHIPS, 0, 0, tiled=True)
    last = jnp.sum(last.astype(F32), axis=0)
    gains = cut_width((last[BLOCK : BLOCK + 16] + last[BLOCK + 16 :]).reshape(2, PAD))

    g_big = g_big.astype(F32)
    mixed = jnp.concatenate([g_big[320:480, :120], g_out[:60, :120]], axis=0)
    mixed = mixed.reshape(220, 2, 60).transpose(1, 0, 2)
    mixed = lax.all_to_all(mixed, "c", 0, 0, tiled=True)
    return (
        result,
        input_grad,
        last[:60, :120].T,
        last[64:84, :120].T,
        last[88:108, :120].T,
        mixed[:, 160:].reshape(120, 60),
        g_big[:160, :120].T,
        g_big[160:320, :120].T,
        mixed[:, :160].reshape(320, 60),
        gains[0],
        gains[1],
    )


def solution(mesh):
    fine = Mesh(mesh.devices.reshape(2, 4, 4, 2, 2), ("zl", "y", "x", "zh", "c"))
    shard, ctx = ("zl", "y"), ("x", "zh", "c")
    both = shard + ctx
    return jax.shard_map(
        body,
        mesh=fine,
        in_specs=(P(both, None),)
        + (P(shard, ctx),) * 7
        + (P(), P(), P(shard, None), P(shard, None), P(both, None)),
        out_specs=(P(both, None), P(both, None)) + (P(shard, ctx),) * 7 + (P(), P()),
        check_vma=False,
    )
```

```python
import jax
import jax.numpy as jnp
from jax import lax
from jax.experimental import pallas as pl
from jax.experimental.pallas import tpu as pltpu
from jax.sharding import Mesh
from jax.sharding import PartitionSpec as P

D = 960
HEADS = 15
KV_HEADS = 5
GROUP = 3
HEAD_DIM = 64
SPAN = 128
PAD = 1024

EPS = 1e-05
ROPE_BASE = 100000.0

BF = jnp.bfloat16
F32 = jnp.float32

PLANE = ("y", "x")
LINE = ("zh", "zl")
CHIPS = ("zl", "y", "x", "zh")
SEQ = ("x", "zh")
SWAP = [(0, 1), (1, 0)]


def pad_width(value):
    rows = value.shape[0]
    blocks = value.reshape(rows, 8, 120)
    return jnp.pad(blocks, ((0, 0), (0, 0), (0, 8))).reshape(rows, PAD)


def cut_width(value):
    rows = value.shape[0]
    return value.reshape(rows, 8, 128)[:, :, :120].reshape(rows, D)


def pad_lanes(value):
    return jnp.pad(value, ((0, 0), (0, 128 - value.shape[1])))


def other_core(value):
    return lax.ppermute(value, "c", SWAP)


def gather_line(block):
    ring = ("zl", "zh")
    held = jnp.stack(
        [block] + [lax.ppermute(block, ring, [(n, n ^ turn) for n in range(4)]) for turn in range(1, 4)]
    )
    here = lax.axis_index(ring)
    wanted = [lax.dynamic_index_in_dim(held, here ^ (2 * zl + zh), 0) for zh in range(2) for zl in range(2)]
    return jnp.concatenate(wanted, axis=0)


def dot_last(left, right):
    return lax.dot_general(left, right, (((1,), (1,)), ((), ())), preferred_element_type=F32)


def dot_first(left, right):
    return lax.dot_general(left, right, (((0,), (0,)), ((), ())), preferred_element_type=F32)


def dot_plain(left, right):
    return jnp.dot(left, right, preferred_element_type=F32)


VMEM_LIMIT = 56 * 1024 * 1024
WIDTH = GROUP * SPAN
TILES = 8
SUB = 2
STEP = TILES * SPAN
SEQ_LEN = 4096
FEED = 640


def sort_blocks(info, sources, target):
    def one(slot, carry):
        at = pl.ds(pl.multiple_of(slot * SPAN, SPAN), SPAN)
        for n, source in enumerate(sources):
            to = pl.ds(pl.multiple_of(info[8 + 16 * n + slot] * SPAN, SPAN), SPAN)
            target[to, :] = source[at, :]
        return carry

    lax.fori_loop(0, 16, one, 0)


def unsort_blocks(info, source, targets):
    def one(slot, carry):
        at = pl.ds(pl.multiple_of(slot * SPAN, SPAN), SPAN)
        for n, target in enumerate(targets):
            to = pl.ds(pl.multiple_of(info[8 + 16 * n + slot] * SPAN, SPAN), SPAN)
            target[at, :] = source[to, :].astype(target.dtype)
        return carry

    lax.fori_loop(0, 16, one, 0)


def causal_steps(info, tile):
    low_half, low = info[0], info[1]
    high = 31 - low
    low_last = lax.div(low, TILES)
    high_last = lax.div(high, TILES)

    def whole(step, carry):
        is_low = step < low_last
        tile(
            jnp.where(is_low, low_half, 1 - low_half),
            jnp.where(is_low, step, step - low_last),
            None,
        )
        return carry

    lax.fori_loop(0, 3, whole, 0, unroll=3)
    tile(low_half, low_last, (low - low_last * TILES) * SPAN)
    tile(1 - low_half, high_last, (high - high_last * TILES) * SPAN)


def key_rows_minus_query_lanes(rows):
    row = lax.broadcasted_iota(jnp.int32, (rows, WIDTH), 0)
    lane = lax.broadcasted_iota(jnp.int32, (rows, WIDTH), 1)
    return row - lax.rem(lane, SPAN)


def attend_kernel(info, mine_ref, other_ref, q_ref, out_ref, total_ref, keys_in_order, query, numer, total):
    sort_blocks(info, (mine_ref, other_ref), keys_in_order)
    query[...] = jnp.zeros_like(query)
    for half in range(2):
        query[half, :HEAD_DIM, :] = q_ref[0, half]
    numer[...] = jnp.zeros_like(numer)
    total[...] = jnp.zeros_like(total)

    def tile(half, step, limit):
        some = STEP // SUB
        parts, sums = [], []
        for n in range(SUB):
            keys = keys_in_order[pl.ds(pl.multiple_of(step * STEP + n * some, some), some), :]
            expo = jnp.exp(dot_plain(keys, query[half]))
            if limit is not None:
                expo = jnp.where(key_rows_minus_query_lanes(some) <= limit - n * some, expo, 0.0)
            parts.append(dot_plain(keys.T[HEAD_DIM:], expo.astype(BF)))
            sums.append(jnp.sum(expo.reshape(some // 8, 8, WIDTH), axis=0))
        numer[half] += sum(parts[1:], parts[0])
        total[half] += sum(sums[1:], sums[0])

    causal_steps(info, tile)
    for half in range(2):
        summed = jnp.sum(total[half], axis=0, keepdims=True)
        total_ref[0, half] = summed
        out_ref[0, half] = numer[half] / summed


HEAD_SPEC = pl.BlockSpec((1, 2, HEAD_DIM, WIDTH), lambda g, s: (g, 0, 0, 0))
ROW_SPEC = pl.BlockSpec((1, 2, 1, WIDTH), lambda g, s: (g, 0, 0, 0))
KV_SPEC = pl.BlockSpec((SEQ_LEN // 2, 2 * HEAD_DIM), lambda g, s: (0, g))
HEAD_F32 = jax.ShapeDtypeStruct((KV_HEADS, 2, HEAD_DIM, WIDTH), F32)


def attend(info, mine, other, query):
    return pl.pallas_call(
        attend_kernel,
        grid_spec=pltpu.PrefetchScalarGridSpec(
            num_scalar_prefetch=1,
            grid=(KV_HEADS,),
            in_specs=[KV_SPEC, KV_SPEC, HEAD_SPEC],
            out_specs=[HEAD_SPEC, ROW_SPEC],
            scratch_shapes=[
                pltpu.VMEM((SEQ_LEN, 2 * HEAD_DIM), BF),
                pltpu.VMEM((2, 2 * HEAD_DIM, WIDTH), BF),
                pltpu.VMEM((2, HEAD_DIM, WIDTH), F32),
                pltpu.VMEM((2, 8, WIDTH), F32),
            ],
        ),
        out_shape=[HEAD_F32, jax.ShapeDtypeStruct((KV_HEADS, 2, 1, WIDTH), F32)],
        compiler_params=pltpu.CompilerParams(vmem_limit_bytes=VMEM_LIMIT),
        cost_estimate=pl.CostEstimate(flops=4 * 10**9, bytes_accessed=8 * 10**6, transcendentals=8 * 10**6),
    )(info, mine, other, query)


def attend_back_kernel(
    info, mine_ref, other_ref, q_ref, dnum_ref, delta_ref, dq_ref, dmine_ref, dother_ref, keys_in_order, wide, tall, dq, dkv
):
    sort_blocks(info, (mine_ref, other_ref), keys_in_order)
    for half in range(2):
        zero = jnp.zeros((HEAD_DIM, WIDTH), BF)
        both = jnp.concatenate(
            [
                jnp.concatenate([q_ref[0, half], zero], axis=1),
                jnp.concatenate([zero, dnum_ref[0, half]], axis=1),
            ],
            axis=0,
        )
        wide[half] = both
        tall[half] = both.T
    dq[...] = jnp.zeros_like(dq)
    dkv[...] = jnp.zeros_like(dkv)

    def tile(half, step, limit):
        some = STEP // SUB
        parts = []
        for n in range(SUB):
            at = pl.ds(pl.multiple_of(step * STEP + n * some, some), some)
            keys = keys_in_order[at, :]
            scores = dot_plain(keys, wide[half])
            expo = jnp.exp(scores[:, :WIDTH])
            if limit is not None:
                expo = jnp.where(key_rows_minus_query_lanes(some) <= limit - n * some, expo, 0.0)
            grads = (expo * (scores[:, WIDTH:] - delta_ref[0, half])).astype(BF)
            pair = jnp.concatenate([grads, expo.astype(BF)], axis=1)
            dkv[at, :] += dot_plain(pair, tall[half])
            parts.append(dot_plain(keys.T[:HEAD_DIM], grads))
        dq[half] += sum(parts[1:], parts[0])

    causal_steps(info, tile)
    for half in range(2):
        dq_ref[0, half] = dq[half] * (HEAD_DIM**-0.5)
    unsort_blocks(info, dkv, (dmine_ref, dother_ref))


def attend_back(info, mine, other, query, dnum, delta):
    return pl.pallas_call(
        attend_back_kernel,
        grid_spec=pltpu.PrefetchScalarGridSpec(
            num_scalar_prefetch=1,
            grid=(KV_HEADS,),
            in_specs=[KV_SPEC, KV_SPEC, HEAD_SPEC, HEAD_SPEC, ROW_SPEC],
            out_specs=[HEAD_SPEC, KV_SPEC, KV_SPEC],
            scratch_shapes=[
                pltpu.VMEM((SEQ_LEN, 2 * HEAD_DIM), BF),
                pltpu.VMEM((2, 2 * HEAD_DIM, 2 * WIDTH), BF),
                pltpu.VMEM((2, 2 * WIDTH, 2 * HEAD_DIM), BF),
                pltpu.VMEM((2, HEAD_DIM, WIDTH), F32),
                pltpu.VMEM((SEQ_LEN, 2 * HEAD_DIM), F32),
            ],
        ),
        out_shape=[HEAD_F32] + [jax.ShapeDtypeStruct(mine.shape, BF)] * 2,
        compiler_params=pltpu.CompilerParams(vmem_limit_bytes=VMEM_LIMIT),
        cost_estimate=pl.CostEstimate(flops=10 * 10**9, bytes_accessed=12 * 10**6, transcendentals=8 * 10**6),
    )(info, mine, other, query, dnum, delta)


PARTS = ((0, 60), (64, 20), (88, 20))
BLOCK = 112


def project_kernel(info, mine_ref, other_ref, normed_ref, cos_ref, sin_ref, w_ref, query_ref, kv_ref, q_rows, k_rows, v_rows, pair):
    step = pl.program_id(0)
    core = info[2]
    for at in range(8):
        lanes = slice(at * 128, at * 128 + 128)
        w_ref[0, core, :, lanes] = mine_ref[at // 4, at % 4, 0, 0]
        w_ref[0, 1 - core, :, lanes] = other_ref[at // 4, at % 4, 0, 0]
    made = dot_last(w_ref[0].reshape(2 * BLOCK, PAD), normed_ref[...])
    for (start, count), rows in zip(PARTS, (q_rows, k_rows, v_rows)):
        pair[0:count] = made[start : start + count]
        pair[count : 2 * count] = made[BLOCK + start : BLOCK + start + count]
        rows[pl.ds(pl.multiple_of(step * 2 * count, 8), 2 * count), :] = pair[0 : 2 * count]

    @pl.when(step == 7)
    def _():
        cosine, sine = cos_ref[...], sin_ref[...]

        def turned(rows, head):
            first = rows[head * 64 : head * 64 + 32]
            second = rows[head * 64 + 32 : head * 64 + 64]
            return jnp.concatenate([first * cosine - second * sine, second * cosine + first * sine], axis=0)

        for g in range(KV_HEADS):
            for r in range(GROUP):
                head = turned(q_rows, GROUP * g + r).astype(BF) * BF(HEAD_DIM**-0.5)
                for half in range(2):
                    query_ref[g, half, :, r * SPAN : (r + 1) * SPAN] = head[:, half * SPAN : (half + 1) * SPAN]
            both = jnp.concatenate([turned(k_rows, g), v_rows[g * 64 : g * 64 + 64]], axis=0)
            kv_ref[:, g * 128 : (g + 1) * 128] = both.T.astype(BF)


def whole_spec(*shape):
    return pl.BlockSpec(shape, lambda j, s: (0,) * len(shape))


SMALL_SPEC = pl.BlockSpec((2, 4, 1, 1, BLOCK, 128), lambda j, s: (0, 0, j // 2, j % 2, 0, 0))
W_SPEC = pl.BlockSpec((1, 2, BLOCK, PAD), lambda j, s: (j, 0, 0, 0))


def project(info, mine, other, normed, cosine, sine):
    rows = normed.shape[0]
    return pl.pallas_call(
        project_kernel,
        grid_spec=pltpu.PrefetchScalarGridSpec(
            num_scalar_prefetch=1,
            grid=(8,),
            in_specs=[SMALL_SPEC, SMALL_SPEC, whole_spec(rows, PAD), whole_spec(32, rows), whole_spec(32, rows)],
            out_specs=[W_SPEC, whole_spec(KV_HEADS, 2, HEAD_DIM, WIDTH), whole_spec(rows, 640)],
            scratch_shapes=[
                pltpu.VMEM((D, rows), F32),
                pltpu.VMEM((320, rows), F32),
                pltpu.VMEM((320, rows), F32),
                pltpu.VMEM((120, rows), F32),
            ],
        ),
        out_shape=[
            jax.ShapeDtypeStruct((8, 2, BLOCK, PAD), BF),
            jax.ShapeDtypeStruct((KV_HEADS, 2, HEAD_DIM, WIDTH), BF),
            jax.ShapeDtypeStruct((rows, 640), BF),
        ],
        compiler_params=pltpu.CompilerParams(vmem_limit_bytes=VMEM_LIMIT),
        cost_estimate=pl.CostEstimate(flops=10**9, bytes_accessed=8 * 10**6, transcendentals=0),
    )(info, mine, other, normed, cosine, sine)


def project_back_kernel(
    info, dq_ref, dkv_ref, normed_ref, cos_ref, sin_ref, w_ref, dn_ref, mine_ref, other_ref, q_rows, k_rows, v_rows, pair, blocks, grads
):
    step = pl.program_id(0)
    core = info[2]

    @pl.when(step == 0)
    def _():
        cosine, sine = cos_ref[...], sin_ref[...]

        def turned_back(value):
            first, second = value[:32], value[32:]
            return jnp.concatenate([first * cosine + second * sine, second * cosine - first * sine], axis=0)

        for g in range(KV_HEADS):
            for r in range(GROUP):
                lanes = slice(r * SPAN, (r + 1) * SPAN)
                head = jnp.concatenate([dq_ref[g, 0, :, lanes], dq_ref[g, 1, :, lanes]], axis=1)
                at = (GROUP * g + r) * 64
                q_rows[at : at + 64] = turned_back(head)
            both = dkv_ref[:, g * 128 : (g + 1) * 128].T
            k_rows[g * 64 : g * 64 + 64] = turned_back(both[:64])
            v_rows[g * 64 : g * 64 + 64] = both[64:]
        blocks[...] = jnp.zeros_like(blocks)
        dn_ref[...] = jnp.zeros_like(dn_ref)

    for (start, count), rows in zip(PARTS, (q_rows, k_rows, v_rows)):
        pair[0 : 2 * count] = rows[pl.ds(pl.multiple_of(step * 2 * count, 8), 2 * count), :]
        blocks[start : start + count] = pair[0:count]
        blocks[BLOCK + start : BLOCK + start + count] = pair[count : 2 * count]
    block = blocks[...].astype(BF)
    dn_ref[...] += dot_first(block, w_ref[0].reshape(2 * BLOCK, PAD))
    grads[...] = dot_plain(block, normed_ref[...]).astype(BF).reshape(2, BLOCK, PAD)
    for at in range(8):
        lanes = slice(at * 128, at * 128 + 128)
        mine_ref[at // 4, at % 4, 0, 0] = grads[core, :, lanes]
        other_ref[at // 4, at % 4, 0, 0] = grads[1 - core, :, lanes]


def project_back(info, dq, dkv, normed, cosine, sine, w_all):
    rows = normed.shape[0]
    small = jax.ShapeDtypeStruct((2, 4, 4, 2, BLOCK, 128), BF)
    return pl.pallas_call(
        project_back_kernel,
        grid_spec=pltpu.PrefetchScalarGridSpec(
            num_scalar_prefetch=1,
            grid=(8,),
            in_specs=[
                whole_spec(KV_HEADS, 2, HEAD_DIM, WIDTH),
                whole_spec(rows, 640),
                whole_spec(rows, PAD),
                whole_spec(32, rows),
                whole_spec(32, rows),
                W_SPEC,
            ],
            out_specs=[whole_spec(rows, PAD), SMALL_SPEC, SMALL_SPEC],
            scratch_shapes=[
                pltpu.VMEM((D, rows), F32),
                pltpu.VMEM((320, rows), F32),
                pltpu.VMEM((320, rows), F32),
                pltpu.VMEM((120, rows), F32),
                pltpu.VMEM((2 * BLOCK, rows), F32),
                pltpu.VMEM((2, BLOCK, PAD), BF),
            ],
        ),
        out_shape=[jax.ShapeDtypeStruct((rows, PAD), F32), small, small],
        compiler_params=pltpu.CompilerParams(vmem_limit_bytes=VMEM_LIMIT),
        cost_estimate=pl.CostEstimate(flops=2 * 10**9, bytes_accessed=10 * 10**6, transcendentals=0),
    )(info, dq, dkv, normed, cosine, sine, w_all)


def feed_kernel(
    gate_ref, up_ref, down_ref, n_mine, n_other, dy_mine, dy_other,
    fed_mine, fed_other, dn_mine, dn_other, grad_ref, normed, dy, wg, wu, wd, fed, dn
):
    step = pl.program_id(0)
    rows = n_mine.shape[0]

    @pl.when(step == 0)
    def _():
        normed[:rows] = n_mine[...]
        normed[rows:] = n_other[...]
        dy[:rows] = dy_mine[...]
        dy[rows:] = dy_other[...]
        fed[...] = jnp.zeros_like(fed)
        dn[...] = jnp.zeros_like(dn)

    for group in range(4):
        part = slice(group * 160, group * 160 + 160)
        for at in range(8):
            lanes = slice(at * 128, at * 128 + 128)
            wg[part, lanes] = gate_ref[at % 4, group // 2, group % 2, at // 4]
            wu[part, lanes] = up_ref[at % 4, group // 2, group % 2, at // 4]
            wd[part, lanes] = down_ref[group, at // 2, at % 2, 0]
    gate = dot_last(normed[...], wg[...])
    upward = dot_last(normed[...], wu[...])
    dact = dot_last(dy[...], wd[...])
    sigma = jax.nn.sigmoid(gate)
    silu_gate = gate * sigma
    active = (silu_gate * upward).astype(BF)
    dgate = (dact * upward * sigma * (1.0 + gate * (1.0 - sigma))).astype(BF)
    dup = (dact * silu_gate).astype(BF)
    fed[...] += dot_plain(active, wd[...])
    dn[...] += dot_plain(dgate, wg[...]) + dot_plain(dup, wu[...])
    g_gate = dot_first(dgate, normed[...]).astype(BF)
    g_up = dot_first(dup, normed[...]).astype(BF)
    g_down = dot_first(active, dy[...]).astype(BF)
    for group in range(4):
        part = slice(group * 160, group * 160 + 160)
        for at in range(8):
            lanes = slice(at * 128, at * 128 + 128)
            grad_ref[at % 4, 2 * step + group // 2, group % 2, at // 4, 0:160] = g_gate[part, lanes]
            grad_ref[at % 4, 2 * step + group // 2, group % 2, at // 4, 160:320] = g_up[part, lanes]
            grad_ref[group, at // 2, at % 2, step, 320:480] = g_down[part, lanes]

    @pl.when(step == 1)
    def _():
        fed_mine[...] = fed[:rows]
        fed_other[...] = fed[rows:].astype(BF)
        dn_mine[...] = dn[:rows]
        dn_other[...] = dn[rows:].astype(BF)


def feed(big, n_mine, n_other, dy_mine, dy_other):
    rows = n_mine.shape[0]
    by_plane = (4, 2, 2, 2, 160, 128)

    def flat(*shape):
        return pl.BlockSpec(shape, lambda k: (0,) * len(shape))

    return pl.pallas_call(
        feed_kernel,
        grid=(2,),
        in_specs=[
            pl.BlockSpec(by_plane, lambda k: (0, k, 0, 0, 0, 0)),
            pl.BlockSpec(by_plane, lambda k: (0, k, 0, 0, 1, 0)),
            pl.BlockSpec((4, 4, 2, 1, 160, 128), lambda k: (0, 0, 0, k, 2, 0)),
        ]
        + [flat(rows, PAD)] * 4,
        out_specs=[flat(rows, PAD)] * 4 + [flat(4, 4, 2, 2, 544, 128)],
        out_shape=[
            jax.ShapeDtypeStruct((rows, PAD), F32),
            jax.ShapeDtypeStruct((rows, PAD), BF),
            jax.ShapeDtypeStruct((rows, PAD), F32),
            jax.ShapeDtypeStruct((rows, PAD), BF),
            jax.ShapeDtypeStruct((4, 4, 2, 2, 544, 128), BF),
        ],
        scratch_shapes=[pltpu.VMEM((2 * rows, PAD), BF)] * 2
        + [pltpu.VMEM((FEED, PAD), BF)] * 3
        + [pltpu.VMEM((2 * rows, PAD), F32)] * 2,
        compiler_params=pltpu.CompilerParams(vmem_limit_bytes=VMEM_LIMIT),
        cost_estimate=pl.CostEstimate(flops=12 * 10**9, bytes_accessed=22 * 10**6, transcendentals=10**6),
    )(big, big, big, n_mine, n_other, dy_mine, dy_other)


def by_half(value):
    rows = value.shape[1]
    split = value.reshape(KV_HEADS, GROUP, rows, 2, SPAN)
    return split.transpose(0, 3, 2, 1, 4).reshape(KV_HEADS, 2, rows, WIDTH)


def by_head(value):
    rows = value.shape[2]
    split = value.reshape(KV_HEADS, 2, rows, GROUP, SPAN)
    return split.transpose(0, 3, 2, 1, 4).reshape(HEADS, rows, 2 * SPAN)


def pad_rows(value, count):
    return jnp.pad(value, ((0, count - value.shape[0]), (0, 0)))


def norm_forward(value, gain):
    inverse = lax.rsqrt(jnp.sum(value * value, axis=-1, keepdims=True) / D + EPS)
    unit = value * inverse
    return unit, inverse, (unit * gain).astype(BF)


def norm_back(grad, unit, inverse, gain):
    scaled = grad * gain
    inner = jnp.sum(scaled * unit, axis=-1, keepdims=True) / D
    return inverse * (scaled - unit * inner), jnp.sum(grad * unit, axis=0)


def body(
    tokens,
    w_query,
    w_key,
    w_value,
    w_out,
    w_gate,
    w_up,
    w_down,
    attention_norm_gain,
    feedforward_norm_gain,
    span_order,
    positions,
    out_grad,
):
    rows = tokens.shape[0]
    core = lax.axis_index("c")
    me = lax.axis_index(("x", "zh", "c"))

    small = jnp.concatenate([pad_rows(w_query.T, 64), pad_rows(w_key.T, 24), pad_rows(w_value.T, 24)], axis=0)
    small = lax.all_to_all(jnp.broadcast_to(pad_lanes(small), (64, BLOCK, 128)), CHIPS, 0, 0, tiled=True)
    small = small.reshape(2, 4, 4, 2, BLOCK, 128)

    mixed = jnp.concatenate([w_down.reshape(2, 160, 60), w_out.reshape(2, 60, 60)], axis=1)
    mixed = lax.all_to_all(mixed, "c", 0, 0, tiled=True)
    mixed = jnp.concatenate([mixed[0], mixed[1]], axis=1)
    big = jnp.concatenate([w_gate.T, w_up.T, mixed], axis=0)
    big = gather_line(pad_rows(pad_lanes(big), 544))
    big, small = lax.optimization_barrier((big, small))
    big = lax.all_gather(big, PLANE, axis=0, tiled=True).reshape(4, 4, 2, 2, 544, 128)

    order = span_order[0]
    own_pair = lax.dynamic_slice_in_dim(order, 2 * me, 2)
    own_low_half = (own_pair[0] > own_pair[1]).astype(jnp.int32)
    spans = order.reshape(8, 2, 2)
    info = jnp.concatenate(
        [
            jnp.stack([own_low_half, jnp.minimum(own_pair[0], own_pair[1]), core.astype(jnp.int32)]),
            jnp.zeros((5,), jnp.int32),
            lax.dynamic_index_in_dim(spans, core, 1, keepdims=False).reshape(16),
            lax.dynamic_index_in_dim(spans, 1 - core, 1, keepdims=False).reshape(16),
        ]
    ).astype(jnp.int32)
    place = jnp.concatenate(
        [
            lax.dynamic_slice_in_dim(positions[0], own_pair[0] * SPAN, SPAN, 0),
            lax.dynamic_slice_in_dim(positions[0], own_pair[1] * SPAN, SPAN, 0),
        ]
    )
    half_dim = HEAD_DIM // 2
    freq = jnp.power(ROPE_BASE, -jnp.arange(half_dim, dtype=F32) / half_dim)
    angle = freq[:, None] * place.astype(F32)[None, :]
    cosine, sine = jnp.cos(angle), jnp.sin(angle)

    gain_one = pad_width(attention_norm_gain[None])
    gain_two = pad_width(feedforward_norm_gain[None])
    layer_input = pad_width(tokens).astype(F32)
    dy = pad_width(out_grad)
    dy_other = other_core(dy)

    unit_one, inverse_one, normed_one = norm_forward(layer_input, gain_one)
    w_all, query, kv_local = project(info, small, other_core(small), normed_one, cosine, sine)

    kv = lax.all_to_all(jnp.broadcast_to(kv_local, (8, rows, 640)), SEQ, 0, 0, tiled=True)
    kv = kv.reshape(8 * rows, 640)
    kv_other = other_core(kv)

    attended, total = attend(info, kv, kv_other, query)
    big, attended = lax.optimization_barrier((big, attended))
    attended = by_head(attended)
    total = by_head(total)
    attended_low = attended.astype(BF).reshape(16, 60, rows)
    attended_low = jnp.pad(attended_low, ((0, 0), (0, 4), (0, 0))).reshape(PAD, rows)

    w_out_h = big[:, :, :, :, 480:].transpose(3, 0, 4, 1, 2, 5).reshape(8, 64, PAD)
    w_out_o = other_core(w_out_h)
    first = core == 0
    w_out_full = jnp.stack(
        [jnp.where(first, w_out_h, w_out_o), jnp.where(first, w_out_o, w_out_h)], axis=1
    ).reshape(PAD, PAD)

    hidden = layer_input + dot_first(attended_low, w_out_full)
    unit_two, inverse_two, normed_two = norm_forward(hidden, gain_two)
    fed, fed_other, dn_two, dn_other, g_big = feed(big, normed_two, other_core(normed_two), dy, dy_other)
    dn_two = dn_two + other_core(dn_other).astype(F32)
    result = cut_width((hidden + (fed + other_core(fed_other).astype(F32))).astype(BF))

    back_two, gain_two_grad = norm_back(dn_two, unit_two, inverse_two, gain_two)
    dh = dy.astype(F32) + back_two
    dh_low = dh.astype(BF)
    dob = dot_last(w_out_full, dh_low).astype(BF).reshape(16, 64, rows)[:, :60]
    dob = dob.reshape(HEADS, HEAD_DIM, rows).astype(F32)
    dnum = (dob / total).astype(BF)
    delta = jnp.sum(dob * attended, axis=1, keepdims=True) / total

    g_out = dot_plain(attended_low, dh_low).astype(BF).reshape(8, 2, 64, PAD)
    keep = lax.dynamic_index_in_dim(g_out, core, 1, keepdims=False)
    give = lax.dynamic_index_in_dim(g_out, 1 - core, 1, keepdims=False)
    g_out = (keep.astype(F32) + other_core(give).astype(F32)).astype(BF)
    g_out = g_out.reshape(2, 4, 64, 4, 2, 128).transpose(1, 3, 4, 0, 2, 5)
    g_big = lax.dynamic_update_slice(g_big, g_out, (0, 0, 0, 0, 480, 0))
    g_big = lax.psum_scatter(g_big.reshape(64 * 544, 128), PLANE, scatter_dimension=0, tiled=True)
    g_big = lax.psum_scatter(g_big, LINE, scatter_dimension=0, tiled=True)

    dq, dkv, dkv_other = attend_back(info, kv, kv_other, query, by_half(dnum), by_half(delta))
    dkv = (dkv.astype(F32) + other_core(dkv_other).astype(F32)).astype(BF)
    dkv = lax.all_to_all(dkv.reshape(8, rows, 640), SEQ, 0, 0, tiled=True)
    dkv = jnp.sum(dkv.astype(F32), axis=0)

    dn_one, g_small, g_other = project_back(info, dq, dkv, normed_one, cosine, sine, w_all)
    back_one, gain_one_grad = norm_back(dn_one, unit_one, inverse_one, gain_one)
    input_grad = cut_width((dh + back_one).astype(BF))

    g_small = (g_small.astype(F32) + other_core(g_other).astype(F32)).astype(BF).reshape(64, BLOCK, 128)
    gains = jnp.stack([gain_one_grad, gain_two_grad])
    gains = gains + other_core(gains)
    gains_high = gains.astype(BF)
    gains_low = (gains - gains_high.astype(F32)).astype(BF)
    gains = jnp.concatenate([gains_high.reshape(16, 128), gains_low.reshape(16, 128)], axis=0)
    last = jnp.concatenate([g_small, jnp.broadcast_to(gains, (64, 32, 128))], axis=1)
    last = lax.all_to_all(last, CHIPS, 0, 0, tiled=True)
    last = jnp.sum(last.astype(F32), axis=0)
    gains = cut_width((last[BLOCK : BLOCK + 16] + last[BLOCK + 16 :]).reshape(2, PAD))

    g_big = g_big.astype(F32)
    mixed = g_big[320:540, :120].reshape(220, 2, 60).transpose(1, 0, 2)
    mixed = lax.all_to_all(mixed, "c", 0, 0, tiled=True)
    return (
        result,
        input_grad,
        last[:60, :120].T,
        last[64:84, :120].T,
        last[88:108, :120].T,
        mixed[:, 160:].reshape(120, 60),
        g_big[:160, :120].T,
        g_big[160:320, :120].T,
        mixed[:, :160].reshape(320, 60),
        gains[0],
        gains[1],
    )


def solution(mesh):
    fine = Mesh(mesh.devices.reshape(2, 4, 4, 2, 2), ("zl", "y", "x", "zh", "c"))
    shard, ctx = ("zl", "y"), ("x", "zh", "c")
    both = shard + ctx
    return jax.shard_map(
        body,
        mesh=fine,
        in_specs=(P(both, None),)
        + (P(shard, ctx),) * 7
        + (P(), P(), P(shard, None), P(shard, None), P(both, None)),
        out_specs=(P(both, None), P(both, None)) + (P(shard, ctx),) * 7 + (P(), P()),
        check_vma=False,
    )
```

```python
import jax
import jax.numpy as jnp
from jax import lax
from jax.experimental import pallas as pl
from jax.experimental.pallas import tpu as pltpu
from jax.sharding import Mesh
from jax.sharding import PartitionSpec as P

D = 960
HEADS = 15
KV_HEADS = 5
GROUP = 3
HEAD_DIM = 64
SPAN = 128
PAD = 1024

EPS = 1e-05
ROPE_BASE = 100000.0

BF = jnp.bfloat16
F32 = jnp.float32

PLANE = ("y", "x")
LINE = ("zh", "zl")
CHIPS = ("zl", "y", "x", "zh")
SEQ = ("x", "zh")
SWAP = [(0, 1), (1, 0)]


def pad_width(value):
    rows = value.shape[0]
    blocks = value.reshape(rows, 8, 120)
    return jnp.pad(blocks, ((0, 0), (0, 0), (0, 8))).reshape(rows, PAD)


def cut_width(value):
    rows = value.shape[0]
    return value.reshape(rows, 8, 128)[:, :, :120].reshape(rows, D)


def pad_lanes(value):
    return jnp.pad(value, ((0, 0), (0, 128 - value.shape[1])))


def other_core(value):
    return lax.ppermute(value, "c", SWAP)


def gather_line(block):
    ring = ("zl", "zh")
    held = jnp.stack(
        [block] + [lax.ppermute(block, ring, [(n, n ^ turn) for n in range(4)]) for turn in range(1, 4)]
    )
    here = lax.axis_index(ring)
    wanted = [lax.dynamic_index_in_dim(held, here ^ (2 * zl + zh), 0) for zh in range(2) for zl in range(2)]
    return jnp.concatenate(wanted, axis=0)


def sum_line(blocks):
    ring = ("zl", "zh")
    here = lax.axis_index(ring)

    def block_of(chip):
        return lax.dynamic_index_in_dim(blocks, 2 * (chip % 2) + chip // 2, 0, keepdims=False)

    total = block_of(here).astype(F32)
    for turn in range(1, 4):
        came = lax.ppermute(block_of(here ^ turn), ring, [(n, n ^ turn) for n in range(4)])
        total = total + came.astype(F32)
    return total


def dot_last(left, right):
    return lax.dot_general(left, right, (((1,), (1,)), ((), ())), preferred_element_type=F32)


def dot_first(left, right):
    return lax.dot_general(left, right, (((0,), (0,)), ((), ())), preferred_element_type=F32)


def dot_plain(left, right):
    return jnp.dot(left, right, preferred_element_type=F32)


VMEM_LIMIT = 56 * 1024 * 1024
WIDTH = GROUP * SPAN
TILES = 8
SUB = 2
STEP = TILES * SPAN
SEQ_LEN = 4096
FEED = 640


def sort_blocks(info, sources, target):
    def one(slot, carry):
        at = pl.ds(pl.multiple_of(slot * SPAN, SPAN), SPAN)
        for n, source in enumerate(sources):
            to = pl.ds(pl.multiple_of(info[8 + 16 * n + slot] * SPAN, SPAN), SPAN)
            target[to, :] = source[at, :]
        return carry

    lax.fori_loop(0, 16, one, 0)


def unsort_blocks(info, source, targets):
    def one(slot, carry):
        at = pl.ds(pl.multiple_of(slot * SPAN, SPAN), SPAN)
        for n, target in enumerate(targets):
            to = pl.ds(pl.multiple_of(info[8 + 16 * n + slot] * SPAN, SPAN), SPAN)
            target[at, :] = source[to, :].astype(target.dtype)
        return carry

    lax.fori_loop(0, 16, one, 0)


def causal_steps(info, tile):
    low_half, low = info[0], info[1]
    high = 31 - low
    low_last = lax.div(low, TILES)
    high_last = lax.div(high, TILES)

    def whole(step, carry):
        is_low = step < low_last
        tile(
            jnp.where(is_low, low_half, 1 - low_half),
            jnp.where(is_low, step, step - low_last),
            None,
        )
        return carry

    lax.fori_loop(0, 3, whole, 0, unroll=3)
    tile(low_half, low_last, (low - low_last * TILES) * SPAN)
    tile(1 - low_half, high_last, (high - high_last * TILES) * SPAN)


def key_rows_minus_query_lanes(rows):
    row = lax.broadcasted_iota(jnp.int32, (rows, WIDTH), 0)
    lane = lax.broadcasted_iota(jnp.int32, (rows, WIDTH), 1)
    return row - lax.rem(lane, SPAN)


def attend_kernel(info, mine_ref, other_ref, q_ref, out_ref, total_ref, keys_in_order, query, numer, total):
    sort_blocks(info, (mine_ref, other_ref), keys_in_order)
    query[...] = jnp.zeros_like(query)
    for half in range(2):
        query[half, :HEAD_DIM, :] = q_ref[0, half]
    numer[...] = jnp.zeros_like(numer)
    total[...] = jnp.zeros_like(total)

    def tile(half, step, limit):
        some = STEP // SUB
        parts, sums = [], []
        for n in range(SUB):
            keys = keys_in_order[pl.ds(pl.multiple_of(step * STEP + n * some, some), some), :]
            expo = jnp.exp(dot_plain(keys, query[half]))
            if limit is not None:
                expo = jnp.where(key_rows_minus_query_lanes(some) <= limit - n * some, expo, 0.0)
            parts.append(dot_plain(keys.T[HEAD_DIM:], expo.astype(BF)))
            sums.append(jnp.sum(expo.reshape(some // 8, 8, WIDTH), axis=0))
        numer[half] += sum(parts[1:], parts[0])
        total[half] += sum(sums[1:], sums[0])

    causal_steps(info, tile)
    for half in range(2):
        summed = jnp.sum(total[half], axis=0, keepdims=True)
        total_ref[0, half] = summed
        out_ref[0, half] = numer[half] / summed


HEAD_SPEC = pl.BlockSpec((1, 2, HEAD_DIM, WIDTH), lambda g, s: (g, 0, 0, 0))
ROW_SPEC = pl.BlockSpec((1, 2, 1, WIDTH), lambda g, s: (g, 0, 0, 0))
KV_SPEC = pl.BlockSpec((SEQ_LEN // 2, 2 * HEAD_DIM), lambda g, s: (0, g))
HEAD_F32 = jax.ShapeDtypeStruct((KV_HEADS, 2, HEAD_DIM, WIDTH), F32)


def attend(info, mine, other, query):
    return pl.pallas_call(
        attend_kernel,
        grid_spec=pltpu.PrefetchScalarGridSpec(
            num_scalar_prefetch=1,
            grid=(KV_HEADS,),
            in_specs=[KV_SPEC, KV_SPEC, HEAD_SPEC],
            out_specs=[HEAD_SPEC, ROW_SPEC],
            scratch_shapes=[
                pltpu.VMEM((SEQ_LEN, 2 * HEAD_DIM), BF),
                pltpu.VMEM((2, 2 * HEAD_DIM, WIDTH), BF),
                pltpu.VMEM((2, HEAD_DIM, WIDTH), F32),
                pltpu.VMEM((2, 8, WIDTH), F32),
            ],
        ),
        out_shape=[HEAD_F32, jax.ShapeDtypeStruct((KV_HEADS, 2, 1, WIDTH), F32)],
        compiler_params=pltpu.CompilerParams(vmem_limit_bytes=VMEM_LIMIT),
        cost_estimate=pl.CostEstimate(flops=4 * 10**9, bytes_accessed=8 * 10**6, transcendentals=8 * 10**6),
    )(info, mine, other, query)


def attend_back_kernel(
    info, mine_ref, other_ref, q_ref, dnum_ref, delta_ref, dq_ref, dmine_ref, dother_ref, keys_in_order, wide, tall, dq, dkv
):
    sort_blocks(info, (mine_ref, other_ref), keys_in_order)
    for half in range(2):
        zero = jnp.zeros((HEAD_DIM, WIDTH), BF)
        both = jnp.concatenate(
            [
                jnp.concatenate([q_ref[0, half], zero], axis=1),
                jnp.concatenate([zero, dnum_ref[0, half]], axis=1),
            ],
            axis=0,
        )
        wide[half] = both
        tall[half] = both.T
    dq[...] = jnp.zeros_like(dq)
    dkv[...] = jnp.zeros_like(dkv)

    def tile(half, step, limit):
        some = STEP // SUB
        parts = []
        for n in range(SUB):
            at = pl.ds(pl.multiple_of(step * STEP + n * some, some), some)
            keys = keys_in_order[at, :]
            scores = dot_plain(keys, wide[half])
            expo = jnp.exp(scores[:, :WIDTH])
            if limit is not None:
                expo = jnp.where(key_rows_minus_query_lanes(some) <= limit - n * some, expo, 0.0)
            grads = (expo * (scores[:, WIDTH:] - delta_ref[0, half])).astype(BF)
            pair = jnp.concatenate([grads, expo.astype(BF)], axis=1)
            dkv[at, :] += dot_plain(pair, tall[half])
            parts.append(dot_plain(keys.T[:HEAD_DIM], grads))
        dq[half] += sum(parts[1:], parts[0])

    causal_steps(info, tile)
    for half in range(2):
        dq_ref[0, half] = dq[half] * (HEAD_DIM**-0.5)
    unsort_blocks(info, dkv, (dmine_ref, dother_ref))


def attend_back(info, mine, other, query, dnum, delta):
    return pl.pallas_call(
        attend_back_kernel,
        grid_spec=pltpu.PrefetchScalarGridSpec(
            num_scalar_prefetch=1,
            grid=(KV_HEADS,),
            in_specs=[KV_SPEC, KV_SPEC, HEAD_SPEC, HEAD_SPEC, ROW_SPEC],
            out_specs=[HEAD_SPEC, KV_SPEC, KV_SPEC],
            scratch_shapes=[
                pltpu.VMEM((SEQ_LEN, 2 * HEAD_DIM), BF),
                pltpu.VMEM((2, 2 * HEAD_DIM, 2 * WIDTH), BF),
                pltpu.VMEM((2, 2 * WIDTH, 2 * HEAD_DIM), BF),
                pltpu.VMEM((2, HEAD_DIM, WIDTH), F32),
                pltpu.VMEM((SEQ_LEN, 2 * HEAD_DIM), F32),
            ],
        ),
        out_shape=[HEAD_F32] + [jax.ShapeDtypeStruct(mine.shape, BF)] * 2,
        compiler_params=pltpu.CompilerParams(vmem_limit_bytes=VMEM_LIMIT),
        cost_estimate=pl.CostEstimate(flops=10 * 10**9, bytes_accessed=12 * 10**6, transcendentals=8 * 10**6),
    )(info, mine, other, query, dnum, delta)


PARTS = ((0, 60), (64, 20), (88, 20))
BLOCK = 112


def project_kernel(info, mine_ref, other_ref, normed_ref, cos_ref, sin_ref, w_ref, query_ref, kv_ref, q_rows, k_rows, v_rows, pair):
    step = pl.program_id(0)
    core = info[2]
    for at in range(8):
        lanes = slice(at * 128, at * 128 + 128)
        w_ref[0, core, :, lanes] = mine_ref[at // 4, at % 4, 0, 0]
        w_ref[0, 1 - core, :, lanes] = other_ref[at // 4, at % 4, 0, 0]
    made = dot_last(w_ref[0].reshape(2 * BLOCK, PAD), normed_ref[...])
    for (start, count), rows in zip(PARTS, (q_rows, k_rows, v_rows)):
        pair[0:count] = made[start : start + count]
        pair[count : 2 * count] = made[BLOCK + start : BLOCK + start + count]
        rows[pl.ds(pl.multiple_of(step * 2 * count, 8), 2 * count), :] = pair[0 : 2 * count]

    @pl.when(step == 7)
    def _():
        cosine, sine = cos_ref[...], sin_ref[...]

        def turned(rows, head):
            first = rows[head * 64 : head * 64 + 32]
            second = rows[head * 64 + 32 : head * 64 + 64]
            return jnp.concatenate([first * cosine - second * sine, second * cosine + first * sine], axis=0)

        for g in range(KV_HEADS):
            for r in range(GROUP):
                head = turned(q_rows, GROUP * g + r).astype(BF) * BF(HEAD_DIM**-0.5)
                for half in range(2):
                    query_ref[g, half, :, r * SPAN : (r + 1) * SPAN] = head[:, half * SPAN : (half + 1) * SPAN]
            both = jnp.concatenate([turned(k_rows, g), v_rows[g * 64 : g * 64 + 64]], axis=0)
            kv_ref[:, g * 128 : (g + 1) * 128] = both.T.astype(BF)


def whole_spec(*shape):
    return pl.BlockSpec(shape, lambda j, s: (0,) * len(shape))


SMALL_SPEC = pl.BlockSpec((2, 4, 1, 1, BLOCK, 128), lambda j, s: (0, 0, j // 2, j % 2, 0, 0))
W_SPEC = pl.BlockSpec((1, 2, BLOCK, PAD), lambda j, s: (j, 0, 0, 0))


def project(info, mine, other, normed, cosine, sine):
    rows = normed.shape[0]
    return pl.pallas_call(
        project_kernel,
        grid_spec=pltpu.PrefetchScalarGridSpec(
            num_scalar_prefetch=1,
            grid=(8,),
            in_specs=[SMALL_SPEC, SMALL_SPEC, whole_spec(rows, PAD), whole_spec(32, rows), whole_spec(32, rows)],
            out_specs=[W_SPEC, whole_spec(KV_HEADS, 2, HEAD_DIM, WIDTH), whole_spec(rows, 640)],
            scratch_shapes=[
                pltpu.VMEM((D, rows), F32),
                pltpu.VMEM((320, rows), F32),
                pltpu.VMEM((320, rows), F32),
                pltpu.VMEM((120, rows), F32),
            ],
        ),
        out_shape=[
            jax.ShapeDtypeStruct((8, 2, BLOCK, PAD), BF),
            jax.ShapeDtypeStruct((KV_HEADS, 2, HEAD_DIM, WIDTH), BF),
            jax.ShapeDtypeStruct((rows, 640), BF),
        ],
        compiler_params=pltpu.CompilerParams(vmem_limit_bytes=VMEM_LIMIT),
        cost_estimate=pl.CostEstimate(flops=10**9, bytes_accessed=8 * 10**6, transcendentals=0),
    )(info, mine, other, normed, cosine, sine)


def project_back_kernel(
    info, dq_ref, dkv_ref, normed_ref, cos_ref, sin_ref, w_ref, dn_ref, mine_ref, other_ref, q_rows, k_rows, v_rows, pair, blocks, grads
):
    step = pl.program_id(0)
    core = info[2]

    @pl.when(step == 0)
    def _():
        cosine, sine = cos_ref[...], sin_ref[...]

        def turned_back(value):
            first, second = value[:32], value[32:]
            return jnp.concatenate([first * cosine + second * sine, second * cosine - first * sine], axis=0)

        for g in range(KV_HEADS):
            for r in range(GROUP):
                lanes = slice(r * SPAN, (r + 1) * SPAN)
                head = jnp.concatenate([dq_ref[g, 0, :, lanes], dq_ref[g, 1, :, lanes]], axis=1)
                at = (GROUP * g + r) * 64
                q_rows[at : at + 64] = turned_back(head)
            both = dkv_ref[:, g * 128 : (g + 1) * 128].T
            k_rows[g * 64 : g * 64 + 64] = turned_back(both[:64])
            v_rows[g * 64 : g * 64 + 64] = both[64:]
        blocks[...] = jnp.zeros_like(blocks)
        dn_ref[...] = jnp.zeros_like(dn_ref)

    for (start, count), rows in zip(PARTS, (q_rows, k_rows, v_rows)):
        pair[0 : 2 * count] = rows[pl.ds(pl.multiple_of(step * 2 * count, 8), 2 * count), :]
        blocks[start : start + count] = pair[0:count]
        blocks[BLOCK + start : BLOCK + start + count] = pair[count : 2 * count]
    block = blocks[...].astype(BF)
    dn_ref[...] += dot_first(block, w_ref[0].reshape(2 * BLOCK, PAD))
    grads[...] = dot_plain(block, normed_ref[...]).astype(BF).reshape(2, BLOCK, PAD)
    for at in range(8):
        lanes = slice(at * 128, at * 128 + 128)
        mine_ref[at // 4, at % 4, 0, 0] = grads[core, :, lanes]
        other_ref[at // 4, at % 4, 0, 0] = grads[1 - core, :, lanes]


def project_back(info, dq, dkv, normed, cosine, sine, w_all):
    rows = normed.shape[0]
    small = jax.ShapeDtypeStruct((2, 4, 4, 2, BLOCK, 128), BF)
    return pl.pallas_call(
        project_back_kernel,
        grid_spec=pltpu.PrefetchScalarGridSpec(
            num_scalar_prefetch=1,
            grid=(8,),
            in_specs=[
                whole_spec(KV_HEADS, 2, HEAD_DIM, WIDTH),
                whole_spec(rows, 640),
                whole_spec(rows, PAD),
                whole_spec(32, rows),
                whole_spec(32, rows),
                W_SPEC,
            ],
            out_specs=[whole_spec(rows, PAD), SMALL_SPEC, SMALL_SPEC],
            scratch_shapes=[
                pltpu.VMEM((D, rows), F32),
                pltpu.VMEM((320, rows), F32),
                pltpu.VMEM((320, rows), F32),
                pltpu.VMEM((120, rows), F32),
                pltpu.VMEM((2 * BLOCK, rows), F32),
                pltpu.VMEM((2, BLOCK, PAD), BF),
            ],
        ),
        out_shape=[jax.ShapeDtypeStruct((rows, PAD), F32), small, small],
        compiler_params=pltpu.CompilerParams(vmem_limit_bytes=VMEM_LIMIT),
        cost_estimate=pl.CostEstimate(flops=2 * 10**9, bytes_accessed=10 * 10**6, transcendentals=0),
    )(info, dq, dkv, normed, cosine, sine, w_all)


def feed_kernel(
    gate_ref, up_ref, down_ref, n_mine, n_other, dy_mine, dy_other,
    fed_mine, fed_other, dn_mine, dn_other, grad_ref, normed, dy, wg, wu, wd, fed, dn
):
    step = pl.program_id(0)
    rows = n_mine.shape[0]

    @pl.when(step == 0)
    def _():
        normed[:rows] = n_mine[...]
        normed[rows:] = n_other[...]
        dy[:rows] = dy_mine[...]
        dy[rows:] = dy_other[...]
        fed[...] = jnp.zeros_like(fed)
        dn[...] = jnp.zeros_like(dn)

    for group in range(4):
        part = slice(group * 160, group * 160 + 160)
        for at in range(8):
            lanes = slice(at * 128, at * 128 + 128)
            wg[part, lanes] = gate_ref[at % 4, group // 2, group % 2, at // 4]
            wu[part, lanes] = up_ref[at % 4, group // 2, group % 2, at // 4]
            wd[part, lanes] = down_ref[group, at // 2, at % 2, 0]
    gate = dot_last(normed[...], wg[...])
    upward = dot_last(normed[...], wu[...])
    dact = dot_last(dy[...], wd[...])
    sigma = jax.nn.sigmoid(gate)
    silu_gate = gate * sigma
    active = (silu_gate * upward).astype(BF)
    dgate = (dact * upward * sigma * (1.0 + gate * (1.0 - sigma))).astype(BF)
    dup = (dact * silu_gate).astype(BF)
    fed[...] += dot_plain(active, wd[...])
    dn[...] += dot_plain(dgate, wg[...]) + dot_plain(dup, wu[...])
    g_gate = dot_first(dgate, normed[...]).astype(BF)
    g_up = dot_first(dup, normed[...]).astype(BF)
    g_down = dot_first(active, dy[...]).astype(BF)
    for group in range(4):
        part = slice(group * 160, group * 160 + 160)
        for at in range(8):
            lanes = slice(at * 128, at * 128 + 128)
            grad_ref[at % 4, 2 * step + group // 2, group % 2, at // 4, 0:160] = g_gate[part, lanes]
            grad_ref[at % 4, 2 * step + group // 2, group % 2, at // 4, 160:320] = g_up[part, lanes]
            grad_ref[group, at // 2, at % 2, step, 320:480] = g_down[part, lanes]

    @pl.when(step == 1)
    def _():
        fed_mine[...] = fed[:rows]
        fed_other[...] = fed[rows:].astype(BF)
        dn_mine[...] = dn[:rows]
        dn_other[...] = dn[rows:].astype(BF)


def feed(big, n_mine, n_other, dy_mine, dy_other):
    rows = n_mine.shape[0]
    by_plane = (4, 2, 2, 2, 160, 128)

    def flat(*shape):
        return pl.BlockSpec(shape, lambda k: (0,) * len(shape))

    return pl.pallas_call(
        feed_kernel,
        grid=(2,),
        in_specs=[
            pl.BlockSpec(by_plane, lambda k: (0, k, 0, 0, 0, 0)),
            pl.BlockSpec(by_plane, lambda k: (0, k, 0, 0, 1, 0)),
            pl.BlockSpec((4, 4, 2, 1, 160, 128), lambda k: (0, 0, 0, k, 2, 0)),
        ]
        + [flat(rows, PAD)] * 4,
        out_specs=[flat(rows, PAD)] * 4 + [flat(4, 4, 2, 2, 544, 128)],
        out_shape=[
            jax.ShapeDtypeStruct((rows, PAD), F32),
            jax.ShapeDtypeStruct((rows, PAD), BF),
            jax.ShapeDtypeStruct((rows, PAD), F32),
            jax.ShapeDtypeStruct((rows, PAD), BF),
            jax.ShapeDtypeStruct((4, 4, 2, 2, 544, 128), BF),
        ],
        scratch_shapes=[pltpu.VMEM((2 * rows, PAD), BF)] * 2
        + [pltpu.VMEM((FEED, PAD), BF)] * 3
        + [pltpu.VMEM((2 * rows, PAD), F32)] * 2,
        compiler_params=pltpu.CompilerParams(vmem_limit_bytes=VMEM_LIMIT),
        cost_estimate=pl.CostEstimate(flops=12 * 10**9, bytes_accessed=22 * 10**6, transcendentals=10**6),
    )(big, big, big, n_mine, n_other, dy_mine, dy_other)


def project_out_kernel(info, o_ref, mine_ref, other_ref, x_ref, gain_ref, hidden_ref, normed_ref, w_ref, ob_ref, rows):
    core = info[2]
    for s in range(8):
        for j in range(8):
            lanes = slice(j * 128, j * 128 + 128)
            w_ref[s, core, :, lanes] = mine_ref[s % 4, j // 2, j % 2, s // 4]
            w_ref[s, 1 - core, :, lanes] = other_ref[s % 4, j // 2, j % 2, s // 4]
    for head in range(HEADS):
        g, r = head // GROUP, head % GROUP
        for half in range(2):
            piece = o_ref[g, half, :, r * SPAN : (r + 1) * SPAN]
            rows[head * 64 : head * 64 + 64, half * SPAN : (half + 1) * SPAN] = piece
    ob_ref[...] = jnp.zeros_like(ob_ref)
    for n in range(16):
        ob_ref[n * 64 : n * 64 + 60] = rows[n * 60 : n * 60 + 60].astype(BF)
    hidden = x_ref[...] + dot_first(ob_ref[...], w_ref[...].reshape(PAD, PAD))
    hidden_ref[...] = hidden
    inverse = lax.rsqrt(jnp.sum(hidden * hidden, axis=-1, keepdims=True) / D + EPS)
    normed_ref[...] = (hidden * inverse * gain_ref[...]).astype(BF)


def one_call(kernel, info, args, outs, scratch, flops):
    return pl.pallas_call(
        kernel,
        in_specs=[pl.BlockSpec(memory_space=pltpu.SMEM)] + [pl.BlockSpec(memory_space=pltpu.VMEM)] * len(args),
        out_specs=[pl.BlockSpec(memory_space=pltpu.VMEM)] * len(outs),
        out_shape=[jax.ShapeDtypeStruct(shape, kind) for shape, kind in outs],
        scratch_shapes=scratch,
        compiler_params=pltpu.CompilerParams(vmem_limit_bytes=VMEM_LIMIT),
        cost_estimate=pl.CostEstimate(flops=flops, bytes_accessed=10 * 10**6, transcendentals=0),
    )(info, *args)


def project_out(info, attended, mine, other, layer_input, gain):
    rows = layer_input.shape[0]
    return one_call(
        project_out_kernel,
        info,
        (attended, mine, other, layer_input, gain),
        [((rows, PAD), F32), ((rows, PAD), BF), ((8, 2, 64, PAD), BF), ((PAD, rows), BF)],
        [pltpu.VMEM((D, rows), F32)],
        10**9,
    )


def between_kernel(
    info, dn_ref, dn_other_ref, hidden_ref, gain_ref, dy_ref, w_ref, ob_ref, o_ref, total_ref,
    dh_ref, dnum_ref, delta_ref, mine_ref, other_ref, gain_grad_ref, rows, grads
):
    core = info[2]
    hidden, gain = hidden_ref[...], gain_ref[...]
    inverse = lax.rsqrt(jnp.sum(hidden * hidden, axis=-1, keepdims=True) / D + EPS)
    unit = hidden * inverse
    dn = dn_ref[...] + dn_other_ref[...].astype(F32)
    back, gain_grad = norm_back(dn, unit, inverse, gain)
    gain_grad_ref[...] = gain_grad[None]
    dh = dy_ref[...].astype(F32) + back
    dh_ref[...] = dh
    dh_low = dh.astype(BF)
    dob = dot_last(w_ref[...].reshape(PAD, PAD), dh_low)
    for n in range(16):
        rows[n * 60 : n * 60 + 60] = dob[n * 64 : n * 64 + 60].astype(BF).astype(F32)
    for head in range(HEADS):
        g, r = head // GROUP, head % GROUP
        for half in range(2):
            lanes = slice(r * SPAN, (r + 1) * SPAN)
            piece = rows[head * 64 : head * 64 + 64, half * SPAN : (half + 1) * SPAN]
            total = total_ref[g, half, :, lanes]
            dnum_ref[g, half, :, lanes] = (piece / total).astype(BF)
            summed = jnp.sum(piece * o_ref[g, half, :, lanes], axis=0, keepdims=True)
            delta_ref[g, half, :, lanes] = summed / total
    grads[...] = dot_plain(ob_ref[...], dh_low).astype(BF).reshape(8, 2, 64, PAD)
    for s in range(8):
        for j in range(8):
            lanes = slice(j * 128, j * 128 + 128)
            mine_ref[s % 4, j // 2, j % 2, s // 4] = grads[s, core, :, lanes]
            other_ref[s % 4, j // 2, j % 2, s // 4] = grads[s, 1 - core, :, lanes]


def between(info, dn, dn_other, hidden, gain, dy, w_out, attended_low, attended, total):
    rows = hidden.shape[0]
    return one_call(
        between_kernel,
        info,
        (dn, dn_other, hidden, gain, dy, w_out, attended_low, attended, total),
        [
            ((rows, PAD), F32),
            ((KV_HEADS, 2, HEAD_DIM, WIDTH), BF),
            ((KV_HEADS, 2, 1, WIDTH), F32),
            ((4, 4, 2, 2, 64, 128), BF),
            ((4, 4, 2, 2, 64, 128), BF),
            ((1, PAD), F32),
        ],
        [pltpu.VMEM((D, rows), F32), pltpu.VMEM((8, 2, 64, PAD), BF)],
        2 * 10**9,
    )


def pad_rows(value, count):
    return jnp.pad(value, ((0, count - value.shape[0]), (0, 0)))


def norm_forward(value, gain):
    inverse = lax.rsqrt(jnp.sum(value * value, axis=-1, keepdims=True) / D + EPS)
    unit = value * inverse
    return unit, inverse, (unit * gain).astype(BF)


def norm_back(grad, unit, inverse, gain):
    scaled = grad * gain
    inner = jnp.sum(scaled * unit, axis=-1, keepdims=True) / D
    return inverse * (scaled - unit * inner), jnp.sum(grad * unit, axis=0)


def body(
    tokens,
    w_query,
    w_key,
    w_value,
    w_out,
    w_gate,
    w_up,
    w_down,
    attention_norm_gain,
    feedforward_norm_gain,
    span_order,
    positions,
    out_grad,
):
    rows = tokens.shape[0]
    core = lax.axis_index("c")
    me = lax.axis_index(("x", "zh", "c"))

    mixed = jnp.concatenate([w_down.reshape(2, 160, 60), w_out.reshape(2, 60, 60)], axis=1)
    mixed = lax.all_to_all(mixed, "c", 0, 0, tiled=True)
    mixed = jnp.concatenate([mixed[0], mixed[1]], axis=1)
    big = jnp.concatenate([w_gate.T, w_up.T, mixed], axis=0)
    big = gather_line(pad_rows(pad_lanes(big), 544))
    small = jnp.concatenate([pad_rows(w_query.T, 64), pad_rows(w_key.T, 24), pad_rows(w_value.T, 24)], axis=0)
    small = pad_lanes(small)
    big, small = lax.optimization_barrier((big, small))
    big = lax.all_gather(big, PLANE, axis=0, tiled=True).reshape(4, 4, 2, 2, 544, 128)
    small = lax.all_to_all(jnp.broadcast_to(small, (64, BLOCK, 128)), CHIPS, 0, 0, tiled=True)
    small = small.reshape(2, 4, 4, 2, BLOCK, 128)

    order = span_order[0]
    own_pair = lax.dynamic_slice_in_dim(order, 2 * me, 2)
    own_low_half = (own_pair[0] > own_pair[1]).astype(jnp.int32)
    spans = order.reshape(8, 2, 2)
    info = jnp.concatenate(
        [
            jnp.stack([own_low_half, jnp.minimum(own_pair[0], own_pair[1]), core.astype(jnp.int32)]),
            jnp.zeros((5,), jnp.int32),
            lax.dynamic_index_in_dim(spans, core, 1, keepdims=False).reshape(16),
            lax.dynamic_index_in_dim(spans, 1 - core, 1, keepdims=False).reshape(16),
        ]
    ).astype(jnp.int32)
    place = jnp.concatenate(
        [
            lax.dynamic_slice_in_dim(positions[0], own_pair[0] * SPAN, SPAN, 0),
            lax.dynamic_slice_in_dim(positions[0], own_pair[1] * SPAN, SPAN, 0),
        ]
    )
    half_dim = HEAD_DIM // 2
    freq = jnp.power(ROPE_BASE, -jnp.arange(half_dim, dtype=F32) / half_dim)
    angle = freq[:, None] * place.astype(F32)[None, :]
    cosine, sine = jnp.cos(angle), jnp.sin(angle)

    gain_one = pad_width(attention_norm_gain[None])
    gain_two = pad_width(feedforward_norm_gain[None])
    layer_input = pad_width(tokens).astype(F32)
    dy = pad_width(out_grad)
    dy_other = other_core(dy)

    unit_one, inverse_one, normed_one = norm_forward(layer_input, gain_one)
    w_all, query, kv_local = project(info, small, other_core(small), normed_one, cosine, sine)

    kv = lax.all_to_all(jnp.broadcast_to(kv_local, (8, rows, 640)), SEQ, 0, 0, tiled=True)
    kv = kv.reshape(8 * rows, 640)
    kv_other = other_core(kv)

    w_out_mine = big[:, :, :, :, 480:]
    attended, total = attend(info, kv, kv_other, query)
    hidden, normed_two, w_out_full, attended_low = project_out(
        info, attended, w_out_mine, other_core(w_out_mine), layer_input, gain_two
    )
    fed, fed_other, dn_two, dn_other, g_big = feed(big, normed_two, other_core(normed_two), dy, dy_other)
    dh, dnum, delta, g_out, g_out_other, gain_two_grad = between(
        info, dn_two, other_core(dn_other), hidden, gain_two, dy, w_out_full, attended_low, attended, total
    )
    result = cut_width((hidden + (fed + other_core(fed_other).astype(F32))).astype(BF))

    g_out = (g_out.astype(F32) + other_core(g_out_other).astype(F32)).astype(BF)
    g_big = lax.dynamic_update_slice(g_big, g_out, (0, 0, 0, 0, 480, 0))
    g_big = lax.psum_scatter(g_big.reshape(64 * 544, 128), PLANE, scatter_dimension=0, tiled=True)
    g_big = sum_line(g_big.reshape(4, 544, 128))

    dq, dkv, dkv_other = attend_back(info, kv, kv_other, query, dnum, delta)
    dkv = (dkv.astype(F32) + other_core(dkv_other).astype(F32)).astype(BF)
    dkv = lax.all_to_all(dkv.reshape(8, rows, 640), SEQ, 0, 0, tiled=True)
    dkv = jnp.sum(dkv.astype(F32), axis=0)

    dn_one, g_small, g_other = project_back(info, dq, dkv, normed_one, cosine, sine, w_all)
    back_one, gain_one_grad = norm_back(dn_one, unit_one, inverse_one, gain_one)
    input_grad = cut_width((dh + back_one).astype(BF))

    g_small = (g_small.astype(F32) + other_core(g_other).astype(F32)).astype(BF).reshape(64, BLOCK, 128)
    gains = jnp.stack([gain_one_grad, gain_two_grad[0]])
    gains = gains + other_core(gains)
    gains_high = gains.astype(BF)
    gains_low = (gains - gains_high.astype(F32)).astype(BF)
    gains = jnp.concatenate([gains_high.reshape(16, 128), gains_low.reshape(16, 128)], axis=0)
    last = jnp.concatenate([g_small, jnp.broadcast_to(gains, (64, 32, 128))], axis=1)
    last, g_big = lax.optimization_barrier((last, g_big))
    last = lax.all_to_all(last, CHIPS, 0, 0, tiled=True)
    last = jnp.sum(last.astype(F32), axis=0)
    gains = cut_width((last[BLOCK : BLOCK + 16] + last[BLOCK + 16 :]).reshape(2, PAD))

    mixed = g_big[320:540, :120].reshape(220, 2, 60).transpose(1, 0, 2)
    mixed = lax.all_to_all(mixed, "c", 0, 0, tiled=True)
    return (
        result,
        input_grad,
        last[:60, :120].T,
        last[64:84, :120].T,
        last[88:108, :120].T,
        mixed[:, 160:].reshape(120, 60),
        g_big[:160, :120].T,
        g_big[160:320, :120].T,
        mixed[:, :160].reshape(320, 60),
        gains[0],
        gains[1],
    )


def solution(mesh):
    fine = Mesh(mesh.devices.reshape(2, 4, 4, 2, 2), ("zl", "y", "x", "zh", "c"))
    shard, ctx = ("zl", "y"), ("x", "zh", "c")
    both = shard + ctx
    return jax.shard_map(
        body,
        mesh=fine,
        in_specs=(P(both, None),)
        + (P(shard, ctx),) * 7
        + (P(), P(), P(shard, None), P(shard, None), P(both, None)),
        out_specs=(P(both, None), P(both, None)) + (P(shard, ctx),) * 7 + (P(), P()),
        check_vma=False,
    )
```

```python
import jax
import jax.numpy as jnp
from jax import lax
from jax.experimental import pallas as pl
from jax.experimental.pallas import tpu as pltpu
from jax.sharding import Mesh
from jax.sharding import PartitionSpec as P

D = 960
HEADS = 15
KV_HEADS = 5
GROUP = 3
HEAD_DIM = 64
SPAN = 128
PAD = 1024

EPS = 1e-05
ROPE_BASE = 100000.0

BF = jnp.bfloat16
F32 = jnp.float32

PLANE = ("y", "x")
LINE = ("zh", "zl")
CHIPS = ("zl", "y", "x", "zh")
SEQ = ("x", "zh")
SWAP = [(0, 1), (1, 0)]


def pad_width(value):
    rows = value.shape[0]
    blocks = value.reshape(rows, 8, 120)
    return jnp.pad(blocks, ((0, 0), (0, 0), (0, 8))).reshape(rows, PAD)


def cut_width(value):
    rows = value.shape[0]
    return value.reshape(rows, 8, 128)[:, :, :120].reshape(rows, D)


def pad_lanes(value):
    return jnp.pad(value, ((0, 0), (0, 128 - value.shape[1])))


def other_core(value):
    return lax.ppermute(value, "c", SWAP)


def sum_line(blocks):
    ring = ("zl", "zh")
    here = lax.axis_index(ring)

    def block_of(chip):
        return lax.dynamic_index_in_dim(blocks, 2 * (chip % 2) + chip // 2, 0, keepdims=False)

    total = block_of(here).astype(F32)
    for turn in range(1, 4):
        came = lax.ppermute(block_of(here ^ turn), ring, [(n, n ^ turn) for n in range(4)])
        total = total + came.astype(F32)
    return total


def to_chips(blocks):
    return lax.all_to_all(blocks, CHIPS, 0, 0, tiled=True)


def high_and_low(value):
    high = value.astype(BF)
    low = (value - high.astype(F32)).astype(BF)
    return jnp.concatenate([high.reshape(8, 128), low.reshape(8, 128)], axis=0)


def dot_last(left, right):
    return lax.dot_general(left, right, (((1,), (1,)), ((), ())), preferred_element_type=F32)


def dot_first(left, right):
    return lax.dot_general(left, right, (((0,), (0,)), ((), ())), preferred_element_type=F32)


def dot_plain(left, right):
    return jnp.dot(left, right, preferred_element_type=F32)


VMEM_LIMIT = 56 * 1024 * 1024
WIDTH = GROUP * SPAN
TILES = 8
SUB = 2
STEP = TILES * SPAN
SEQ_LEN = 4096
FEED = 640


def sort_blocks(info, sources, target):
    def one(slot, carry):
        at = pl.ds(pl.multiple_of(slot * SPAN, SPAN), SPAN)
        for n, source in enumerate(sources):
            to = pl.ds(pl.multiple_of(info[8 + 16 * n + slot] * SPAN, SPAN), SPAN)
            target[to, :] = source[at, :]
        return carry

    lax.fori_loop(0, 16, one, 0)


def unsort_blocks(info, source, targets):
    def one(slot, carry):
        at = pl.ds(pl.multiple_of(slot * SPAN, SPAN), SPAN)
        for n, target in enumerate(targets):
            to = pl.ds(pl.multiple_of(info[8 + 16 * n + slot] * SPAN, SPAN), SPAN)
            target[at, :] = source[to, :].astype(target.dtype)
        return carry

    lax.fori_loop(0, 16, one, 0)


def causal_steps(info, tile):
    low_half, low = info[0], info[1]
    high = 31 - low
    low_last = lax.div(low, TILES)
    high_last = lax.div(high, TILES)

    def whole(step, carry):
        is_low = step < low_last
        tile(
            jnp.where(is_low, low_half, 1 - low_half),
            jnp.where(is_low, step, step - low_last),
            None,
        )
        return carry

    lax.fori_loop(0, 3, whole, 0, unroll=3)
    tile(low_half, low_last, (low - low_last * TILES) * SPAN)
    tile(1 - low_half, high_last, (high - high_last * TILES) * SPAN)


def key_rows_minus_query_lanes(rows):
    row = lax.broadcasted_iota(jnp.int32, (rows, WIDTH), 0)
    lane = lax.broadcasted_iota(jnp.int32, (rows, WIDTH), 1)
    return row - lax.rem(lane, SPAN)


def attend_kernel(info, mine_ref, other_ref, q_ref, out_ref, total_ref, keys_in_order, query, numer, total):
    sort_blocks(info, (mine_ref, other_ref), keys_in_order)
    query[...] = jnp.zeros_like(query)
    for half in range(2):
        query[half, :HEAD_DIM, :] = q_ref[0, half]
    numer[...] = jnp.zeros_like(numer)
    total[...] = jnp.zeros_like(total)

    def tile(half, step, limit):
        some = STEP // SUB
        parts, sums = [], []
        for n in range(SUB):
            keys = keys_in_order[pl.ds(pl.multiple_of(step * STEP + n * some, some), some), :]
            expo = jnp.exp(dot_plain(keys, query[half]))
            if limit is not None:
                expo = jnp.where(key_rows_minus_query_lanes(some) <= limit - n * some, expo, 0.0)
            parts.append(dot_plain(keys.T[HEAD_DIM:], expo.astype(BF)))
            sums.append(jnp.sum(expo.reshape(some // 8, 8, WIDTH), axis=0))
        numer[half] += sum(parts[1:], parts[0])
        total[half] += sum(sums[1:], sums[0])

    causal_steps(info, tile)
    for half in range(2):
        summed = jnp.sum(total[half], axis=0, keepdims=True)
        total_ref[0, half] = summed
        out_ref[0, half] = numer[half] / summed


HEAD_SPEC = pl.BlockSpec((1, 2, HEAD_DIM, WIDTH), lambda g, s: (g, 0, 0, 0))
ROW_SPEC = pl.BlockSpec((1, 2, 1, WIDTH), lambda g, s: (g, 0, 0, 0))
KV_SPEC = pl.BlockSpec((SEQ_LEN // 2, 2 * HEAD_DIM), lambda g, s: (0, g))
HEAD_F32 = jax.ShapeDtypeStruct((KV_HEADS, 2, HEAD_DIM, WIDTH), F32)


def attend(info, mine, other, query):
    return pl.pallas_call(
        attend_kernel,
        grid_spec=pltpu.PrefetchScalarGridSpec(
            num_scalar_prefetch=1,
            grid=(KV_HEADS,),
            in_specs=[KV_SPEC, KV_SPEC, HEAD_SPEC],
            out_specs=[HEAD_SPEC, ROW_SPEC],
            scratch_shapes=[
                pltpu.VMEM((SEQ_LEN, 2 * HEAD_DIM), BF),
                pltpu.VMEM((2, 2 * HEAD_DIM, WIDTH), BF),
                pltpu.VMEM((2, HEAD_DIM, WIDTH), F32),
                pltpu.VMEM((2, 8, WIDTH), F32),
            ],
        ),
        out_shape=[HEAD_F32, jax.ShapeDtypeStruct((KV_HEADS, 2, 1, WIDTH), F32)],
        compiler_params=pltpu.CompilerParams(vmem_limit_bytes=VMEM_LIMIT),
        cost_estimate=pl.CostEstimate(flops=4 * 10**9, bytes_accessed=8 * 10**6, transcendentals=8 * 10**6),
    )(info, mine, other, query)


def attend_back_kernel(
    info, mine_ref, other_ref, q_ref, dnum_ref, delta_ref, dq_ref, dmine_ref, dother_ref, keys_in_order, wide, tall, dq, dkv
):
    sort_blocks(info, (mine_ref, other_ref), keys_in_order)
    for half in range(2):
        zero = jnp.zeros((HEAD_DIM, WIDTH), BF)
        both = jnp.concatenate(
            [
                jnp.concatenate([q_ref[0, half], zero], axis=1),
                jnp.concatenate([zero, dnum_ref[0, half]], axis=1),
            ],
            axis=0,
        )
        wide[half] = both
        tall[half] = both.T
    dq[...] = jnp.zeros_like(dq)
    dkv[...] = jnp.zeros_like(dkv)

    def tile(half, step, limit):
        some = STEP // SUB
        parts = []
        for n in range(SUB):
            at = pl.ds(pl.multiple_of(step * STEP + n * some, some), some)
            keys = keys_in_order[at, :]
            scores = dot_plain(keys, wide[half])
            expo = jnp.exp(scores[:, :WIDTH])
            if limit is not None:
                expo = jnp.where(key_rows_minus_query_lanes(some) <= limit - n * some, expo, 0.0)
            grads = (expo * (scores[:, WIDTH:] - delta_ref[0, half])).astype(BF)
            pair = jnp.concatenate([grads, expo.astype(BF)], axis=1)
            dkv[at, :] += dot_plain(pair, tall[half])
            parts.append(dot_plain(keys.T[:HEAD_DIM], grads))
        dq[half] += sum(parts[1:], parts[0])

    causal_steps(info, tile)
    for half in range(2):
        dq_ref[0, half] = dq[half] * (HEAD_DIM**-0.5)
    unsort_blocks(info, dkv, (dmine_ref, dother_ref))


def attend_back(info, mine, other, query, dnum, delta, first, count):
    rows = mine.shape[0]

    def at(shape, offset):
        return pl.BlockSpec(shape, lambda g, s: (g + offset, 0, 0, 0))

    def kv_at(offset):
        return pl.BlockSpec((rows, 2 * HEAD_DIM), lambda g, s: (0, g + offset))

    head, row = (1, 2, HEAD_DIM, WIDTH), (1, 2, 1, WIDTH)
    return pl.pallas_call(
        attend_back_kernel,
        grid_spec=pltpu.PrefetchScalarGridSpec(
            num_scalar_prefetch=1,
            grid=(count,),
            in_specs=[kv_at(first), kv_at(first), at(head, first), at(head, first), at(row, first)],
            out_specs=[at(head, 0), kv_at(0), kv_at(0)],
            scratch_shapes=[
                pltpu.VMEM((SEQ_LEN, 2 * HEAD_DIM), BF),
                pltpu.VMEM((2, 2 * HEAD_DIM, 2 * WIDTH), BF),
                pltpu.VMEM((2, 2 * WIDTH, 2 * HEAD_DIM), BF),
                pltpu.VMEM((2, HEAD_DIM, WIDTH), F32),
                pltpu.VMEM((SEQ_LEN, 2 * HEAD_DIM), F32),
            ],
        ),
        out_shape=[jax.ShapeDtypeStruct((count, 2, HEAD_DIM, WIDTH), F32)]
        + [jax.ShapeDtypeStruct((rows, count * 2 * HEAD_DIM), BF)] * 2,
        compiler_params=pltpu.CompilerParams(vmem_limit_bytes=VMEM_LIMIT),
        cost_estimate=pl.CostEstimate(
            flops=2 * count * 10**9, bytes_accessed=count * 3 * 10**6, transcendentals=count * 2 * 10**6
        ),
    )(info, mine, other, query, dnum, delta)


PARTS = ((0, 60), (64, 20), (88, 20))
BLOCK = 112


def project_kernel(info, mine_ref, other_ref, normed_ref, cos_ref, sin_ref, w_ref, query_ref, kv_ref, q_rows, k_rows, v_rows, pair):
    step = pl.program_id(0)
    core = info[2]
    for at in range(8):
        lanes = slice(at * 128, at * 128 + 128)
        w_ref[0, core, :, lanes] = mine_ref[at // 4, at % 4, 0, 0]
        w_ref[0, 1 - core, :, lanes] = other_ref[at // 4, at % 4, 0, 0]
    made = dot_last(w_ref[0].reshape(2 * BLOCK, PAD), normed_ref[...])
    for (start, count), rows in zip(PARTS, (q_rows, k_rows, v_rows)):
        pair[0:count] = made[start : start + count]
        pair[count : 2 * count] = made[BLOCK + start : BLOCK + start + count]
        rows[pl.ds(pl.multiple_of(step * 2 * count, 8), 2 * count), :] = pair[0 : 2 * count]

    @pl.when(step == 7)
    def _():
        cosine, sine = cos_ref[...], sin_ref[...]

        def turned(rows, head):
            first = rows[head * 64 : head * 64 + 32]
            second = rows[head * 64 + 32 : head * 64 + 64]
            return jnp.concatenate([first * cosine - second * sine, second * cosine + first * sine], axis=0)

        for g in range(KV_HEADS):
            for r in range(GROUP):
                head = turned(q_rows, GROUP * g + r).astype(BF) * BF(HEAD_DIM**-0.5)
                for half in range(2):
                    query_ref[g, half, :, r * SPAN : (r + 1) * SPAN] = head[:, half * SPAN : (half + 1) * SPAN]
            both = jnp.concatenate([turned(k_rows, g), v_rows[g * 64 : g * 64 + 64]], axis=0)
            kv_ref[:, g * 128 : (g + 1) * 128] = both.T.astype(BF)


def whole_spec(*shape):
    return pl.BlockSpec(shape, lambda j, s: (0,) * len(shape))


SMALL_SPEC = pl.BlockSpec((2, 4, 1, 1, BLOCK, 128), lambda j, s: (0, 0, j // 2, j % 2, 0, 0))
W_SPEC = pl.BlockSpec((1, 2, BLOCK, PAD), lambda j, s: (j, 0, 0, 0))


def project(info, mine, other, normed, cosine, sine):
    rows = normed.shape[0]
    return pl.pallas_call(
        project_kernel,
        grid_spec=pltpu.PrefetchScalarGridSpec(
            num_scalar_prefetch=1,
            grid=(8,),
            in_specs=[SMALL_SPEC, SMALL_SPEC, whole_spec(rows, PAD), whole_spec(32, rows), whole_spec(32, rows)],
            out_specs=[W_SPEC, whole_spec(KV_HEADS, 2, HEAD_DIM, WIDTH), whole_spec(rows, 640)],
            scratch_shapes=[
                pltpu.VMEM((D, rows), F32),
                pltpu.VMEM((320, rows), F32),
                pltpu.VMEM((320, rows), F32),
                pltpu.VMEM((120, rows), F32),
            ],
        ),
        out_shape=[
            jax.ShapeDtypeStruct((8, 2, BLOCK, PAD), BF),
            jax.ShapeDtypeStruct((KV_HEADS, 2, HEAD_DIM, WIDTH), BF),
            jax.ShapeDtypeStruct((rows, 640), BF),
        ],
        compiler_params=pltpu.CompilerParams(vmem_limit_bytes=VMEM_LIMIT),
        cost_estimate=pl.CostEstimate(flops=10**9, bytes_accessed=8 * 10**6, transcendentals=0),
    )(info, mine, other, normed, cosine, sine)


def project_back_kernel(
    info, dq_ref, dq_last_ref, dkv_ref, normed_ref, cos_ref, sin_ref, w_ref, dn_ref, mine_ref, other_ref, q_rows, k_rows, v_rows, pair, blocks, grads
):
    step = pl.program_id(0)
    core = info[2]

    @pl.when(step == 0)
    def _():
        cosine, sine = cos_ref[...], sin_ref[...]

        def turned_back(value):
            first, second = value[:32], value[32:]
            return jnp.concatenate([first * cosine + second * sine, second * cosine - first * sine], axis=0)

        for g in range(KV_HEADS):
            for r in range(GROUP):
                lanes = slice(r * SPAN, (r + 1) * SPAN)
                own, n = (dq_ref, g) if g < KV_HEADS - 1 else (dq_last_ref, 0)
                head = jnp.concatenate([own[n, 0, :, lanes], own[n, 1, :, lanes]], axis=1)
                at = (GROUP * g + r) * 64
                q_rows[at : at + 64] = turned_back(head)
            both = dkv_ref[:, g * 128 : (g + 1) * 128].T
            k_rows[g * 64 : g * 64 + 64] = turned_back(both[:64])
            v_rows[g * 64 : g * 64 + 64] = both[64:]
        blocks[...] = jnp.zeros_like(blocks)
        dn_ref[...] = jnp.zeros_like(dn_ref)

    for (start, count), rows in zip(PARTS, (q_rows, k_rows, v_rows)):
        pair[0 : 2 * count] = rows[pl.ds(pl.multiple_of(step * 2 * count, 8), 2 * count), :]
        blocks[start : start + count] = pair[0:count]
        blocks[BLOCK + start : BLOCK + start + count] = pair[count : 2 * count]
    block = blocks[...].astype(BF)
    dn_ref[...] += dot_first(block, w_ref[0].reshape(2 * BLOCK, PAD))
    grads[...] = dot_plain(block, normed_ref[...]).astype(BF).reshape(2, BLOCK, PAD)
    for at in range(8):
        lanes = slice(at * 128, at * 128 + 128)
        mine_ref[at // 4, at % 4, 0, 0] = grads[core, :, lanes]
        other_ref[at // 4, at % 4, 0, 0] = grads[1 - core, :, lanes]


def project_back(info, dq, dq_last, dkv, normed, cosine, sine, w_all):
    rows = normed.shape[0]
    small = jax.ShapeDtypeStruct((2, 4, 4, 2, BLOCK, 128), BF)
    return pl.pallas_call(
        project_back_kernel,
        grid_spec=pltpu.PrefetchScalarGridSpec(
            num_scalar_prefetch=1,
            grid=(8,),
            in_specs=[
                whole_spec(*dq.shape),
                whole_spec(*dq_last.shape),
                whole_spec(rows, 640),
                whole_spec(rows, PAD),
                whole_spec(32, rows),
                whole_spec(32, rows),
                W_SPEC,
            ],
            out_specs=[whole_spec(rows, PAD), SMALL_SPEC, SMALL_SPEC],
            scratch_shapes=[
                pltpu.VMEM((D, rows), F32),
                pltpu.VMEM((320, rows), F32),
                pltpu.VMEM((320, rows), F32),
                pltpu.VMEM((120, rows), F32),
                pltpu.VMEM((2 * BLOCK, rows), F32),
                pltpu.VMEM((2, BLOCK, PAD), BF),
            ],
        ),
        out_shape=[jax.ShapeDtypeStruct((rows, PAD), F32), small, small],
        compiler_params=pltpu.CompilerParams(vmem_limit_bytes=VMEM_LIMIT),
        cost_estimate=pl.CostEstimate(flops=2 * 10**9, bytes_accessed=10 * 10**6, transcendentals=0),
    )(info, dq, dq_last, dkv, normed, cosine, sine, w_all)


def feed_kernel(
    gate_ref, up_ref, down_ref, n_mine, n_other, dy_mine, dy_other,
    fed_mine, fed_other, dn_mine, dn_other, grad_ref, normed, dy, wg, wu, wd, fed, dn
):
    step = pl.program_id(0)
    rows = n_mine.shape[0]

    @pl.when(step == 0)
    def _():
        normed[:rows] = n_mine[...]
        normed[rows:] = n_other[...]
        dy[:rows] = dy_mine[...]
        dy[rows:] = dy_other[...]
        fed[...] = jnp.zeros_like(fed)
        dn[...] = jnp.zeros_like(dn)

    for group in range(4):
        part = slice(group * 160, group * 160 + 160)
        for at in range(8):
            lanes = slice(at * 128, at * 128 + 128)
            wg[part, lanes] = gate_ref[at % 4, group // 2, group % 2, at // 4]
            wu[part, lanes] = up_ref[at % 4, group // 2, group % 2, at // 4]
            wd[part, lanes] = down_ref[group, at // 2, at % 2, 0]
    gate = dot_last(normed[...], wg[...])
    upward = dot_last(normed[...], wu[...])
    dact = dot_last(dy[...], wd[...])
    sigma = jax.nn.sigmoid(gate)
    silu_gate = gate * sigma
    active = (silu_gate * upward).astype(BF)
    dgate = (dact * upward * sigma * (1.0 + gate * (1.0 - sigma))).astype(BF)
    dup = (dact * silu_gate).astype(BF)
    fed[...] += dot_plain(active, wd[...])
    dn[...] += dot_plain(dgate, wg[...]) + dot_plain(dup, wu[...])
    g_gate = dot_first(dgate, normed[...]).astype(BF)
    g_up = dot_first(dup, normed[...]).astype(BF)
    g_down = dot_first(active, dy[...]).astype(BF)
    for group in range(4):
        part = slice(group * 160, group * 160 + 160)
        for at in range(8):
            lanes = slice(at * 128, at * 128 + 128)
            grad_ref[at % 4, 2 * step + group // 2, group % 2, at // 4, 0:160] = g_gate[part, lanes]
            grad_ref[at % 4, 2 * step + group // 2, group % 2, at // 4, 160:320] = g_up[part, lanes]
            grad_ref[group, at // 2, at % 2, step, 320:480] = g_down[part, lanes]

    @pl.when(step == 1)
    def _():
        fed_mine[...] = fed[:rows]
        fed_other[...] = fed[rows:].astype(BF)
        dn_mine[...] = dn[:rows]
        dn_other[...] = dn[rows:].astype(BF)


def feed(big, n_mine, n_other, dy_mine, dy_other):
    rows = n_mine.shape[0]
    by_plane = (4, 2, 2, 2, 160, 128)

    def flat(*shape):
        return pl.BlockSpec(shape, lambda k: (0,) * len(shape))

    return pl.pallas_call(
        feed_kernel,
        grid=(2,),
        in_specs=[
            pl.BlockSpec(by_plane, lambda k: (0, k, 0, 0, 0, 0)),
            pl.BlockSpec(by_plane, lambda k: (0, k, 0, 0, 1, 0)),
            pl.BlockSpec((4, 4, 2, 1, 160, 128), lambda k: (0, 0, 0, k, 2, 0)),
        ]
        + [flat(rows, PAD)] * 4,
        out_specs=[flat(rows, PAD)] * 4 + [flat(4, 4, 2, 2, 480, 128)],
        out_shape=[
            jax.ShapeDtypeStruct((rows, PAD), F32),
            jax.ShapeDtypeStruct((rows, PAD), BF),
            jax.ShapeDtypeStruct((rows, PAD), F32),
            jax.ShapeDtypeStruct((rows, PAD), BF),
            jax.ShapeDtypeStruct((4, 4, 2, 2, 480, 128), BF),
        ],
        scratch_shapes=[pltpu.VMEM((2 * rows, PAD), BF)] * 2
        + [pltpu.VMEM((FEED, PAD), BF)] * 3
        + [pltpu.VMEM((2 * rows, PAD), F32)] * 2,
        compiler_params=pltpu.CompilerParams(vmem_limit_bytes=VMEM_LIMIT),
        cost_estimate=pl.CostEstimate(flops=12 * 10**9, bytes_accessed=22 * 10**6, transcendentals=10**6),
    )(big, big, big, n_mine, n_other, dy_mine, dy_other)


def project_out_kernel(info, o_ref, mine_ref, other_ref, x_ref, gain_ref, hidden_ref, normed_ref, w_ref, ob_ref, rows):
    core = info[2]
    for s in range(8):
        for j in range(8):
            lanes = slice(j * 128, j * 128 + 128)
            w_ref[s, core, :, lanes] = mine_ref[s // 4, s % 4, j // 2, j % 2]
            w_ref[s, 1 - core, :, lanes] = other_ref[s // 4, s % 4, j // 2, j % 2]
    for head in range(HEADS):
        g, r = head // GROUP, head % GROUP
        for half in range(2):
            piece = o_ref[g, half, :, r * SPAN : (r + 1) * SPAN]
            rows[head * 64 : head * 64 + 64, half * SPAN : (half + 1) * SPAN] = piece
    ob_ref[...] = jnp.zeros_like(ob_ref)
    for n in range(16):
        ob_ref[n * 64 : n * 64 + 60] = rows[n * 60 : n * 60 + 60].astype(BF)
    hidden = x_ref[...] + dot_first(ob_ref[...], w_ref[...].reshape(PAD, PAD))
    hidden_ref[...] = hidden
    inverse = lax.rsqrt(jnp.sum(hidden * hidden, axis=-1, keepdims=True) / D + EPS)
    normed_ref[...] = (hidden * inverse * gain_ref[...]).astype(BF)


def one_call(kernel, info, args, outs, scratch, flops):
    return pl.pallas_call(
        kernel,
        in_specs=[pl.BlockSpec(memory_space=pltpu.SMEM)] + [pl.BlockSpec(memory_space=pltpu.VMEM)] * len(args),
        out_specs=[pl.BlockSpec(memory_space=pltpu.VMEM)] * len(outs),
        out_shape=[jax.ShapeDtypeStruct(shape, kind) for shape, kind in outs],
        scratch_shapes=scratch,
        compiler_params=pltpu.CompilerParams(vmem_limit_bytes=VMEM_LIMIT),
        cost_estimate=pl.CostEstimate(flops=flops, bytes_accessed=10 * 10**6, transcendentals=0),
    )(info, *args)


def project_out(info, attended, mine, other, layer_input, gain):
    rows = layer_input.shape[0]
    return one_call(
        project_out_kernel,
        info,
        (attended, mine, other, layer_input, gain),
        [((rows, PAD), F32), ((rows, PAD), BF), ((8, 2, 64, PAD), BF), ((PAD, rows), BF)],
        [pltpu.VMEM((D, rows), F32)],
        10**9,
    )


def between_kernel(
    info, dn_ref, dn_other_ref, hidden_ref, gain_ref, dy_ref, w_ref, ob_ref, o_ref, total_ref,
    dh_ref, dnum_ref, delta_ref, mine_ref, other_ref, gain_grad_ref, rows, grads
):
    core = info[2]
    hidden, gain = hidden_ref[...], gain_ref[...]
    inverse = lax.rsqrt(jnp.sum(hidden * hidden, axis=-1, keepdims=True) / D + EPS)
    unit = hidden * inverse
    dn = dn_ref[...] + dn_other_ref[...].astype(F32)
    back, gain_grad = norm_back(dn, unit, inverse, gain)
    gain_grad_ref[...] = gain_grad[None]
    dh = dy_ref[...].astype(F32) + back
    dh_ref[...] = dh
    dh_low = dh.astype(BF)
    dob = dot_last(w_ref[...].reshape(PAD, PAD), dh_low)
    for n in range(16):
        rows[n * 60 : n * 60 + 60] = dob[n * 64 : n * 64 + 60].astype(BF).astype(F32)
    for head in range(HEADS):
        g, r = head // GROUP, head % GROUP
        for half in range(2):
            lanes = slice(r * SPAN, (r + 1) * SPAN)
            piece = rows[head * 64 : head * 64 + 64, half * SPAN : (half + 1) * SPAN]
            total = total_ref[g, half, :, lanes]
            dnum_ref[g, half, :, lanes] = (piece / total).astype(BF)
            summed = jnp.sum(piece * o_ref[g, half, :, lanes], axis=0, keepdims=True)
            delta_ref[g, half, :, lanes] = summed / total
    grads[...] = dot_plain(ob_ref[...], dh_low).astype(BF).reshape(8, 2, 64, PAD)
    for s in range(8):
        for j in range(8):
            lanes = slice(j * 128, j * 128 + 128)
            mine_ref[s // 4, s % 4, j // 2, j % 2] = grads[s, core, :, lanes]
            other_ref[s // 4, s % 4, j // 2, j % 2] = grads[s, 1 - core, :, lanes]


def between(info, dn, dn_other, hidden, gain, dy, w_out, attended_low, attended, total):
    rows = hidden.shape[0]
    return one_call(
        between_kernel,
        info,
        (dn, dn_other, hidden, gain, dy, w_out, attended_low, attended, total),
        [
            ((rows, PAD), F32),
            ((KV_HEADS, 2, HEAD_DIM, WIDTH), BF),
            ((KV_HEADS, 2, 1, WIDTH), F32),
            ((2, 4, 4, 2, 64, 128), BF),
            ((2, 4, 4, 2, 64, 128), BF),
            ((1, PAD), F32),
        ],
        [pltpu.VMEM((D, rows), F32), pltpu.VMEM((8, 2, 64, PAD), BF)],
        2 * 10**9,
    )


def pad_rows(value, count):
    return jnp.pad(value, ((0, count - value.shape[0]), (0, 0)))


def norm_forward(value, gain):
    inverse = lax.rsqrt(jnp.sum(value * value, axis=-1, keepdims=True) / D + EPS)
    unit = value * inverse
    return unit, inverse, (unit * gain).astype(BF)


def norm_back(grad, unit, inverse, gain):
    scaled = grad * gain
    inner = jnp.sum(scaled * unit, axis=-1, keepdims=True) / D
    return inverse * (scaled - unit * inner), jnp.sum(grad * unit, axis=0)


def body(
    tokens,
    w_query,
    w_key,
    w_value,
    w_out,
    w_gate,
    w_up,
    w_down,
    attention_norm_gain,
    feedforward_norm_gain,
    span_order,
    positions,
    out_grad,
):
    rows = tokens.shape[0]
    core = lax.axis_index("c")
    me = lax.axis_index(("x", "zh", "c"))

    small = jnp.concatenate([pad_rows(w_query.T, 64), pad_rows(w_key.T, 24), pad_rows(w_value.T, 24)], axis=0)
    small = to_chips(jnp.broadcast_to(pad_lanes(small), (64, BLOCK, 128)))
    mixed = jnp.concatenate([w_down.reshape(2, 160, 60), w_out.reshape(2, 60, 60)], axis=1)
    mixed = lax.all_to_all(mixed, "c", 0, 0, tiled=True)
    mixed = jnp.concatenate([mixed[0], mixed[1]], axis=1)
    big = pad_lanes(jnp.concatenate([w_gate.T, w_up.T, mixed[:160]], axis=0))
    big = lax.all_gather(big, ("x",) + LINE, axis=0, tiled=True)
    w_out_block = pad_rows(pad_lanes(mixed[160:]), 64)

    order = span_order[0]
    own_pair = lax.dynamic_slice_in_dim(order, 2 * me, 2)
    own_low_half = (own_pair[0] > own_pair[1]).astype(jnp.int32)
    spans = order.reshape(8, 2, 2)
    info = jnp.concatenate(
        [
            jnp.stack([own_low_half, jnp.minimum(own_pair[0], own_pair[1]), core.astype(jnp.int32)]),
            jnp.zeros((5,), jnp.int32),
            lax.dynamic_index_in_dim(spans, core, 1, keepdims=False).reshape(16),
            lax.dynamic_index_in_dim(spans, 1 - core, 1, keepdims=False).reshape(16),
        ]
    ).astype(jnp.int32)
    place = jnp.concatenate(
        [
            lax.dynamic_slice_in_dim(positions[0], own_pair[0] * SPAN, SPAN, 0),
            lax.dynamic_slice_in_dim(positions[0], own_pair[1] * SPAN, SPAN, 0),
        ]
    )
    half_dim = HEAD_DIM // 2
    freq = jnp.power(ROPE_BASE, -jnp.arange(half_dim, dtype=F32) / half_dim)
    angle = freq[:, None] * place.astype(F32)[None, :]
    cosine, sine = jnp.cos(angle), jnp.sin(angle)

    gain_one = pad_width(attention_norm_gain[None])
    gain_two = pad_width(feedforward_norm_gain[None])
    layer_input = pad_width(tokens).astype(F32)
    dy = pad_width(out_grad)
    dy_other = other_core(dy)

    unit_one, inverse_one, normed_one = norm_forward(layer_input, gain_one)
    small, normed_one, info, cosine, sine = lax.optimization_barrier((small, normed_one, info, cosine, sine))
    small = small.reshape(2, 4, 4, 2, BLOCK, 128)
    small_other = other_core(small)
    big, _ = lax.optimization_barrier((big, small_other))
    big = lax.all_gather(big, "y", axis=0, tiled=True).reshape(4, 4, 2, 2, 480, 128)
    w_all, query, kv_local = project(info, small, small_other, normed_one, cosine, sine)

    kv = lax.all_to_all(jnp.broadcast_to(kv_local, (8, rows, 640)), SEQ, 0, 0, tiled=True)
    kv = kv.reshape(8 * rows, 640)
    kv_other = other_core(kv)

    w_out_block, kv, kv_other = lax.optimization_barrier((w_out_block, kv, kv_other))
    w_out_mine = to_chips(jnp.broadcast_to(w_out_block, (64, 64, 128)))
    attended, total = attend(info, kv, kv_other, query)
    big, w_out_mine, attended = lax.optimization_barrier((big, w_out_mine, attended))
    w_out_mine = w_out_mine.reshape(2, 4, 4, 2, 64, 128)
    hidden, normed_two, w_out_full, attended_low = project_out(
        info, attended, w_out_mine, other_core(w_out_mine), layer_input, gain_two
    )
    fed, fed_other, dn_two, dn_other, g_big = feed(big, normed_two, other_core(normed_two), dy, dy_other)
    dh, dnum, delta, g_out, g_out_other, gain_two_grad = between(
        info, dn_two, other_core(dn_other), hidden, gain_two, dy, w_out_full, attended_low, attended, total
    )
    result = cut_width((hidden + (fed + other_core(fed_other).astype(F32))).astype(BF))

    g_big = lax.psum_scatter(g_big.reshape(64 * 480, 128), PLANE, scatter_dimension=0, tiled=True)
    g_big = sum_line(g_big.reshape(4, 480, 128))

    g_out = (g_out.astype(F32) + other_core(g_out_other).astype(F32)).astype(BF).reshape(64, 64, 128)
    gain_two_grad = high_and_low(gain_two_grad + other_core(gain_two_grad))
    g_out = jnp.concatenate([g_out, jnp.broadcast_to(gain_two_grad, (64, 16, 128))], axis=1)

    many = KV_HEADS - 1
    g_out, dnum = lax.optimization_barrier((g_out, dnum))
    g_out = to_chips(g_out)
    dq, dkv, dkv_other = attend_back(info, kv, kv_other, query, dnum, delta, 0, many)
    g_out, dnum = lax.optimization_barrier((g_out, dnum))
    dq_last, dkv_last, dkv_last_other = attend_back(info, kv, kv_other, query, dnum, delta, many, 1)
    dkv = dkv.astype(F32) + other_core(dkv_other).astype(F32)
    dkv_last = dkv_last.astype(F32) + other_core(dkv_last_other).astype(F32)
    dkv = jnp.concatenate([dkv, dkv_last], axis=1).astype(BF)
    dkv = lax.all_to_all(dkv.reshape(8, rows, 640), SEQ, 0, 0, tiled=True)
    dkv = jnp.sum(dkv.astype(F32), axis=0)

    dn_one, g_small, g_other = project_back(info, dq, dq_last, dkv, normed_one, cosine, sine, w_all)
    back_one, gain_one_grad = norm_back(dn_one, unit_one, inverse_one, gain_one)
    input_grad = cut_width((dh + back_one).astype(BF))

    g_small = (g_small.astype(F32) + other_core(g_other).astype(F32)).astype(BF).reshape(64, BLOCK, 128)
    gain_one_grad = high_and_low(gain_one_grad + other_core(gain_one_grad))
    last = jnp.concatenate([g_small, jnp.broadcast_to(gain_one_grad, (64, 16, 128))], axis=1)
    last, g_big = lax.optimization_barrier((last, g_big))
    last = jnp.sum(to_chips(last).astype(F32), axis=0)
    g_out = jnp.sum(g_out.astype(F32), axis=0)
    gain_one_grad = cut_width((last[112:120] + last[120:128]).reshape(1, PAD))[0]
    gain_two_grad = cut_width((g_out[64:72] + g_out[72:80]).reshape(1, PAD))[0]

    mixed = jnp.concatenate([g_big[320:], g_out[:60]], axis=0)[:, :120]
    halves = mixed.reshape(220, 2, 60)
    keep = lax.dynamic_index_in_dim(halves, core, 1, keepdims=False)
    came = other_core(lax.dynamic_index_in_dim(halves, 1 - core, 1, keepdims=False))
    first = core == 0
    mixed = jnp.stack([jnp.where(first, keep, came), jnp.where(first, came, keep)])
    return (
        result,
        input_grad,
        last[:60, :120].T,
        last[64:84, :120].T,
        last[88:108, :120].T,
        mixed[:, 160:].reshape(120, 60),
        g_big[:160, :120].T,
        g_big[160:320, :120].T,
        mixed[:, :160].reshape(320, 60),
        gain_one_grad,
        gain_two_grad,
    )


def solution(mesh):
    fine = Mesh(mesh.devices.reshape(2, 4, 4, 2, 2), ("zl", "y", "x", "zh", "c"))
    shard, ctx = ("zl", "y"), ("x", "zh", "c")
    both = shard + ctx
    return jax.shard_map(
        body,
        mesh=fine,
        in_specs=(P(both, None),)
        + (P(shard, ctx),) * 7
        + (P(), P(), P(shard, None), P(shard, None), P(both, None)),
        out_specs=(P(both, None), P(both, None)) + (P(shard, ctx),) * 7 + (P(), P()),
        check_vma=False,
    )
```

```python
import jax
import jax.numpy as jnp
from jax import lax
from jax.experimental import pallas as pl
from jax.experimental.pallas import tpu as pltpu
from jax.sharding import Mesh
from jax.sharding import PartitionSpec as P

D = 960
HEADS = 15
KV_HEADS = 5
GROUP = 3
HEAD_DIM = 64
SPAN = 128
PAD = 1024

EPS = 1e-05
ROPE_BASE = 100000.0

BF = jnp.bfloat16
F32 = jnp.float32

PLANE = ("y", "x")
LINE = ("zh", "zl")
CHIPS = ("zl", "y", "x", "zh")
SEQ = ("x", "zh")
SWAP = [(0, 1), (1, 0)]


def pad_width(value):
    rows = value.shape[0]
    blocks = value.reshape(rows, 8, 120)
    return jnp.pad(blocks, ((0, 0), (0, 0), (0, 8))).reshape(rows, PAD)


def cut_width(value):
    rows = value.shape[0]
    return value.reshape(rows, 8, 128)[:, :, :120].reshape(rows, D)


def pad_lanes(value):
    return jnp.pad(value, ((0, 0), (0, 128 - value.shape[1])))


def other_core(value):
    return lax.ppermute(value, "c", SWAP)


def sum_line(blocks):
    ring = ("zl", "zh")
    here = lax.axis_index(ring)

    def block_of(chip):
        return lax.dynamic_index_in_dim(blocks, 2 * (chip % 2) + chip // 2, 0, keepdims=False)

    total = block_of(here).astype(F32)
    for turn in range(1, 4):
        came = lax.ppermute(block_of(here ^ turn), ring, [(n, n ^ turn) for n in range(4)])
        total = total + came.astype(F32)
    return total


def to_chips(blocks):
    return lax.all_to_all(blocks, CHIPS, 0, 0, tiled=True)


def high_and_low(value):
    high = value.astype(BF)
    low = (value - high.astype(F32)).astype(BF)
    return jnp.concatenate([high.reshape(16, 128), low.reshape(16, 128)], axis=0)


def dot_last(left, right):
    return lax.dot_general(left, right, (((1,), (1,)), ((), ())), preferred_element_type=F32)


def dot_first(left, right):
    return lax.dot_general(left, right, (((0,), (0,)), ((), ())), preferred_element_type=F32)


def dot_plain(left, right):
    return jnp.dot(left, right, preferred_element_type=F32)


VMEM_LIMIT = 56 * 1024 * 1024
WIDTH = GROUP * SPAN
TILES = 8
SUB = 2
STEP = TILES * SPAN
SEQ_LEN = 4096
FEED = 640


def sort_blocks(info, sources, target):
    def one(slot, carry):
        at = pl.ds(pl.multiple_of(slot * SPAN, SPAN), SPAN)
        for n, source in enumerate(sources):
            to = pl.ds(pl.multiple_of(info[8 + 16 * n + slot] * SPAN, SPAN), SPAN)
            target[to, :] = source[at, :]
        return carry

    lax.fori_loop(0, 16, one, 0)


def unsort_blocks(info, source, targets):
    def one(slot, carry):
        at = pl.ds(pl.multiple_of(slot * SPAN, SPAN), SPAN)
        for n, target in enumerate(targets):
            to = pl.ds(pl.multiple_of(info[8 + 16 * n + slot] * SPAN, SPAN), SPAN)
            target[at, :] = source[to, :].astype(target.dtype)
        return carry

    lax.fori_loop(0, 16, one, 0)


def causal_steps(info, tile):
    low_half, low = info[0], info[1]
    high = 31 - low
    low_last = lax.div(low, TILES)
    high_last = lax.div(high, TILES)

    def whole(step, carry):
        is_low = step < low_last
        tile(
            jnp.where(is_low, low_half, 1 - low_half),
            jnp.where(is_low, step, step - low_last),
            None,
        )
        return carry

    lax.fori_loop(0, 3, whole, 0, unroll=3)
    tile(low_half, low_last, (low - low_last * TILES) * SPAN)
    tile(1 - low_half, high_last, (high - high_last * TILES) * SPAN)


def key_rows_minus_query_lanes(rows):
    row = lax.broadcasted_iota(jnp.int32, (rows, WIDTH), 0)
    lane = lax.broadcasted_iota(jnp.int32, (rows, WIDTH), 1)
    return row - lax.rem(lane, SPAN)


def attend_kernel(info, mine_ref, other_ref, q_ref, out_ref, total_ref, keys_in_order, query, numer, total):
    sort_blocks(info, (mine_ref, other_ref), keys_in_order)
    query[...] = jnp.zeros_like(query)
    for half in range(2):
        query[half, :HEAD_DIM, :] = q_ref[0, half]
    numer[...] = jnp.zeros_like(numer)
    total[...] = jnp.zeros_like(total)

    def tile(half, step, limit):
        some = STEP // SUB
        parts, sums = [], []
        for n in range(SUB):
            keys = keys_in_order[pl.ds(pl.multiple_of(step * STEP + n * some, some), some), :]
            expo = jnp.exp(dot_plain(keys, query[half]))
            if limit is not None:
                expo = jnp.where(key_rows_minus_query_lanes(some) <= limit - n * some, expo, 0.0)
            parts.append(dot_plain(keys.T[HEAD_DIM:], expo.astype(BF)))
            sums.append(jnp.sum(expo.reshape(some // 8, 8, WIDTH), axis=0))
        numer[half] += sum(parts[1:], parts[0])
        total[half] += sum(sums[1:], sums[0])

    causal_steps(info, tile)
    for half in range(2):
        summed = jnp.sum(total[half], axis=0, keepdims=True)
        total_ref[0, half] = summed
        out_ref[0, half] = numer[half] / summed


HEAD_SPEC = pl.BlockSpec((1, 2, HEAD_DIM, WIDTH), lambda g, s: (g, 0, 0, 0))
ROW_SPEC = pl.BlockSpec((1, 2, 1, WIDTH), lambda g, s: (g, 0, 0, 0))
KV_SPEC = pl.BlockSpec((SEQ_LEN // 2, 2 * HEAD_DIM), lambda g, s: (0, g))
HEAD_F32 = jax.ShapeDtypeStruct((KV_HEADS, 2, HEAD_DIM, WIDTH), F32)


def attend(info, mine, other, query):
    return pl.pallas_call(
        attend_kernel,
        grid_spec=pltpu.PrefetchScalarGridSpec(
            num_scalar_prefetch=1,
            grid=(KV_HEADS,),
            in_specs=[KV_SPEC, KV_SPEC, HEAD_SPEC],
            out_specs=[HEAD_SPEC, ROW_SPEC],
            scratch_shapes=[
                pltpu.VMEM((SEQ_LEN, 2 * HEAD_DIM), BF),
                pltpu.VMEM((2, 2 * HEAD_DIM, WIDTH), BF),
                pltpu.VMEM((2, HEAD_DIM, WIDTH), F32),
                pltpu.VMEM((2, 8, WIDTH), F32),
            ],
        ),
        out_shape=[HEAD_F32, jax.ShapeDtypeStruct((KV_HEADS, 2, 1, WIDTH), F32)],
        compiler_params=pltpu.CompilerParams(vmem_limit_bytes=VMEM_LIMIT),
        cost_estimate=pl.CostEstimate(flops=4 * 10**9, bytes_accessed=8 * 10**6, transcendentals=8 * 10**6),
    )(info, mine, other, query)


def attend_back_kernel(
    info, mine_ref, other_ref, q_ref, dnum_ref, delta_ref, dq_ref, dmine_ref, dother_ref, keys_in_order, wide, tall, dq, dkv
):
    sort_blocks(info, (mine_ref, other_ref), keys_in_order)
    for half in range(2):
        zero = jnp.zeros((HEAD_DIM, WIDTH), BF)
        both = jnp.concatenate(
            [
                jnp.concatenate([q_ref[0, half], zero], axis=1),
                jnp.concatenate([zero, dnum_ref[0, half]], axis=1),
            ],
            axis=0,
        )
        wide[half] = both
        tall[half] = both.T
    dq[...] = jnp.zeros_like(dq)
    dkv[...] = jnp.zeros_like(dkv)

    def tile(half, step, limit):
        some = STEP // SUB
        parts = []
        for n in range(SUB):
            at = pl.ds(pl.multiple_of(step * STEP + n * some, some), some)
            keys = keys_in_order[at, :]
            scores = dot_plain(keys, wide[half])
            expo = jnp.exp(scores[:, :WIDTH])
            if limit is not None:
                expo = jnp.where(key_rows_minus_query_lanes(some) <= limit - n * some, expo, 0.0)
            grads = (expo * (scores[:, WIDTH:] - delta_ref[0, half])).astype(BF)
            pair = jnp.concatenate([grads, expo.astype(BF)], axis=1)
            dkv[at, :] += dot_plain(pair, tall[half])
            parts.append(dot_plain(keys.T[:HEAD_DIM], grads))
        dq[half] += sum(parts[1:], parts[0])

    causal_steps(info, tile)
    for half in range(2):
        dq_ref[0, half] = dq[half] * (HEAD_DIM**-0.5)
    unsort_blocks(info, dkv, (dmine_ref, dother_ref))


def attend_back(info, mine, other, query, dnum, delta, first, count):
    rows = mine.shape[0]

    def at(shape, offset):
        return pl.BlockSpec(shape, lambda g, s: (g + offset, 0, 0, 0))

    def kv_at(offset):
        return pl.BlockSpec((rows, 2 * HEAD_DIM), lambda g, s: (0, g + offset))

    head, row = (1, 2, HEAD_DIM, WIDTH), (1, 2, 1, WIDTH)
    return pl.pallas_call(
        attend_back_kernel,
        grid_spec=pltpu.PrefetchScalarGridSpec(
            num_scalar_prefetch=1,
            grid=(count,),
            in_specs=[kv_at(first), kv_at(first), at(head, first), at(head, first), at(row, first)],
            out_specs=[at(head, 0), kv_at(0), kv_at(0)],
            scratch_shapes=[
                pltpu.VMEM((SEQ_LEN, 2 * HEAD_DIM), BF),
                pltpu.VMEM((2, 2 * HEAD_DIM, 2 * WIDTH), BF),
                pltpu.VMEM((2, 2 * WIDTH, 2 * HEAD_DIM), BF),
                pltpu.VMEM((2, HEAD_DIM, WIDTH), F32),
                pltpu.VMEM((SEQ_LEN, 2 * HEAD_DIM), F32),
            ],
        ),
        out_shape=[jax.ShapeDtypeStruct((count, 2, HEAD_DIM, WIDTH), F32)]
        + [jax.ShapeDtypeStruct((rows, count * 2 * HEAD_DIM), BF)] * 2,
        compiler_params=pltpu.CompilerParams(vmem_limit_bytes=VMEM_LIMIT),
        cost_estimate=pl.CostEstimate(
            flops=2 * count * 10**9, bytes_accessed=count * 3 * 10**6, transcendentals=count * 2 * 10**6
        ),
    )(info, mine, other, query, dnum, delta)


PARTS = ((0, 60), (64, 20), (88, 20))
BLOCK = 112


def project_kernel(info, mine_ref, other_ref, normed_ref, cos_ref, sin_ref, w_ref, query_ref, kv_ref, q_rows, k_rows, v_rows, pair):
    step = pl.program_id(0)
    core = info[2]
    for at in range(8):
        lanes = slice(at * 128, at * 128 + 128)
        w_ref[0, core, :, lanes] = mine_ref[at // 4, at % 4, 0, 0]
        w_ref[0, 1 - core, :, lanes] = other_ref[at // 4, at % 4, 0, 0]
    made = dot_last(w_ref[0].reshape(2 * BLOCK, PAD), normed_ref[...])
    for (start, count), rows in zip(PARTS, (q_rows, k_rows, v_rows)):
        pair[0:count] = made[start : start + count]
        pair[count : 2 * count] = made[BLOCK + start : BLOCK + start + count]
        rows[pl.ds(pl.multiple_of(step * 2 * count, 8), 2 * count), :] = pair[0 : 2 * count]

    @pl.when(step == 7)
    def _():
        cosine, sine = cos_ref[...], sin_ref[...]

        def turned(rows, head):
            first = rows[head * 64 : head * 64 + 32]
            second = rows[head * 64 + 32 : head * 64 + 64]
            return jnp.concatenate([first * cosine - second * sine, second * cosine + first * sine], axis=0)

        for g in range(KV_HEADS):
            for r in range(GROUP):
                head = turned(q_rows, GROUP * g + r).astype(BF) * BF(HEAD_DIM**-0.5)
                for half in range(2):
                    query_ref[g, half, :, r * SPAN : (r + 1) * SPAN] = head[:, half * SPAN : (half + 1) * SPAN]
            both = jnp.concatenate([turned(k_rows, g), v_rows[g * 64 : g * 64 + 64]], axis=0)
            kv_ref[:, g * 128 : (g + 1) * 128] = both.T.astype(BF)


def whole_spec(*shape):
    return pl.BlockSpec(shape, lambda j, s: (0,) * len(shape))


SMALL_SPEC = pl.BlockSpec((2, 4, 1, 1, BLOCK, 128), lambda j, s: (0, 0, j // 2, j % 2, 0, 0))
W_SPEC = pl.BlockSpec((1, 2, BLOCK, PAD), lambda j, s: (j, 0, 0, 0))


def project(info, mine, other, normed, cosine, sine):
    rows = normed.shape[0]
    return pl.pallas_call(
        project_kernel,
        grid_spec=pltpu.PrefetchScalarGridSpec(
            num_scalar_prefetch=1,
            grid=(8,),
            in_specs=[SMALL_SPEC, SMALL_SPEC, whole_spec(rows, PAD), whole_spec(32, rows), whole_spec(32, rows)],
            out_specs=[W_SPEC, whole_spec(KV_HEADS, 2, HEAD_DIM, WIDTH), whole_spec(rows, 640)],
            scratch_shapes=[
                pltpu.VMEM((D, rows), F32),
                pltpu.VMEM((320, rows), F32),
                pltpu.VMEM((320, rows), F32),
                pltpu.VMEM((120, rows), F32),
            ],
        ),
        out_shape=[
            jax.ShapeDtypeStruct((8, 2, BLOCK, PAD), BF),
            jax.ShapeDtypeStruct((KV_HEADS, 2, HEAD_DIM, WIDTH), BF),
            jax.ShapeDtypeStruct((rows, 640), BF),
        ],
        compiler_params=pltpu.CompilerParams(vmem_limit_bytes=VMEM_LIMIT),
        cost_estimate=pl.CostEstimate(flops=10**9, bytes_accessed=8 * 10**6, transcendentals=0),
    )(info, mine, other, normed, cosine, sine)


def project_back_kernel(
    info, dq_ref, dkv_ref, normed_ref, cos_ref, sin_ref, w_ref, dn_ref, mine_ref, other_ref, q_rows, k_rows, v_rows, pair, blocks, grads
):
    step = pl.program_id(0)
    core = info[2]

    @pl.when(step == 0)
    def _():
        cosine, sine = cos_ref[...], sin_ref[...]

        def turned_back(value):
            first, second = value[:32], value[32:]
            return jnp.concatenate([first * cosine + second * sine, second * cosine - first * sine], axis=0)

        for g in range(KV_HEADS):
            for r in range(GROUP):
                lanes = slice(r * SPAN, (r + 1) * SPAN)
                head = jnp.concatenate([dq_ref[g, 0, :, lanes], dq_ref[g, 1, :, lanes]], axis=1)
                at = (GROUP * g + r) * 64
                q_rows[at : at + 64] = turned_back(head)
            both = dkv_ref[:, g * 128 : (g + 1) * 128].T
            k_rows[g * 64 : g * 64 + 64] = turned_back(both[:64])
            v_rows[g * 64 : g * 64 + 64] = both[64:]
        blocks[...] = jnp.zeros_like(blocks)
        dn_ref[...] = jnp.zeros_like(dn_ref)

    for (start, count), rows in zip(PARTS, (q_rows, k_rows, v_rows)):
        pair[0 : 2 * count] = rows[pl.ds(pl.multiple_of(step * 2 * count, 8), 2 * count), :]
        blocks[start : start + count] = pair[0:count]
        blocks[BLOCK + start : BLOCK + start + count] = pair[count : 2 * count]
    block = blocks[...].astype(BF)
    dn_ref[...] += dot_first(block, w_ref[0].reshape(2 * BLOCK, PAD))
    grads[...] = dot_plain(block, normed_ref[...]).astype(BF).reshape(2, BLOCK, PAD)
    for at in range(8):
        lanes = slice(at * 128, at * 128 + 128)
        mine_ref[at // 4, at % 4, 0, 0] = grads[core, :, lanes]
        other_ref[at // 4, at % 4, 0, 0] = grads[1 - core, :, lanes]


def project_back(info, dq, dkv, normed, cosine, sine, w_all):
    rows = normed.shape[0]
    small = jax.ShapeDtypeStruct((2, 4, 4, 2, BLOCK, 128), BF)
    return pl.pallas_call(
        project_back_kernel,
        grid_spec=pltpu.PrefetchScalarGridSpec(
            num_scalar_prefetch=1,
            grid=(8,),
            in_specs=[
                whole_spec(*dq.shape),
                whole_spec(rows, 640),
                whole_spec(rows, PAD),
                whole_spec(32, rows),
                whole_spec(32, rows),
                W_SPEC,
            ],
            out_specs=[whole_spec(rows, PAD), SMALL_SPEC, SMALL_SPEC],
            scratch_shapes=[
                pltpu.VMEM((D, rows), F32),
                pltpu.VMEM((320, rows), F32),
                pltpu.VMEM((320, rows), F32),
                pltpu.VMEM((120, rows), F32),
                pltpu.VMEM((2 * BLOCK, rows), F32),
                pltpu.VMEM((2, BLOCK, PAD), BF),
            ],
        ),
        out_shape=[jax.ShapeDtypeStruct((rows, PAD), F32), small, small],
        compiler_params=pltpu.CompilerParams(vmem_limit_bytes=VMEM_LIMIT),
        cost_estimate=pl.CostEstimate(flops=2 * 10**9, bytes_accessed=10 * 10**6, transcendentals=0),
    )(info, dq, dkv, normed, cosine, sine, w_all)


def feed_kernel(
    gate_ref, up_ref, down_ref, n_mine, n_other, dy_mine, dy_other,
    fed_mine, fed_other, dn_mine, dn_other, grad_ref, normed, dy, wg, wu, wd, fed, dn
):
    step = pl.program_id(0)
    rows = n_mine.shape[0]

    @pl.when(step == 0)
    def _():
        normed[:rows] = n_mine[...]
        normed[rows:] = n_other[...]
        dy[:rows] = dy_mine[...]
        dy[rows:] = dy_other[...]
        fed[...] = jnp.zeros_like(fed)
        dn[...] = jnp.zeros_like(dn)

    for group in range(4):
        part = slice(group * 160, group * 160 + 160)
        for at in range(8):
            lanes = slice(at * 128, at * 128 + 128)
            wg[part, lanes] = gate_ref[at % 4, group // 2, group % 2, at // 4]
            wu[part, lanes] = up_ref[at % 4, group // 2, group % 2, at // 4]
            wd[part, lanes] = down_ref[group, at // 2, at % 2, 0]
    gate = dot_last(normed[...], wg[...])
    upward = dot_last(normed[...], wu[...])
    dact = dot_last(dy[...], wd[...])
    sigma = jax.nn.sigmoid(gate)
    silu_gate = gate * sigma
    active = (silu_gate * upward).astype(BF)
    dgate = (dact * upward * sigma * (1.0 + gate * (1.0 - sigma))).astype(BF)
    dup = (dact * silu_gate).astype(BF)
    fed[...] += dot_plain(active, wd[...])
    dn[...] += dot_plain(dgate, wg[...]) + dot_plain(dup, wu[...])
    g_gate = dot_first(dgate, normed[...]).astype(BF)
    g_up = dot_first(dup, normed[...]).astype(BF)
    g_down = dot_first(active, dy[...]).astype(BF)
    for group in range(4):
        part = slice(group * 160, group * 160 + 160)
        for at in range(8):
            lanes = slice(at * 128, at * 128 + 128)
            grad_ref[at % 4, 2 * step + group // 2, group % 2, at // 4, 0:160] = g_gate[part, lanes]
            grad_ref[at % 4, 2 * step + group // 2, group % 2, at // 4, 160:320] = g_up[part, lanes]
            grad_ref[group, at // 2, at % 2, step, 320:480] = g_down[part, lanes]

    @pl.when(step == 1)
    def _():
        fed_mine[...] = fed[:rows]
        fed_other[...] = fed[rows:].astype(BF)
        dn_mine[...] = dn[:rows]
        dn_other[...] = dn[rows:].astype(BF)


def feed(big, n_mine, n_other, dy_mine, dy_other):
    rows = n_mine.shape[0]
    by_plane = (4, 2, 2, 2, 160, 128)

    def flat(*shape):
        return pl.BlockSpec(shape, lambda k: (0,) * len(shape))

    return pl.pallas_call(
        feed_kernel,
        grid=(2,),
        in_specs=[
            pl.BlockSpec(by_plane, lambda k: (0, k, 0, 0, 0, 0)),
            pl.BlockSpec(by_plane, lambda k: (0, k, 0, 0, 1, 0)),
            pl.BlockSpec((4, 4, 2, 1, 160, 128), lambda k: (0, 0, 0, k, 2, 0)),
        ]
        + [flat(rows, PAD)] * 4,
        out_specs=[flat(rows, PAD)] * 4 + [flat(4, 4, 2, 2, 480, 128)],
        out_shape=[
            jax.ShapeDtypeStruct((rows, PAD), F32),
            jax.ShapeDtypeStruct((rows, PAD), BF),
            jax.ShapeDtypeStruct((rows, PAD), F32),
            jax.ShapeDtypeStruct((rows, PAD), BF),
            jax.ShapeDtypeStruct((4, 4, 2, 2, 480, 128), BF),
        ],
        scratch_shapes=[pltpu.VMEM((2 * rows, PAD), BF)] * 2
        + [pltpu.VMEM((FEED, PAD), BF)] * 3
        + [pltpu.VMEM((2 * rows, PAD), F32)] * 2,
        compiler_params=pltpu.CompilerParams(vmem_limit_bytes=VMEM_LIMIT),
        cost_estimate=pl.CostEstimate(flops=12 * 10**9, bytes_accessed=22 * 10**6, transcendentals=10**6),
    )(big, big, big, n_mine, n_other, dy_mine, dy_other)


def project_out_kernel(info, o_ref, mine_ref, other_ref, x_ref, gain_ref, hidden_ref, normed_ref, w_ref, ob_ref, rows):
    core = info[2]
    for s in range(8):
        for j in range(8):
            lanes = slice(j * 128, j * 128 + 128)
            w_ref[s, core, :, lanes] = mine_ref[s // 4, s % 4, j // 2, j % 2]
            w_ref[s, 1 - core, :, lanes] = other_ref[s // 4, s % 4, j // 2, j % 2]
    for head in range(HEADS):
        g, r = head // GROUP, head % GROUP
        for half in range(2):
            piece = o_ref[g, half, :, r * SPAN : (r + 1) * SPAN]
            rows[head * 64 : head * 64 + 64, half * SPAN : (half + 1) * SPAN] = piece
    ob_ref[...] = jnp.zeros_like(ob_ref)
    for n in range(16):
        ob_ref[n * 64 : n * 64 + 60] = rows[n * 60 : n * 60 + 60].astype(BF)
    hidden = x_ref[...] + dot_first(ob_ref[...], w_ref[...].reshape(PAD, PAD))
    hidden_ref[...] = hidden
    inverse = lax.rsqrt(jnp.sum(hidden * hidden, axis=-1, keepdims=True) / D + EPS)
    normed_ref[...] = (hidden * inverse * gain_ref[...]).astype(BF)


def one_call(kernel, info, args, outs, scratch, flops):
    return pl.pallas_call(
        kernel,
        in_specs=[pl.BlockSpec(memory_space=pltpu.SMEM)] + [pl.BlockSpec(memory_space=pltpu.VMEM)] * len(args),
        out_specs=[pl.BlockSpec(memory_space=pltpu.VMEM)] * len(outs),
        out_shape=[jax.ShapeDtypeStruct(shape, kind) for shape, kind in outs],
        scratch_shapes=scratch,
        compiler_params=pltpu.CompilerParams(vmem_limit_bytes=VMEM_LIMIT),
        cost_estimate=pl.CostEstimate(flops=flops, bytes_accessed=10 * 10**6, transcendentals=0),
    )(info, *args)


def project_out(info, attended, mine, other, layer_input, gain):
    rows = layer_input.shape[0]
    return one_call(
        project_out_kernel,
        info,
        (attended, mine, other, layer_input, gain),
        [((rows, PAD), F32), ((rows, PAD), BF), ((8, 2, 64, PAD), BF), ((PAD, rows), BF)],
        [pltpu.VMEM((D, rows), F32)],
        10**9,
    )


def between_kernel(
    info, dn_ref, dn_other_ref, hidden_ref, gain_ref, dy_ref, w_ref, ob_ref, o_ref, total_ref,
    dh_ref, dnum_ref, delta_ref, mine_ref, other_ref, gain_grad_ref, rows, grads
):
    core = info[2]
    hidden, gain = hidden_ref[...], gain_ref[...]
    inverse = lax.rsqrt(jnp.sum(hidden * hidden, axis=-1, keepdims=True) / D + EPS)
    unit = hidden * inverse
    dn = dn_ref[...] + dn_other_ref[...].astype(F32)
    back, gain_grad = norm_back(dn, unit, inverse, gain)
    gain_grad_ref[...] = gain_grad[None]
    dh = dy_ref[...].astype(F32) + back
    dh_ref[...] = dh
    dh_low = dh.astype(BF)
    dob = dot_last(w_ref[...].reshape(PAD, PAD), dh_low)
    for n in range(16):
        rows[n * 60 : n * 60 + 60] = dob[n * 64 : n * 64 + 60].astype(BF).astype(F32)
    for head in range(HEADS):
        g, r = head // GROUP, head % GROUP
        for half in range(2):
            lanes = slice(r * SPAN, (r + 1) * SPAN)
            piece = rows[head * 64 : head * 64 + 64, half * SPAN : (half + 1) * SPAN]
            total = total_ref[g, half, :, lanes]
            dnum_ref[g, half, :, lanes] = (piece / total).astype(BF)
            summed = jnp.sum(piece * o_ref[g, half, :, lanes], axis=0, keepdims=True)
            delta_ref[g, half, :, lanes] = summed / total
    grads[...] = dot_plain(ob_ref[...], dh_low).astype(BF).reshape(8, 2, 64, PAD)
    for s in range(8):
        for j in range(8):
            lanes = slice(j * 128, j * 128 + 128)
            mine_ref[s // 4, s % 4, j // 2, j % 2] = grads[s, core, :, lanes]
            other_ref[s // 4, s % 4, j // 2, j % 2] = grads[s, 1 - core, :, lanes]


def between(info, dn, dn_other, hidden, gain, dy, w_out, attended_low, attended, total):
    rows = hidden.shape[0]
    return one_call(
        between_kernel,
        info,
        (dn, dn_other, hidden, gain, dy, w_out, attended_low, attended, total),
        [
            ((rows, PAD), F32),
            ((KV_HEADS, 2, HEAD_DIM, WIDTH), BF),
            ((KV_HEADS, 2, 1, WIDTH), F32),
            ((2, 4, 4, 2, 64, 128), BF),
            ((2, 4, 4, 2, 64, 128), BF),
            ((1, PAD), F32),
        ],
        [pltpu.VMEM((D, rows), F32), pltpu.VMEM((8, 2, 64, PAD), BF)],
        2 * 10**9,
    )


def pad_rows(value, count):
    return jnp.pad(value, ((0, count - value.shape[0]), (0, 0)))


def norm_forward(value, gain):
    inverse = lax.rsqrt(jnp.sum(value * value, axis=-1, keepdims=True) / D + EPS)
    unit = value * inverse
    return unit, inverse, (unit * gain).astype(BF)


def norm_back(grad, unit, inverse, gain):
    scaled = grad * gain
    inner = jnp.sum(scaled * unit, axis=-1, keepdims=True) / D
    return inverse * (scaled - unit * inner), jnp.sum(grad * unit, axis=0)


def body(
    tokens,
    w_query,
    w_key,
    w_value,
    w_out,
    w_gate,
    w_up,
    w_down,
    attention_norm_gain,
    feedforward_norm_gain,
    span_order,
    positions,
    out_grad,
):
    rows = tokens.shape[0]
    core = lax.axis_index("c")
    me = lax.axis_index(("x", "zh", "c"))

    small = jnp.concatenate([pad_rows(w_query.T, 64), pad_rows(w_key.T, 24), pad_rows(w_value.T, 24)], axis=0)
    small = pad_lanes(small)
    mixed = jnp.concatenate([w_down.reshape(2, 160, 60), w_out.reshape(2, 60, 60)], axis=1)
    mixed = lax.all_to_all(mixed, "c", 0, 0, tiled=True)
    mixed = jnp.concatenate([mixed[0], mixed[1]], axis=1)
    big = pad_lanes(jnp.concatenate([w_gate.T, w_up.T, mixed[:160]], axis=0))
    big = lax.all_gather(big, ("x",) + LINE, axis=0, tiled=True)
    w_out_block = pad_rows(pad_lanes(mixed[160:]), 64)

    order = span_order[0]
    own_pair = lax.dynamic_slice_in_dim(order, 2 * me, 2)
    own_low_half = (own_pair[0] > own_pair[1]).astype(jnp.int32)
    spans = order.reshape(8, 2, 2)
    info = jnp.concatenate(
        [
            jnp.stack([own_low_half, jnp.minimum(own_pair[0], own_pair[1]), core.astype(jnp.int32)]),
            jnp.zeros((5,), jnp.int32),
            lax.dynamic_index_in_dim(spans, core, 1, keepdims=False).reshape(16),
            lax.dynamic_index_in_dim(spans, 1 - core, 1, keepdims=False).reshape(16),
        ]
    ).astype(jnp.int32)
    place = jnp.concatenate(
        [
            lax.dynamic_slice_in_dim(positions[0], own_pair[0] * SPAN, SPAN, 0),
            lax.dynamic_slice_in_dim(positions[0], own_pair[1] * SPAN, SPAN, 0),
        ]
    )
    half_dim = HEAD_DIM // 2
    freq = jnp.power(ROPE_BASE, -jnp.arange(half_dim, dtype=F32) / half_dim)
    angle = freq[:, None] * place.astype(F32)[None, :]
    cosine, sine = jnp.cos(angle), jnp.sin(angle)

    gain_one = pad_width(attention_norm_gain[None])
    gain_two = pad_width(feedforward_norm_gain[None])
    layer_input = pad_width(tokens).astype(F32)
    dy = pad_width(out_grad)
    dy_other = other_core(dy)

    unit_one, inverse_one, normed_one = norm_forward(layer_input, gain_one)
    small, normed_one, info, cosine, sine = lax.optimization_barrier((small, normed_one, info, cosine, sine))
    small = to_chips(jnp.broadcast_to(small, (64, BLOCK, 128)))
    small = small.reshape(2, 4, 4, 2, BLOCK, 128)
    small_other = other_core(small)
    big, _ = lax.optimization_barrier((big, small_other))
    big = lax.all_gather(big, "y", axis=0, tiled=True).reshape(4, 4, 2, 2, 480, 128)
    w_all, query, kv_local = project(info, small, small_other, normed_one, cosine, sine)

    kv = lax.all_to_all(jnp.broadcast_to(kv_local, (8, rows, 640)), SEQ, 0, 0, tiled=True)
    kv = kv.reshape(8 * rows, 640)
    kv_other = other_core(kv)

    w_out_block, kv, kv_other = lax.optimization_barrier((w_out_block, kv, kv_other))
    w_out_mine = to_chips(jnp.broadcast_to(w_out_block, (64, 64, 128)))
    attended, total = attend(info, kv, kv_other, query)
    w_out_mine, attended = lax.optimization_barrier((w_out_mine, attended))
    w_out_mine = w_out_mine.reshape(2, 4, 4, 2, 64, 128)
    hidden, normed_two, w_out_full, attended_low = project_out(
        info, attended, w_out_mine, other_core(w_out_mine), layer_input, gain_two
    )
    big, normed_two = lax.optimization_barrier((big, normed_two))
    fed, fed_other, dn_two, dn_other, g_big = feed(big, normed_two, other_core(normed_two), dy, dy_other)
    dh, dnum, delta, g_out, g_out_other, gain_two_grad = between(
        info, dn_two, other_core(dn_other), hidden, gain_two, dy, w_out_full, attended_low, attended, total
    )
    result = cut_width((hidden + (fed + other_core(fed_other).astype(F32))).astype(BF))

    g_big = lax.psum_scatter(g_big.reshape(64 * 480, 128), "y", scatter_dimension=0, tiled=True)

    dq, dkv, dkv_other = attend_back(info, kv, kv_other, query, dnum, delta, 0, KV_HEADS)
    dkv = (dkv.astype(F32) + other_core(dkv_other).astype(F32)).astype(BF)
    dkv = lax.all_to_all(dkv.reshape(8, rows, 640), SEQ, 0, 0, tiled=True)
    dkv, g_big = lax.optimization_barrier((dkv, g_big))
    g_big = lax.psum_scatter(g_big, ("x",) + LINE, scatter_dimension=0, tiled=True)
    dkv = jnp.sum(dkv.astype(F32), axis=0)

    dn_one, g_small, g_other = project_back(info, dq, dkv, normed_one, cosine, sine, w_all)
    back_one, gain_one_grad = norm_back(dn_one, unit_one, inverse_one, gain_one)
    input_grad = cut_width((dh + back_one).astype(BF))

    g_small = (g_small.astype(F32) + other_core(g_other).astype(F32)).astype(BF).reshape(64, BLOCK, 128)
    g_out = (g_out.astype(F32) + other_core(g_out_other).astype(F32)).astype(BF).reshape(64, 64, 128)
    gain_grads = jnp.stack([gain_one_grad, gain_two_grad[0]])
    gain_grads = high_and_low(gain_grads + other_core(gain_grads))
    last = jnp.concatenate([g_small, g_out, jnp.broadcast_to(gain_grads, (64, 32, 128))], axis=1)
    last = jnp.sum(to_chips(last).astype(F32), axis=0)
    gain_grads = cut_width((last[176:192] + last[192:208]).reshape(2, PAD))

    g_big = g_big.astype(F32)
    mixed = jnp.concatenate([g_big[320:], last[112:172]], axis=0)[:, :120]
    halves = mixed.reshape(220, 2, 60)
    keep = lax.dynamic_index_in_dim(halves, core, 1, keepdims=False)
    came = other_core(lax.dynamic_index_in_dim(halves, 1 - core, 1, keepdims=False))
    first = core == 0
    mixed = jnp.stack([jnp.where(first, keep, came), jnp.where(first, came, keep)])
    return (
        result,
        input_grad,
        last[:60, :120].T,
        last[64:84, :120].T,
        last[88:108, :120].T,
        mixed[:, 160:].reshape(120, 60),
        g_big[:160, :120].T,
        g_big[160:320, :120].T,
        mixed[:, :160].reshape(320, 60),
        gain_grads[0],
        gain_grads[1],
    )


def solution(mesh):
    fine = Mesh(mesh.devices.reshape(2, 4, 4, 2, 2), ("zl", "y", "x", "zh", "c"))
    shard, ctx = ("zl", "y"), ("x", "zh", "c")
    both = shard + ctx
    return jax.shard_map(
        body,
        mesh=fine,
        in_specs=(P(both, None),)
        + (P(shard, ctx),) * 7
        + (P(), P(), P(shard, None), P(shard, None), P(both, None)),
        out_specs=(P(both, None), P(both, None)) + (P(shard, ctx),) * 7 + (P(), P()),
        check_vma=False,
    )
```

```python
import jax
import jax.numpy as jnp
from jax import lax
from jax.experimental import pallas as pl
from jax.experimental.pallas import tpu as pltpu
from jax.sharding import Mesh
from jax.sharding import PartitionSpec as P

D = 960
HEADS = 15
KV_HEADS = 5
GROUP = 3
HEAD_DIM = 64
SPAN = 128
PAD = 1024

EPS = 1e-05
ROPE_BASE = 100000.0

BF = jnp.bfloat16
F32 = jnp.float32

PLANE = ("y", "x")
LINE = ("zh", "zl")
CHIPS = ("zl", "y", "x", "zh")
SEQ = ("x", "zh")
SWAP = [(0, 1), (1, 0)]


def pad_width(value):
    rows = value.shape[0]
    blocks = value.reshape(rows, 8, 120)
    return jnp.pad(blocks, ((0, 0), (0, 0), (0, 8))).reshape(rows, PAD)


def cut_width(value):
    rows = value.shape[0]
    return value.reshape(rows, 8, 128)[:, :, :120].reshape(rows, D)


def pad_lanes(value):
    return jnp.pad(value, ((0, 0), (0, 128 - value.shape[1])))


def other_core(value):
    return lax.ppermute(value, "c", SWAP)


def sum_line(blocks):
    ring = ("zl", "zh")
    here = lax.axis_index(ring)

    def block_of(chip):
        return lax.dynamic_index_in_dim(blocks, 2 * (chip % 2) + chip // 2, 0, keepdims=False)

    total = block_of(here).astype(F32)
    for turn in range(1, 4):
        came = lax.ppermute(block_of(here ^ turn), ring, [(n, n ^ turn) for n in range(4)])
        total = total + came.astype(F32)
    return total


def to_chips(blocks):
    return lax.all_to_all(blocks, CHIPS, 0, 0, tiled=True)


def high_and_low(value):
    high = value.astype(BF)
    low = (value - high.astype(F32)).astype(BF)
    return jnp.concatenate([high.reshape(16, 128), low.reshape(16, 128)], axis=0)


def dot_last(left, right):
    return lax.dot_general(left, right, (((1,), (1,)), ((), ())), preferred_element_type=F32)


def dot_first(left, right):
    return lax.dot_general(left, right, (((0,), (0,)), ((), ())), preferred_element_type=F32)


def dot_plain(left, right):
    return jnp.dot(left, right, preferred_element_type=F32)


VMEM_LIMIT = 56 * 1024 * 1024
WIDTH = GROUP * SPAN
TILES = 8
SUB = 2
STEP = TILES * SPAN
SEQ_LEN = 4096
FEED = 640


def sort_blocks(info, sources, target):
    def one(slot, carry):
        at = pl.ds(pl.multiple_of(slot * SPAN, SPAN), SPAN)
        for n, source in enumerate(sources):
            to = pl.ds(pl.multiple_of(info[8 + 16 * n + slot] * SPAN, SPAN), SPAN)
            target[to, :] = source[at, :]
        return carry

    lax.fori_loop(0, 16, one, 0)


def unsort_blocks(info, source, targets):
    def one(slot, carry):
        at = pl.ds(pl.multiple_of(slot * SPAN, SPAN), SPAN)
        for n, target in enumerate(targets):
            to = pl.ds(pl.multiple_of(info[8 + 16 * n + slot] * SPAN, SPAN), SPAN)
            target[at, :] = source[to, :].astype(target.dtype)
        return carry

    lax.fori_loop(0, 16, one, 0)


def causal_steps(info, tile):
    low_half, low = info[0], info[1]
    high = 31 - low
    low_last = lax.div(low, TILES)
    high_last = lax.div(high, TILES)

    def whole(step, carry):
        is_low = step < low_last
        tile(
            jnp.where(is_low, low_half, 1 - low_half),
            jnp.where(is_low, step, step - low_last),
            None,
        )
        return carry

    lax.fori_loop(0, 3, whole, 0, unroll=3)
    tile(low_half, low_last, (low - low_last * TILES) * SPAN)
    tile(1 - low_half, high_last, (high - high_last * TILES) * SPAN)


def key_rows_minus_query_lanes(rows):
    row = lax.broadcasted_iota(jnp.int32, (rows, WIDTH), 0)
    lane = lax.broadcasted_iota(jnp.int32, (rows, WIDTH), 1)
    return row - lax.rem(lane, SPAN)


def attend_kernel(info, mine_ref, other_ref, q_ref, out_ref, total_ref, keys_in_order, query, numer, total):
    sort_blocks(info, (mine_ref, other_ref), keys_in_order)
    query[...] = jnp.zeros_like(query)
    for half in range(2):
        query[half, :HEAD_DIM, :] = q_ref[0, half]
    numer[...] = jnp.zeros_like(numer)
    total[...] = jnp.zeros_like(total)

    def tile(half, step, limit):
        some = STEP // SUB
        parts, sums = [], []
        for n in range(SUB):
            keys = keys_in_order[pl.ds(pl.multiple_of(step * STEP + n * some, some), some), :]
            expo = jnp.exp(dot_plain(keys, query[half]))
            if limit is not None:
                expo = jnp.where(key_rows_minus_query_lanes(some) <= limit - n * some, expo, 0.0)
            parts.append(dot_plain(keys.T[HEAD_DIM:], expo.astype(BF)))
            sums.append(jnp.sum(expo.reshape(some // 8, 8, WIDTH), axis=0))
        numer[half] += sum(parts[1:], parts[0])
        total[half] += sum(sums[1:], sums[0])

    causal_steps(info, tile)
    for half in range(2):
        summed = jnp.sum(total[half], axis=0, keepdims=True)
        total_ref[0, half] = summed
        out_ref[0, half] = numer[half] / summed


HEAD_SPEC = pl.BlockSpec((1, 2, HEAD_DIM, WIDTH), lambda g, s: (g, 0, 0, 0))
ROW_SPEC = pl.BlockSpec((1, 2, 1, WIDTH), lambda g, s: (g, 0, 0, 0))
KV_SPEC = pl.BlockSpec((SEQ_LEN // 2, 2 * HEAD_DIM), lambda g, s: (0, g))
HEAD_F32 = jax.ShapeDtypeStruct((KV_HEADS, 2, HEAD_DIM, WIDTH), F32)


def attend(info, mine, other, query):
    return pl.pallas_call(
        attend_kernel,
        grid_spec=pltpu.PrefetchScalarGridSpec(
            num_scalar_prefetch=1,
            grid=(KV_HEADS,),
            in_specs=[KV_SPEC, KV_SPEC, HEAD_SPEC],
            out_specs=[HEAD_SPEC, ROW_SPEC],
            scratch_shapes=[
                pltpu.VMEM((SEQ_LEN, 2 * HEAD_DIM), BF),
                pltpu.VMEM((2, 2 * HEAD_DIM, WIDTH), BF),
                pltpu.VMEM((2, HEAD_DIM, WIDTH), F32),
                pltpu.VMEM((2, 8, WIDTH), F32),
            ],
        ),
        out_shape=[HEAD_F32, jax.ShapeDtypeStruct((KV_HEADS, 2, 1, WIDTH), F32)],
        compiler_params=pltpu.CompilerParams(vmem_limit_bytes=VMEM_LIMIT),
        cost_estimate=pl.CostEstimate(flops=4 * 10**9, bytes_accessed=8 * 10**6, transcendentals=8 * 10**6),
    )(info, mine, other, query)


def attend_back_kernel(
    info, mine_ref, other_ref, q_ref, dnum_ref, delta_ref, dq_ref, dmine_ref, dother_ref, keys_in_order, wide, tall, dq, dkv
):
    sort_blocks(info, (mine_ref, other_ref), keys_in_order)
    for half in range(2):
        zero = jnp.zeros((HEAD_DIM, WIDTH), BF)
        both = jnp.concatenate(
            [
                jnp.concatenate([q_ref[0, half], zero], axis=1),
                jnp.concatenate([zero, dnum_ref[0, half]], axis=1),
            ],
            axis=0,
        )
        wide[half] = both
        tall[half] = both.T
    dq[...] = jnp.zeros_like(dq)
    dkv[...] = jnp.zeros_like(dkv)

    def tile(half, step, limit):
        some = STEP // SUB
        parts = []
        for n in range(SUB):
            at = pl.ds(pl.multiple_of(step * STEP + n * some, some), some)
            keys = keys_in_order[at, :]
            scores = dot_plain(keys, wide[half])
            expo = jnp.exp(scores[:, :WIDTH])
            if limit is not None:
                expo = jnp.where(key_rows_minus_query_lanes(some) <= limit - n * some, expo, 0.0)
            grads = (expo * (scores[:, WIDTH:] - delta_ref[0, half])).astype(BF)
            pair = jnp.concatenate([grads, expo.astype(BF)], axis=1)
            dkv[at, :] += dot_plain(pair, tall[half])
            parts.append(dot_plain(keys.T[:HEAD_DIM], grads))
        dq[half] += sum(parts[1:], parts[0])

    causal_steps(info, tile)
    for half in range(2):
        dq_ref[0, half] = dq[half] * (HEAD_DIM**-0.5)
    unsort_blocks(info, dkv, (dmine_ref, dother_ref))


def attend_back(info, mine, other, query, dnum, delta, first, count):
    rows = mine.shape[0]

    def at(shape, offset):
        return pl.BlockSpec(shape, lambda g, s: (g + offset, 0, 0, 0))

    def kv_at(offset):
        return pl.BlockSpec((rows, 2 * HEAD_DIM), lambda g, s: (0, g + offset))

    head, row = (1, 2, HEAD_DIM, WIDTH), (1, 2, 1, WIDTH)
    return pl.pallas_call(
        attend_back_kernel,
        grid_spec=pltpu.PrefetchScalarGridSpec(
            num_scalar_prefetch=1,
            grid=(count,),
            in_specs=[kv_at(first), kv_at(first), at(head, first), at(head, first), at(row, first)],
            out_specs=[at(head, 0), kv_at(0), kv_at(0)],
            scratch_shapes=[
                pltpu.VMEM((SEQ_LEN, 2 * HEAD_DIM), BF),
                pltpu.VMEM((2, 2 * HEAD_DIM, 2 * WIDTH), BF),
                pltpu.VMEM((2, 2 * WIDTH, 2 * HEAD_DIM), BF),
                pltpu.VMEM((2, HEAD_DIM, WIDTH), F32),
                pltpu.VMEM((SEQ_LEN, 2 * HEAD_DIM), F32),
            ],
        ),
        out_shape=[jax.ShapeDtypeStruct((count, 2, HEAD_DIM, WIDTH), F32)]
        + [jax.ShapeDtypeStruct((rows, count * 2 * HEAD_DIM), BF)] * 2,
        compiler_params=pltpu.CompilerParams(vmem_limit_bytes=VMEM_LIMIT),
        cost_estimate=pl.CostEstimate(
            flops=2 * count * 10**9, bytes_accessed=count * 3 * 10**6, transcendentals=count * 2 * 10**6
        ),
    )(info, mine, other, query, dnum, delta)


PARTS = ((0, 60), (64, 20), (88, 20))
BLOCK = 112


def project_kernel(info, mine_ref, other_ref, normed_ref, cos_ref, sin_ref, w_ref, query_ref, kv_ref, q_rows, k_rows, v_rows, pair):
    step = pl.program_id(0)
    core = info[2]
    for at in range(8):
        lanes = slice(at * 128, at * 128 + 128)
        w_ref[0, core, :, lanes] = mine_ref[at // 4, at % 4, 0, 0]
        w_ref[0, 1 - core, :, lanes] = other_ref[at // 4, at % 4, 0, 0]
    made = dot_last(w_ref[0].reshape(2 * BLOCK, PAD), normed_ref[...])
    for (start, count), rows in zip(PARTS, (q_rows, k_rows, v_rows)):
        pair[0:count] = made[start : start + count]
        pair[count : 2 * count] = made[BLOCK + start : BLOCK + start + count]
        rows[pl.ds(pl.multiple_of(step * 2 * count, 8), 2 * count), :] = pair[0 : 2 * count]

    @pl.when(step == 7)
    def _():
        cosine, sine = cos_ref[...], sin_ref[...]

        def turned(rows, head):
            first = rows[head * 64 : head * 64 + 32]
            second = rows[head * 64 + 32 : head * 64 + 64]
            return jnp.concatenate([first * cosine - second * sine, second * cosine + first * sine], axis=0)

        for g in range(KV_HEADS):
            for r in range(GROUP):
                head = turned(q_rows, GROUP * g + r).astype(BF) * BF(HEAD_DIM**-0.5)
                for half in range(2):
                    query_ref[g, half, :, r * SPAN : (r + 1) * SPAN] = head[:, half * SPAN : (half + 1) * SPAN]
            both = jnp.concatenate([turned(k_rows, g), v_rows[g * 64 : g * 64 + 64]], axis=0)
            kv_ref[:, g * 128 : (g + 1) * 128] = both.T.astype(BF)


def whole_spec(*shape):
    return pl.BlockSpec(shape, lambda j, s: (0,) * len(shape))


SMALL_SPEC = pl.BlockSpec((2, 4, 1, 1, BLOCK, 128), lambda j, s: (0, 0, j // 2, j % 2, 0, 0))
W_SPEC = pl.BlockSpec((1, 2, BLOCK, PAD), lambda j, s: (j, 0, 0, 0))


def project(info, mine, other, normed, cosine, sine):
    rows = normed.shape[0]
    return pl.pallas_call(
        project_kernel,
        grid_spec=pltpu.PrefetchScalarGridSpec(
            num_scalar_prefetch=1,
            grid=(8,),
            in_specs=[SMALL_SPEC, SMALL_SPEC, whole_spec(rows, PAD), whole_spec(32, rows), whole_spec(32, rows)],
            out_specs=[W_SPEC, whole_spec(KV_HEADS, 2, HEAD_DIM, WIDTH), whole_spec(rows, 640)],
            scratch_shapes=[
                pltpu.VMEM((D, rows), F32),
                pltpu.VMEM((320, rows), F32),
                pltpu.VMEM((320, rows), F32),
                pltpu.VMEM((120, rows), F32),
            ],
        ),
        out_shape=[
            jax.ShapeDtypeStruct((8, 2, BLOCK, PAD), BF),
            jax.ShapeDtypeStruct((KV_HEADS, 2, HEAD_DIM, WIDTH), BF),
            jax.ShapeDtypeStruct((rows, 640), BF),
        ],
        compiler_params=pltpu.CompilerParams(vmem_limit_bytes=VMEM_LIMIT),
        cost_estimate=pl.CostEstimate(flops=10**9, bytes_accessed=8 * 10**6, transcendentals=0),
    )(info, mine, other, normed, cosine, sine)


def project_back_kernel(
    info, dq_ref, dkv_ref, normed_ref, cos_ref, sin_ref, w_ref, dn_ref, mine_ref, other_ref, q_rows, k_rows, v_rows, pair, blocks, grads
):
    step = pl.program_id(0)
    core = info[2]

    @pl.when(step == 0)
    def _():
        cosine, sine = cos_ref[...], sin_ref[...]

        def turned_back(value):
            first, second = value[:32], value[32:]
            return jnp.concatenate([first * cosine + second * sine, second * cosine - first * sine], axis=0)

        for g in range(KV_HEADS):
            for r in range(GROUP):
                lanes = slice(r * SPAN, (r + 1) * SPAN)
                head = jnp.concatenate([dq_ref[g, 0, :, lanes], dq_ref[g, 1, :, lanes]], axis=1)
                at = (GROUP * g + r) * 64
                q_rows[at : at + 64] = turned_back(head)
            both = dkv_ref[:, g * 128 : (g + 1) * 128].T
            k_rows[g * 64 : g * 64 + 64] = turned_back(both[:64])
            v_rows[g * 64 : g * 64 + 64] = both[64:]
        blocks[...] = jnp.zeros_like(blocks)
        dn_ref[...] = jnp.zeros_like(dn_ref)

    for (start, count), rows in zip(PARTS, (q_rows, k_rows, v_rows)):
        pair[0 : 2 * count] = rows[pl.ds(pl.multiple_of(step * 2 * count, 8), 2 * count), :]
        blocks[start : start + count] = pair[0:count]
        blocks[BLOCK + start : BLOCK + start + count] = pair[count : 2 * count]
    block = blocks[...].astype(BF)
    dn_ref[...] += dot_first(block, w_ref[0].reshape(2 * BLOCK, PAD))
    grads[...] = dot_plain(block, normed_ref[...]).astype(BF).reshape(2, BLOCK, PAD)
    for at in range(8):
        lanes = slice(at * 128, at * 128 + 128)
        mine_ref[at // 4, at % 4, 0, 0] = grads[core, :, lanes]
        other_ref[at // 4, at % 4, 0, 0] = grads[1 - core, :, lanes]


def project_back(info, dq, dkv, normed, cosine, sine, w_all):
    rows = normed.shape[0]
    small = jax.ShapeDtypeStruct((2, 4, 4, 2, BLOCK, 128), BF)
    return pl.pallas_call(
        project_back_kernel,
        grid_spec=pltpu.PrefetchScalarGridSpec(
            num_scalar_prefetch=1,
            grid=(8,),
            in_specs=[
                whole_spec(*dq.shape),
                whole_spec(rows, 640),
                whole_spec(rows, PAD),
                whole_spec(32, rows),
                whole_spec(32, rows),
                W_SPEC,
            ],
            out_specs=[whole_spec(rows, PAD), SMALL_SPEC, SMALL_SPEC],
            scratch_shapes=[
                pltpu.VMEM((D, rows), F32),
                pltpu.VMEM((320, rows), F32),
                pltpu.VMEM((320, rows), F32),
                pltpu.VMEM((120, rows), F32),
                pltpu.VMEM((2 * BLOCK, rows), F32),
                pltpu.VMEM((2, BLOCK, PAD), BF),
            ],
        ),
        out_shape=[jax.ShapeDtypeStruct((rows, PAD), F32), small, small],
        compiler_params=pltpu.CompilerParams(vmem_limit_bytes=VMEM_LIMIT),
        cost_estimate=pl.CostEstimate(flops=2 * 10**9, bytes_accessed=10 * 10**6, transcendentals=0),
    )(info, dq, dkv, normed, cosine, sine, w_all)


def feed_kernel(
    gate_ref, up_ref, down_ref, n_mine, n_other, dy_mine, dy_other,
    fed_mine, fed_other, dn_mine, dn_other, grad_ref, normed, dy, wg, wu, wd, fed, dn
):
    step = pl.program_id(0)
    rows = n_mine.shape[0]

    @pl.when(step == 0)
    def _():
        normed[:rows] = n_mine[...]
        normed[rows:] = n_other[...]
        dy[:rows] = dy_mine[...]
        dy[rows:] = dy_other[...]
        fed[...] = jnp.zeros_like(fed)
        dn[...] = jnp.zeros_like(dn)

    for group in range(4):
        part = slice(group * 160, group * 160 + 160)
        for at in range(8):
            lanes = slice(at * 128, at * 128 + 128)
            wg[part, lanes] = gate_ref[at % 4, group // 2, group % 2, at // 4]
            wu[part, lanes] = up_ref[at % 4, group // 2, group % 2, at // 4]
            wd[part, lanes] = down_ref[group, at // 2, at % 2, 0]
    gate = dot_last(normed[...], wg[...])
    upward = dot_last(normed[...], wu[...])
    dact = dot_last(dy[...], wd[...])
    sigma = jax.nn.sigmoid(gate)
    silu_gate = gate * sigma
    active = (silu_gate * upward).astype(BF)
    dgate = (dact * upward * sigma * (1.0 + gate * (1.0 - sigma))).astype(BF)
    dup = (dact * silu_gate).astype(BF)
    fed[...] += dot_plain(active, wd[...])
    dn[...] += dot_plain(dgate, wg[...]) + dot_plain(dup, wu[...])
    g_gate = dot_first(dgate, normed[...]).astype(BF)
    g_up = dot_first(dup, normed[...]).astype(BF)
    g_down = dot_first(active, dy[...]).astype(BF)
    for group in range(4):
        part = slice(group * 160, group * 160 + 160)
        for at in range(8):
            lanes = slice(at * 128, at * 128 + 128)
            grad_ref[at % 4, 2 * step + group // 2, group % 2, at // 4, 0:160] = g_gate[part, lanes]
            grad_ref[at % 4, 2 * step + group // 2, group % 2, at // 4, 160:320] = g_up[part, lanes]
            grad_ref[group, at // 2, at % 2, step, 320:480] = g_down[part, lanes]

    @pl.when(step == 1)
    def _():
        fed_mine[...] = fed[:rows]
        fed_other[...] = fed[rows:].astype(BF)
        dn_mine[...] = dn[:rows]
        dn_other[...] = dn[rows:].astype(BF)


def feed(big, n_mine, n_other, dy_mine, dy_other):
    rows = n_mine.shape[0]
    by_plane = (4, 2, 2, 2, 160, 128)

    def flat(*shape):
        return pl.BlockSpec(shape, lambda k: (0,) * len(shape))

    return pl.pallas_call(
        feed_kernel,
        grid=(2,),
        in_specs=[
            pl.BlockSpec(by_plane, lambda k: (0, k, 0, 0, 0, 0)),
            pl.BlockSpec(by_plane, lambda k: (0, k, 0, 0, 1, 0)),
            pl.BlockSpec((4, 4, 2, 1, 160, 128), lambda k: (0, 0, 0, k, 2, 0)),
        ]
        + [flat(rows, PAD)] * 4,
        out_specs=[flat(rows, PAD)] * 4 + [flat(4, 4, 2, 2, 480, 128)],
        out_shape=[
            jax.ShapeDtypeStruct((rows, PAD), F32),
            jax.ShapeDtypeStruct((rows, PAD), BF),
            jax.ShapeDtypeStruct((rows, PAD), F32),
            jax.ShapeDtypeStruct((rows, PAD), BF),
            jax.ShapeDtypeStruct((4, 4, 2, 2, 480, 128), BF),
        ],
        scratch_shapes=[pltpu.VMEM((2 * rows, PAD), BF)] * 2
        + [pltpu.VMEM((FEED, PAD), BF)] * 3
        + [pltpu.VMEM((2 * rows, PAD), F32)] * 2,
        compiler_params=pltpu.CompilerParams(vmem_limit_bytes=VMEM_LIMIT),
        cost_estimate=pl.CostEstimate(flops=12 * 10**9, bytes_accessed=22 * 10**6, transcendentals=10**6),
    )(big, big, big, n_mine, n_other, dy_mine, dy_other)


def project_out_kernel(info, o_ref, mine_ref, other_ref, x_ref, gain_ref, hidden_ref, normed_ref, w_ref, ob_ref, rows):
    core = info[2]
    for s in range(8):
        for j in range(8):
            lanes = slice(j * 128, j * 128 + 128)
            w_ref[s, core, :, lanes] = mine_ref[s // 4, s % 4, j // 2, j % 2]
            w_ref[s, 1 - core, :, lanes] = other_ref[s // 4, s % 4, j // 2, j % 2]
    for head in range(HEADS):
        g, r = head // GROUP, head % GROUP
        for half in range(2):
            piece = o_ref[g, half, :, r * SPAN : (r + 1) * SPAN]
            rows[head * 64 : head * 64 + 64, half * SPAN : (half + 1) * SPAN] = piece
    ob_ref[...] = jnp.zeros_like(ob_ref)
    for n in range(16):
        ob_ref[n * 64 : n * 64 + 60] = rows[n * 60 : n * 60 + 60].astype(BF)
    hidden = x_ref[...] + dot_first(ob_ref[...], w_ref[...].reshape(PAD, PAD))
    hidden_ref[...] = hidden
    inverse = lax.rsqrt(jnp.sum(hidden * hidden, axis=-1, keepdims=True) / D + EPS)
    normed_ref[...] = (hidden * inverse * gain_ref[...]).astype(BF)


def one_call(kernel, info, args, outs, scratch, flops):
    return pl.pallas_call(
        kernel,
        in_specs=[pl.BlockSpec(memory_space=pltpu.SMEM)] + [pl.BlockSpec(memory_space=pltpu.VMEM)] * len(args),
        out_specs=[pl.BlockSpec(memory_space=pltpu.VMEM)] * len(outs),
        out_shape=[jax.ShapeDtypeStruct(shape, kind) for shape, kind in outs],
        scratch_shapes=scratch,
        compiler_params=pltpu.CompilerParams(vmem_limit_bytes=VMEM_LIMIT),
        cost_estimate=pl.CostEstimate(flops=flops, bytes_accessed=10 * 10**6, transcendentals=0),
    )(info, *args)


def project_out(info, attended, mine, other, layer_input, gain):
    rows = layer_input.shape[0]
    return one_call(
        project_out_kernel,
        info,
        (attended, mine, other, layer_input, gain),
        [((rows, PAD), F32), ((rows, PAD), BF), ((8, 2, 64, PAD), BF), ((PAD, rows), BF)],
        [pltpu.VMEM((D, rows), F32)],
        10**9,
    )


def between_kernel(
    info, dn_ref, dn_other_ref, hidden_ref, gain_ref, dy_ref, w_ref, ob_ref, o_ref, total_ref,
    dh_ref, dnum_ref, delta_ref, mine_ref, other_ref, gain_grad_ref, rows, grads
):
    core = info[2]
    hidden, gain = hidden_ref[...], gain_ref[...]
    inverse = lax.rsqrt(jnp.sum(hidden * hidden, axis=-1, keepdims=True) / D + EPS)
    unit = hidden * inverse
    dn = dn_ref[...] + dn_other_ref[...].astype(F32)
    back, gain_grad = norm_back(dn, unit, inverse, gain)
    gain_grad_ref[...] = gain_grad[None]
    dh = dy_ref[...].astype(F32) + back
    dh_ref[...] = dh
    dh_low = dh.astype(BF)
    dob = dot_last(w_ref[...].reshape(PAD, PAD), dh_low)
    for n in range(16):
        rows[n * 60 : n * 60 + 60] = dob[n * 64 : n * 64 + 60].astype(BF).astype(F32)
    for head in range(HEADS):
        g, r = head // GROUP, head % GROUP
        for half in range(2):
            lanes = slice(r * SPAN, (r + 1) * SPAN)
            piece = rows[head * 64 : head * 64 + 64, half * SPAN : (half + 1) * SPAN]
            total = total_ref[g, half, :, lanes]
            dnum_ref[g, half, :, lanes] = (piece / total).astype(BF)
            summed = jnp.sum(piece * o_ref[g, half, :, lanes], axis=0, keepdims=True)
            delta_ref[g, half, :, lanes] = summed / total
    grads[...] = dot_plain(ob_ref[...], dh_low).astype(BF).reshape(8, 2, 64, PAD)
    for s in range(8):
        for j in range(8):
            lanes = slice(j * 128, j * 128 + 128)
            mine_ref[s // 4, s % 4, j // 2, j % 2] = grads[s, core, :, lanes]
            other_ref[s // 4, s % 4, j // 2, j % 2] = grads[s, 1 - core, :, lanes]


def between(info, dn, dn_other, hidden, gain, dy, w_out, attended_low, attended, total):
    rows = hidden.shape[0]
    return one_call(
        between_kernel,
        info,
        (dn, dn_other, hidden, gain, dy, w_out, attended_low, attended, total),
        [
            ((rows, PAD), F32),
            ((KV_HEADS, 2, HEAD_DIM, WIDTH), BF),
            ((KV_HEADS, 2, 1, WIDTH), F32),
            ((2, 4, 4, 2, 64, 128), BF),
            ((2, 4, 4, 2, 64, 128), BF),
            ((1, PAD), F32),
        ],
        [pltpu.VMEM((D, rows), F32), pltpu.VMEM((8, 2, 64, PAD), BF)],
        2 * 10**9,
    )


def pad_rows(value, count):
    return jnp.pad(value, ((0, count - value.shape[0]), (0, 0)))


def norm_forward(value, gain):
    inverse = lax.rsqrt(jnp.sum(value * value, axis=-1, keepdims=True) / D + EPS)
    unit = value * inverse
    return unit, inverse, (unit * gain).astype(BF)


def norm_back(grad, unit, inverse, gain):
    scaled = grad * gain
    inner = jnp.sum(scaled * unit, axis=-1, keepdims=True) / D
    return inverse * (scaled - unit * inner), jnp.sum(grad * unit, axis=0)


def body(
    tokens,
    w_query,
    w_key,
    w_value,
    w_out,
    w_gate,
    w_up,
    w_down,
    attention_norm_gain,
    feedforward_norm_gain,
    span_order,
    positions,
    out_grad,
):
    rows = tokens.shape[0]
    core = lax.axis_index("c")
    me = lax.axis_index(("x", "zh", "c"))

    small = jnp.concatenate([pad_rows(w_query.T, 64), pad_rows(w_key.T, 24), pad_rows(w_value.T, 24)], axis=0)
    small = pad_lanes(small)
    mixed = jnp.concatenate([w_down.reshape(2, 160, 60), w_out.reshape(2, 60, 60)], axis=1)
    mixed = lax.all_to_all(mixed, "c", 0, 0, tiled=True)
    mixed = jnp.concatenate([mixed[0], mixed[1]], axis=1)
    big = pad_lanes(jnp.concatenate([w_gate.T, w_up.T, mixed[:160]], axis=0))
    big = lax.all_gather(big, ("x",) + LINE, axis=0, tiled=True)
    w_out_block = pad_rows(pad_lanes(mixed[160:]), 64)

    order = span_order[0]
    own_pair = lax.dynamic_slice_in_dim(order, 2 * me, 2)
    own_low_half = (own_pair[0] > own_pair[1]).astype(jnp.int32)
    spans = order.reshape(8, 2, 2)
    info = jnp.concatenate(
        [
            jnp.stack([own_low_half, jnp.minimum(own_pair[0], own_pair[1]), core.astype(jnp.int32)]),
            jnp.zeros((5,), jnp.int32),
            lax.dynamic_index_in_dim(spans, core, 1, keepdims=False).reshape(16),
            lax.dynamic_index_in_dim(spans, 1 - core, 1, keepdims=False).reshape(16),
        ]
    ).astype(jnp.int32)
    place = jnp.concatenate(
        [
            lax.dynamic_slice_in_dim(positions[0], own_pair[0] * SPAN, SPAN, 0),
            lax.dynamic_slice_in_dim(positions[0], own_pair[1] * SPAN, SPAN, 0),
        ]
    )
    half_dim = HEAD_DIM // 2
    freq = jnp.power(ROPE_BASE, -jnp.arange(half_dim, dtype=F32) / half_dim)
    angle = freq[:, None] * place.astype(F32)[None, :]
    cosine, sine = jnp.cos(angle), jnp.sin(angle)

    gain_one = pad_width(attention_norm_gain[None])
    gain_two = pad_width(feedforward_norm_gain[None])
    layer_input = pad_width(tokens).astype(F32)
    dy = pad_width(out_grad)
    dy_other = other_core(dy)

    unit_one, inverse_one, normed_one = norm_forward(layer_input, gain_one)
    small, normed_one, info, cosine, sine = lax.optimization_barrier((small, normed_one, info, cosine, sine))
    small = to_chips(jnp.broadcast_to(small, (64, BLOCK, 128)))
    small = small.reshape(2, 4, 4, 2, BLOCK, 128)
    small_other = other_core(small)
    big, _ = lax.optimization_barrier((big, small_other))
    big = lax.all_gather(big, "y", axis=0, tiled=True).reshape(4, 4, 2, 2, 480, 128)
    w_all, query, kv_local = project(info, small, small_other, normed_one, cosine, sine)

    kv = lax.all_to_all(jnp.broadcast_to(kv_local, (8, rows, 640)), SEQ, 0, 0, tiled=True)
    kv = kv.reshape(8 * rows, 640)
    kv_other = other_core(kv)

    w_out_block, kv, kv_other = lax.optimization_barrier((w_out_block, kv, kv_other))
    w_out_mine = to_chips(jnp.broadcast_to(w_out_block, (64, 64, 128)))
    attended, total = attend(info, kv, kv_other, query)
    w_out_mine, attended = lax.optimization_barrier((w_out_mine, attended))
    w_out_mine = w_out_mine.reshape(2, 4, 4, 2, 64, 128)
    hidden, normed_two, w_out_full, attended_low = project_out(
        info, attended, w_out_mine, other_core(w_out_mine), layer_input, gain_two
    )
    big, normed_two = lax.optimization_barrier((big, normed_two))
    fed, fed_other, dn_two, dn_other, g_big = feed(big, normed_two, other_core(normed_two), dy, dy_other)
    dh, dnum, delta, g_out, g_out_other, gain_two_grad = between(
        info, dn_two, other_core(dn_other), hidden, gain_two, dy, w_out_full, attended_low, attended, total
    )
    result = cut_width((hidden + (fed + other_core(fed_other).astype(F32))).astype(BF))

    g_big = lax.psum_scatter(g_big.reshape(64 * 480, 128), "y", scatter_dimension=0, tiled=True)

    dq, dkv, dkv_other = attend_back(info, kv, kv_other, query, dnum, delta, 0, KV_HEADS)
    dkv = (dkv.astype(F32) + other_core(dkv_other).astype(F32)).astype(BF)
    dkv = lax.all_to_all(dkv.reshape(8, rows, 640), SEQ, 0, 0, tiled=True)
    dkv, g_big = lax.optimization_barrier((dkv, g_big))
    g_big = lax.psum_scatter(g_big, "x", scatter_dimension=0, tiled=True)
    g_big = sum_line(g_big.reshape(4, 480, 128))
    dkv = jnp.sum(dkv.astype(F32), axis=0)

    dn_one, g_small, g_other = project_back(info, dq, dkv, normed_one, cosine, sine, w_all)
    back_one, gain_one_grad = norm_back(dn_one, unit_one, inverse_one, gain_one)
    input_grad = cut_width((dh + back_one).astype(BF))

    g_small = (g_small.astype(F32) + other_core(g_other).astype(F32)).astype(BF).reshape(64, BLOCK, 128)
    g_out = (g_out.astype(F32) + other_core(g_out_other).astype(F32)).astype(BF).reshape(64, 64, 128)
    gain_grads = jnp.stack([gain_one_grad, gain_two_grad[0]])
    gain_grads = high_and_low(gain_grads + other_core(gain_grads))
    last = jnp.concatenate([g_small, g_out, jnp.broadcast_to(gain_grads, (64, 32, 128))], axis=1)
    last, g_big = lax.optimization_barrier((to_chips(last), g_big))
    last = jnp.sum(last.astype(F32), axis=0)
    gain_grads = cut_width((last[176:192] + last[192:208]).reshape(2, PAD))

    mixed = jnp.concatenate([g_big[320:], last[112:172]], axis=0)[:, :120]
    halves = mixed.reshape(220, 2, 60)
    keep = lax.dynamic_index_in_dim(halves, core, 1, keepdims=False)
    came = other_core(lax.dynamic_index_in_dim(halves, 1 - core, 1, keepdims=False))
    first = core == 0
    mixed = jnp.stack([jnp.where(first, keep, came), jnp.where(first, came, keep)])
    return (
        result,
        input_grad,
        last[:60, :120].T,
        last[64:84, :120].T,
        last[88:108, :120].T,
        mixed[:, 160:].reshape(120, 60),
        g_big[:160, :120].T,
        g_big[160:320, :120].T,
        mixed[:, :160].reshape(320, 60),
        gain_grads[0],
        gain_grads[1],
    )


def solution(mesh):
    fine = Mesh(mesh.devices.reshape(2, 4, 4, 2, 2), ("zl", "y", "x", "zh", "c"))
    shard, ctx = ("zl", "y"), ("x", "zh", "c")
    both = shard + ctx
    return jax.shard_map(
        body,
        mesh=fine,
        in_specs=(P(both, None),)
        + (P(shard, ctx),) * 7
        + (P(), P(), P(shard, None), P(shard, None), P(both, None)),
        out_specs=(P(both, None), P(both, None)) + (P(shard, ctx),) * 7 + (P(), P()),
        check_vma=False,
    )
```

```python
import jax
import jax.numpy as jnp
from jax import lax
from jax.experimental import pallas as pl
from jax.experimental.pallas import tpu as pltpu
from jax.sharding import Mesh
from jax.sharding import PartitionSpec as P

D = 960
HEADS = 15
KV_HEADS = 5
GROUP = 3
HEAD_DIM = 64
SPAN = 128
PAD = 1024

EPS = 1e-05
ROPE_BASE = 100000.0

BF = jnp.bfloat16
F32 = jnp.float32

PLANE = ("y", "x")
LINE = ("zh", "zl")
CHIPS = ("zl", "y", "x", "zh")
SEQ = ("x", "zh")
SWAP = [(0, 1), (1, 0)]


def pad_width(value):
    rows = value.shape[0]
    blocks = value.reshape(rows, 8, 120)
    return jnp.pad(blocks, ((0, 0), (0, 0), (0, 8))).reshape(rows, PAD)


def cut_width(value):
    rows = value.shape[0]
    return value.reshape(rows, 8, 128)[:, :, :120].reshape(rows, D)


def pad_lanes(value):
    return jnp.pad(value, ((0, 0), (0, 128 - value.shape[1])))


def other_core(value):
    return lax.ppermute(value, "c", SWAP)


def sum_line(blocks):
    ring = ("zl", "zh")
    here = lax.axis_index(ring)

    def block_of(chip):
        return lax.dynamic_index_in_dim(blocks, 2 * (chip % 2) + chip // 2, 0, keepdims=False)

    total = block_of(here).astype(F32)
    for turn in range(1, 4):
        came = lax.ppermute(block_of(here ^ turn), ring, [(n, n ^ turn) for n in range(4)])
        total = total + came.astype(F32)
    return total


def to_chips(blocks):
    return lax.all_to_all(blocks, CHIPS, 0, 0, tiled=True)


def dot_last(left, right):
    return lax.dot_general(left, right, (((1,), (1,)), ((), ())), preferred_element_type=F32)


def dot_first(left, right):
    return lax.dot_general(left, right, (((0,), (0,)), ((), ())), preferred_element_type=F32)


def dot_plain(left, right):
    return jnp.dot(left, right, preferred_element_type=F32)


VMEM_LIMIT = 56 * 1024 * 1024
WIDTH = GROUP * SPAN
TILES = 8
SUB = 2
STEP = TILES * SPAN
SEQ_LEN = 4096
FEED = 640


def sort_blocks(info, sources, target):
    def one(slot, carry):
        at = pl.ds(pl.multiple_of(slot * SPAN, SPAN), SPAN)
        for n, source in enumerate(sources):
            to = pl.ds(pl.multiple_of(info[8 + 16 * n + slot] * SPAN, SPAN), SPAN)
            target[to, :] = source[at, :]
        return carry

    lax.fori_loop(0, 16, one, 0)


def unsort_blocks(info, source, targets):
    def one(slot, carry):
        at = pl.ds(pl.multiple_of(slot * SPAN, SPAN), SPAN)
        for n, target in enumerate(targets):
            to = pl.ds(pl.multiple_of(info[8 + 16 * n + slot] * SPAN, SPAN), SPAN)
            target[at, :] = source[to, :].astype(target.dtype)
        return carry

    lax.fori_loop(0, 16, one, 0)


def causal_steps(info, tile):
    low_half, low = info[0], info[1]
    high = 31 - low
    low_last = lax.div(low, TILES)
    high_last = lax.div(high, TILES)

    def whole(step, carry):
        is_low = step < low_last
        tile(
            jnp.where(is_low, low_half, 1 - low_half),
            jnp.where(is_low, step, step - low_last),
            None,
        )
        return carry

    lax.fori_loop(0, 3, whole, 0, unroll=3)
    tile(low_half, low_last, (low - low_last * TILES) * SPAN)
    tile(1 - low_half, high_last, (high - high_last * TILES) * SPAN)


def key_rows_minus_query_lanes(rows):
    row = lax.broadcasted_iota(jnp.int32, (rows, WIDTH), 0)
    lane = lax.broadcasted_iota(jnp.int32, (rows, WIDTH), 1)
    return row - lax.rem(lane, SPAN)


def attend_kernel(info, mine_ref, other_ref, q_ref, out_ref, total_ref, keys_in_order, query, numer, total):
    sort_blocks(info, (mine_ref, other_ref), keys_in_order)
    query[...] = jnp.zeros_like(query)
    for half in range(2):
        query[half, :HEAD_DIM, :] = q_ref[0, half]
    numer[...] = jnp.zeros_like(numer)
    total[...] = jnp.zeros_like(total)

    def tile(half, step, limit):
        some = STEP // SUB
        parts, sums = [], []
        for n in range(SUB):
            keys = keys_in_order[pl.ds(pl.multiple_of(step * STEP + n * some, some), some), :]
            expo = jnp.exp(dot_plain(keys, query[half]))
            if limit is not None:
                expo = jnp.where(key_rows_minus_query_lanes(some) <= limit - n * some, expo, 0.0)
            parts.append(dot_plain(keys.T[HEAD_DIM:], expo.astype(BF)))
            sums.append(jnp.sum(expo.reshape(some // 8, 8, WIDTH), axis=0))
        numer[half] += sum(parts[1:], parts[0])
        total[half] += sum(sums[1:], sums[0])

    causal_steps(info, tile)
    for half in range(2):
        summed = jnp.sum(total[half], axis=0, keepdims=True)
        total_ref[0, half] = summed
        out_ref[0, half] = numer[half] / summed


HEAD_SPEC = pl.BlockSpec((1, 2, HEAD_DIM, WIDTH), lambda g, s: (g, 0, 0, 0))
ROW_SPEC = pl.BlockSpec((1, 2, 1, WIDTH), lambda g, s: (g, 0, 0, 0))
KV_SPEC = pl.BlockSpec((SEQ_LEN // 2, 2 * HEAD_DIM), lambda g, s: (0, g))
HEAD_F32 = jax.ShapeDtypeStruct((KV_HEADS, 2, HEAD_DIM, WIDTH), F32)


def attend(info, mine, other, query):
    return pl.pallas_call(
        attend_kernel,
        grid_spec=pltpu.PrefetchScalarGridSpec(
            num_scalar_prefetch=1,
            grid=(KV_HEADS,),
            in_specs=[KV_SPEC, KV_SPEC, HEAD_SPEC],
            out_specs=[HEAD_SPEC, ROW_SPEC],
            scratch_shapes=[
                pltpu.VMEM((SEQ_LEN, 2 * HEAD_DIM), BF),
                pltpu.VMEM((2, 2 * HEAD_DIM, WIDTH), BF),
                pltpu.VMEM((2, HEAD_DIM, WIDTH), F32),
                pltpu.VMEM((2, 8, WIDTH), F32),
            ],
        ),
        out_shape=[HEAD_F32, jax.ShapeDtypeStruct((KV_HEADS, 2, 1, WIDTH), F32)],
        compiler_params=pltpu.CompilerParams(vmem_limit_bytes=VMEM_LIMIT),
        cost_estimate=pl.CostEstimate(flops=4 * 10**9, bytes_accessed=8 * 10**6, transcendentals=8 * 10**6),
    )(info, mine, other, query)


def attend_back_kernel(
    info, mine_ref, other_ref, q_ref, dnum_ref, delta_ref, dq_ref, dmine_ref, dother_ref, keys_in_order, wide, tall, dq, dkv
):
    sort_blocks(info, (mine_ref, other_ref), keys_in_order)
    for half in range(2):
        zero = jnp.zeros((HEAD_DIM, WIDTH), BF)
        both = jnp.concatenate(
            [
                jnp.concatenate([q_ref[0, half], zero], axis=1),
                jnp.concatenate([zero, dnum_ref[0, half]], axis=1),
            ],
            axis=0,
        )
        wide[half] = both
        tall[half] = both.T
    dq[...] = jnp.zeros_like(dq)
    dkv[...] = jnp.zeros_like(dkv)

    def tile(half, step, limit):
        some = STEP // SUB
        parts = []
        for n in range(SUB):
            at = pl.ds(pl.multiple_of(step * STEP + n * some, some), some)
            keys = keys_in_order[at, :]
            scores = dot_plain(keys, wide[half])
            expo = jnp.exp(scores[:, :WIDTH])
            if limit is not None:
                expo = jnp.where(key_rows_minus_query_lanes(some) <= limit - n * some, expo, 0.0)
            grads = (expo * (scores[:, WIDTH:] - delta_ref[0, half])).astype(BF)
            pair = jnp.concatenate([grads, expo.astype(BF)], axis=1)
            dkv[at, :] += dot_plain(pair, tall[half])
            parts.append(dot_plain(keys.T[:HEAD_DIM], grads))
        dq[half] += sum(parts[1:], parts[0])

    causal_steps(info, tile)
    for half in range(2):
        dq_ref[0, half] = dq[half] * (HEAD_DIM**-0.5)
    unsort_blocks(info, dkv, (dmine_ref, dother_ref))


def attend_back(info, mine, other, query, dnum, delta, first, count):
    rows = mine.shape[0]

    def at(shape, offset):
        return pl.BlockSpec(shape, lambda g, s: (g + offset, 0, 0, 0))

    def kv_at(offset):
        return pl.BlockSpec((rows, 2 * HEAD_DIM), lambda g, s: (0, g + offset))

    head, row = (1, 2, HEAD_DIM, WIDTH), (1, 2, 1, WIDTH)
    return pl.pallas_call(
        attend_back_kernel,
        grid_spec=pltpu.PrefetchScalarGridSpec(
            num_scalar_prefetch=1,
            grid=(count,),
            in_specs=[kv_at(first), kv_at(first), at(head, first), at(head, first), at(row, first)],
            out_specs=[at(head, 0), kv_at(0), kv_at(0)],
            scratch_shapes=[
                pltpu.VMEM((SEQ_LEN, 2 * HEAD_DIM), BF),
                pltpu.VMEM((2, 2 * HEAD_DIM, 2 * WIDTH), BF),
                pltpu.VMEM((2, 2 * WIDTH, 2 * HEAD_DIM), BF),
                pltpu.VMEM((2, HEAD_DIM, WIDTH), F32),
                pltpu.VMEM((SEQ_LEN, 2 * HEAD_DIM), F32),
            ],
        ),
        out_shape=[jax.ShapeDtypeStruct((count, 2, HEAD_DIM, WIDTH), F32)]
        + [jax.ShapeDtypeStruct((rows, count * 2 * HEAD_DIM), BF)] * 2,
        compiler_params=pltpu.CompilerParams(vmem_limit_bytes=VMEM_LIMIT),
        cost_estimate=pl.CostEstimate(
            flops=2 * count * 10**9, bytes_accessed=count * 3 * 10**6, transcendentals=count * 2 * 10**6
        ),
    )(info, mine, other, query, dnum, delta)


PARTS = ((0, 60), (64, 20), (88, 20))
BLOCK = 112


def project_kernel(info, mine_ref, other_ref, normed_ref, cos_ref, sin_ref, w_ref, query_ref, kv_ref, q_rows, k_rows, v_rows, pair):
    step = pl.program_id(0)
    core = info[2]
    for at in range(8):
        lanes = slice(at * 128, at * 128 + 128)
        w_ref[0, core, :, lanes] = mine_ref[at // 4, at % 4, 0, 0]
        w_ref[0, 1 - core, :, lanes] = other_ref[at // 4, at % 4, 0, 0]
    made = dot_last(w_ref[0].reshape(2 * BLOCK, PAD), normed_ref[...])
    for (start, count), rows in zip(PARTS, (q_rows, k_rows, v_rows)):
        pair[0:count] = made[start : start + count]
        pair[count : 2 * count] = made[BLOCK + start : BLOCK + start + count]
        rows[pl.ds(pl.multiple_of(step * 2 * count, 8), 2 * count), :] = pair[0 : 2 * count]

    @pl.when(step == 7)
    def _():
        cosine, sine = cos_ref[...], sin_ref[...]

        def turned(rows, head):
            first = rows[head * 64 : head * 64 + 32]
            second = rows[head * 64 + 32 : head * 64 + 64]
            return jnp.concatenate([first * cosine - second * sine, second * cosine + first * sine], axis=0)

        for g in range(KV_HEADS):
            for r in range(GROUP):
                head = turned(q_rows, GROUP * g + r).astype(BF) * BF(HEAD_DIM**-0.5)
                for half in range(2):
                    query_ref[g, half, :, r * SPAN : (r + 1) * SPAN] = head[:, half * SPAN : (half + 1) * SPAN]
            both = jnp.concatenate([turned(k_rows, g), v_rows[g * 64 : g * 64 + 64]], axis=0)
            kv_ref[:, g * 128 : (g + 1) * 128] = both.T.astype(BF)


def whole_spec(*shape):
    return pl.BlockSpec(shape, lambda j, s: (0,) * len(shape))


SMALL_SPEC = pl.BlockSpec((2, 4, 1, 1, BLOCK, 128), lambda j, s: (0, 0, j // 2, j % 2, 0, 0))
W_SPEC = pl.BlockSpec((1, 2, BLOCK, PAD), lambda j, s: (j, 0, 0, 0))


def project(info, mine, other, normed, cosine, sine):
    rows = normed.shape[0]
    return pl.pallas_call(
        project_kernel,
        grid_spec=pltpu.PrefetchScalarGridSpec(
            num_scalar_prefetch=1,
            grid=(8,),
            in_specs=[SMALL_SPEC, SMALL_SPEC, whole_spec(rows, PAD), whole_spec(32, rows), whole_spec(32, rows)],
            out_specs=[W_SPEC, whole_spec(KV_HEADS, 2, HEAD_DIM, WIDTH), whole_spec(rows, 640)],
            scratch_shapes=[
                pltpu.VMEM((D, rows), F32),
                pltpu.VMEM((320, rows), F32),
                pltpu.VMEM((320, rows), F32),
                pltpu.VMEM((120, rows), F32),
            ],
        ),
        out_shape=[
            jax.ShapeDtypeStruct((8, 2, BLOCK, PAD), BF),
            jax.ShapeDtypeStruct((KV_HEADS, 2, HEAD_DIM, WIDTH), BF),
            jax.ShapeDtypeStruct((rows, 640), BF),
        ],
        compiler_params=pltpu.CompilerParams(vmem_limit_bytes=VMEM_LIMIT),
        cost_estimate=pl.CostEstimate(flops=10**9, bytes_accessed=8 * 10**6, transcendentals=0),
    )(info, mine, other, normed, cosine, sine)


def project_back_kernel(
    info, dq_ref, dkv_ref, normed_ref, cos_ref, sin_ref, w_ref, dn_ref, mine_ref, other_ref, q_rows, k_rows, v_rows, pair, blocks, grads
):
    step = pl.program_id(0)
    core = info[2]

    @pl.when(step == 0)
    def _():
        cosine, sine = cos_ref[...], sin_ref[...]

        def turned_back(value):
            first, second = value[:32], value[32:]
            return jnp.concatenate([first * cosine + second * sine, second * cosine - first * sine], axis=0)

        for g in range(KV_HEADS):
            for r in range(GROUP):
                lanes = slice(r * SPAN, (r + 1) * SPAN)
                head = jnp.concatenate([dq_ref[g, 0, :, lanes], dq_ref[g, 1, :, lanes]], axis=1)
                at = (GROUP * g + r) * 64
                q_rows[at : at + 64] = turned_back(head)
            both = dkv_ref[:, g * 128 : (g + 1) * 128].T
            k_rows[g * 64 : g * 64 + 64] = turned_back(both[:64])
            v_rows[g * 64 : g * 64 + 64] = both[64:]
        blocks[...] = jnp.zeros_like(blocks)
        dn_ref[...] = jnp.zeros_like(dn_ref)

    for (start, count), rows in zip(PARTS, (q_rows, k_rows, v_rows)):
        pair[0 : 2 * count] = rows[pl.ds(pl.multiple_of(step * 2 * count, 8), 2 * count), :]
        blocks[start : start + count] = pair[0:count]
        blocks[BLOCK + start : BLOCK + start + count] = pair[count : 2 * count]
    block = blocks[...].astype(BF)
    dn_ref[...] += dot_first(block, w_ref[0].reshape(2 * BLOCK, PAD))
    grads[...] = dot_plain(block, normed_ref[...]).astype(BF).reshape(2, BLOCK, PAD)
    for at in range(8):
        lanes = slice(at * 128, at * 128 + 128)
        mine_ref[at // 4, at % 4, 0, 0] = grads[core, :, lanes]
        other_ref[at // 4, at % 4, 0, 0] = grads[1 - core, :, lanes]


def project_back(info, dq, dkv, normed, cosine, sine, w_all):
    rows = normed.shape[0]
    small = jax.ShapeDtypeStruct((2, 4, 4, 2, BLOCK, 128), BF)
    return pl.pallas_call(
        project_back_kernel,
        grid_spec=pltpu.PrefetchScalarGridSpec(
            num_scalar_prefetch=1,
            grid=(8,),
            in_specs=[
                whole_spec(*dq.shape),
                whole_spec(rows, 640),
                whole_spec(rows, PAD),
                whole_spec(32, rows),
                whole_spec(32, rows),
                W_SPEC,
            ],
            out_specs=[whole_spec(rows, PAD), SMALL_SPEC, SMALL_SPEC],
            scratch_shapes=[
                pltpu.VMEM((D, rows), F32),
                pltpu.VMEM((320, rows), F32),
                pltpu.VMEM((320, rows), F32),
                pltpu.VMEM((120, rows), F32),
                pltpu.VMEM((2 * BLOCK, rows), F32),
                pltpu.VMEM((2, BLOCK, PAD), BF),
            ],
        ),
        out_shape=[jax.ShapeDtypeStruct((rows, PAD), F32), small, small],
        compiler_params=pltpu.CompilerParams(vmem_limit_bytes=VMEM_LIMIT),
        cost_estimate=pl.CostEstimate(flops=2 * 10**9, bytes_accessed=10 * 10**6, transcendentals=0),
    )(info, dq, dkv, normed, cosine, sine, w_all)


def feed_kernel(
    gate_ref, up_ref, down_ref, n_mine, n_other, dy_mine, dy_other,
    fed_mine, fed_other, dn_mine, dn_other, grad_ref, normed, dy, wg, wu, wd, fed, dn
):
    step = pl.program_id(0)
    rows = n_mine.shape[0]

    @pl.when(step == 0)
    def _():
        normed[:rows] = n_mine[...]
        normed[rows:] = n_other[...]
        dy[:rows] = dy_mine[...]
        dy[rows:] = dy_other[...]
        fed[...] = jnp.zeros_like(fed)
        dn[...] = jnp.zeros_like(dn)

    for group in range(4):
        part = slice(group * 160, group * 160 + 160)
        for at in range(8):
            lanes = slice(at * 128, at * 128 + 128)
            wg[part, lanes] = gate_ref[at % 4, group // 2, group % 2, at // 4]
            wu[part, lanes] = up_ref[at % 4, group // 2, group % 2, at // 4]
            wd[part, lanes] = down_ref[group, at // 2, at % 2, 0]
    gate = dot_last(normed[...], wg[...])
    upward = dot_last(normed[...], wu[...])
    dact = dot_last(dy[...], wd[...])
    sigma = jax.nn.sigmoid(gate)
    silu_gate = gate * sigma
    active = (silu_gate * upward).astype(BF)
    dgate = (dact * upward * sigma * (1.0 + gate * (1.0 - sigma))).astype(BF)
    dup = (dact * silu_gate).astype(BF)
    fed[...] += dot_plain(active, wd[...])
    dn[...] += dot_plain(dgate, wg[...]) + dot_plain(dup, wu[...])
    g_gate = dot_first(dgate, normed[...]).astype(BF)
    g_up = dot_first(dup, normed[...]).astype(BF)
    g_down = dot_first(active, dy[...]).astype(BF)
    for group in range(4):
        part = slice(group * 160, group * 160 + 160)
        for at in range(8):
            lanes = slice(at * 128, at * 128 + 128)
            grad_ref[at % 4, 2 * step + group // 2, group % 2, at // 4, 0:160] = g_gate[part, lanes]
            grad_ref[at % 4, 2 * step + group // 2, group % 2, at // 4, 160:320] = g_up[part, lanes]
            grad_ref[group, at // 2, at % 2, step, 320:480] = g_down[part, lanes]

    @pl.when(step == 1)
    def _():
        fed_mine[...] = fed[:rows]
        fed_other[...] = fed[rows:].astype(BF)
        dn_mine[...] = dn[:rows]
        dn_other[...] = dn[rows:].astype(BF)


def feed(big, n_mine, n_other, dy_mine, dy_other):
    rows = n_mine.shape[0]
    by_plane = (4, 2, 2, 2, 160, 128)

    def flat(*shape):
        return pl.BlockSpec(shape, lambda k: (0,) * len(shape))

    return pl.pallas_call(
        feed_kernel,
        grid=(2,),
        in_specs=[
            pl.BlockSpec(by_plane, lambda k: (0, k, 0, 0, 0, 0)),
            pl.BlockSpec(by_plane, lambda k: (0, k, 0, 0, 1, 0)),
            pl.BlockSpec((4, 4, 2, 1, 160, 128), lambda k: (0, 0, 0, k, 2, 0)),
        ]
        + [flat(rows, PAD)] * 4,
        out_specs=[flat(rows, PAD)] * 4 + [flat(4, 4, 2, 2, 480, 128)],
        out_shape=[
            jax.ShapeDtypeStruct((rows, PAD), F32),
            jax.ShapeDtypeStruct((rows, PAD), BF),
            jax.ShapeDtypeStruct((rows, PAD), F32),
            jax.ShapeDtypeStruct((rows, PAD), BF),
            jax.ShapeDtypeStruct((4, 4, 2, 2, 480, 128), BF),
        ],
        scratch_shapes=[pltpu.VMEM((2 * rows, PAD), BF)] * 2
        + [pltpu.VMEM((FEED, PAD), BF)] * 3
        + [pltpu.VMEM((2 * rows, PAD), F32)] * 2,
        compiler_params=pltpu.CompilerParams(vmem_limit_bytes=VMEM_LIMIT),
        cost_estimate=pl.CostEstimate(flops=12 * 10**9, bytes_accessed=22 * 10**6, transcendentals=10**6),
    )(big, big, big, n_mine, n_other, dy_mine, dy_other)


def project_out_kernel(info, o_ref, mine_ref, other_ref, x_ref, gain_ref, hidden_ref, normed_ref, w_ref, ob_ref, rows):
    core = info[2]
    for s in range(8):
        for j in range(8):
            lanes = slice(j * 128, j * 128 + 128)
            w_ref[s, core, :, lanes] = mine_ref[s // 4, s % 4, j // 2, j % 2]
            w_ref[s, 1 - core, :, lanes] = other_ref[s // 4, s % 4, j // 2, j % 2]
    for head in range(HEADS):
        g, r = head // GROUP, head % GROUP
        for half in range(2):
            piece = o_ref[g, half, :, r * SPAN : (r + 1) * SPAN]
            rows[head * 64 : head * 64 + 64, half * SPAN : (half + 1) * SPAN] = piece
    ob_ref[...] = jnp.zeros_like(ob_ref)
    for n in range(16):
        ob_ref[n * 64 : n * 64 + 60] = rows[n * 60 : n * 60 + 60].astype(BF)
    hidden = x_ref[...] + dot_first(ob_ref[...], w_ref[...].reshape(PAD, PAD))
    hidden_ref[...] = hidden
    inverse = lax.rsqrt(jnp.sum(hidden * hidden, axis=-1, keepdims=True) / D + EPS)
    normed_ref[...] = (hidden * inverse * gain_ref[...]).astype(BF)


def one_call(kernel, info, args, outs, scratch, flops):
    return pl.pallas_call(
        kernel,
        in_specs=[pl.BlockSpec(memory_space=pltpu.SMEM)] + [pl.BlockSpec(memory_space=pltpu.VMEM)] * len(args),
        out_specs=[pl.BlockSpec(memory_space=pltpu.VMEM)] * len(outs),
        out_shape=[jax.ShapeDtypeStruct(shape, kind) for shape, kind in outs],
        scratch_shapes=scratch,
        compiler_params=pltpu.CompilerParams(vmem_limit_bytes=VMEM_LIMIT),
        cost_estimate=pl.CostEstimate(flops=flops, bytes_accessed=10 * 10**6, transcendentals=0),
    )(info, *args)


def project_out(info, attended, mine, other, layer_input, gain):
    rows = layer_input.shape[0]
    return one_call(
        project_out_kernel,
        info,
        (attended, mine, other, layer_input, gain),
        [((rows, PAD), F32), ((rows, PAD), BF), ((8, 2, 64, PAD), BF), ((PAD, rows), BF)],
        [pltpu.VMEM((D, rows), F32)],
        10**9,
    )


def between_kernel(
    info, dn_ref, dn_other_ref, hidden_ref, gain_ref, dy_ref, w_ref, ob_ref, o_ref, total_ref,
    dh_ref, dnum_ref, delta_ref, mine_ref, other_ref, gain_grad_ref, rows, grads
):
    core = info[2]
    hidden, gain = hidden_ref[...], gain_ref[...]
    inverse = lax.rsqrt(jnp.sum(hidden * hidden, axis=-1, keepdims=True) / D + EPS)
    unit = hidden * inverse
    dn = dn_ref[...] + dn_other_ref[...].astype(F32)
    back, gain_grad = norm_back(dn, unit, inverse, gain)
    gain_grad_ref[...] = gain_grad[None]
    dh = dy_ref[...].astype(F32) + back
    dh_ref[...] = dh
    dh_low = dh.astype(BF)
    dob = dot_last(w_ref[...].reshape(PAD, PAD), dh_low)
    for n in range(16):
        rows[n * 60 : n * 60 + 60] = dob[n * 64 : n * 64 + 60].astype(BF).astype(F32)
    for head in range(HEADS):
        g, r = head // GROUP, head % GROUP
        for half in range(2):
            lanes = slice(r * SPAN, (r + 1) * SPAN)
            piece = rows[head * 64 : head * 64 + 64, half * SPAN : (half + 1) * SPAN]
            total = total_ref[g, half, :, lanes]
            dnum_ref[g, half, :, lanes] = (piece / total).astype(BF)
            summed = jnp.sum(piece * o_ref[g, half, :, lanes], axis=0, keepdims=True)
            delta_ref[g, half, :, lanes] = summed / total
    grads[...] = dot_plain(ob_ref[...], dh_low).astype(BF).reshape(8, 2, 64, PAD)
    for s in range(8):
        for j in range(8):
            lanes = slice(j * 128, j * 128 + 128)
            mine_ref[s // 4, s % 4, j // 2, j % 2] = grads[s, core, :, lanes]
            other_ref[s // 4, s % 4, j // 2, j % 2] = grads[s, 1 - core, :, lanes]


def between(info, dn, dn_other, hidden, gain, dy, w_out, attended_low, attended, total):
    rows = hidden.shape[0]
    return one_call(
        between_kernel,
        info,
        (dn, dn_other, hidden, gain, dy, w_out, attended_low, attended, total),
        [
            ((rows, PAD), F32),
            ((KV_HEADS, 2, HEAD_DIM, WIDTH), BF),
            ((KV_HEADS, 2, 1, WIDTH), F32),
            ((2, 4, 4, 2, 64, 128), BF),
            ((2, 4, 4, 2, 64, 128), BF),
            ((1, PAD), F32),
        ],
        [pltpu.VMEM((D, rows), F32), pltpu.VMEM((8, 2, 64, PAD), BF)],
        2 * 10**9,
    )


def pad_rows(value, count):
    return jnp.pad(value, ((0, count - value.shape[0]), (0, 0)))


def norm_forward(value, gain):
    inverse = lax.rsqrt(jnp.sum(value * value, axis=-1, keepdims=True) / D + EPS)
    unit = value * inverse
    return unit, inverse, (unit * gain).astype(BF)


def norm_back(grad, unit, inverse, gain):
    scaled = grad * gain
    inner = jnp.sum(scaled * unit, axis=-1, keepdims=True) / D
    return inverse * (scaled - unit * inner), jnp.sum(grad * unit, axis=0)


def body(
    tokens,
    w_query,
    w_key,
    w_value,
    w_out,
    w_gate,
    w_up,
    w_down,
    attention_norm_gain,
    feedforward_norm_gain,
    span_order,
    positions,
    out_grad,
):
    rows = tokens.shape[0]
    core = lax.axis_index("c")
    me = lax.axis_index(("x", "zh", "c"))

    small = jnp.concatenate([pad_rows(w_query.T, 64), pad_rows(w_key.T, 24), pad_rows(w_value.T, 24)], axis=0)
    small = pad_lanes(small)
    mixed = jnp.concatenate([w_down.reshape(2, 160, 60), w_out.reshape(2, 60, 60)], axis=1)
    mixed = lax.all_to_all(mixed, "c", 0, 0, tiled=True)
    mixed = jnp.concatenate([mixed[0], mixed[1]], axis=1)
    big = pad_lanes(jnp.concatenate([w_gate.T, w_up.T, mixed[:160]], axis=0))
    big = lax.all_gather(big, ("x",) + LINE, axis=0, tiled=True)
    w_out_block = pad_rows(pad_lanes(mixed[160:]), 64)

    order = span_order[0]
    own_pair = lax.dynamic_slice_in_dim(order, 2 * me, 2)
    own_low_half = (own_pair[0] > own_pair[1]).astype(jnp.int32)
    spans = order.reshape(8, 2, 2)
    info = jnp.concatenate(
        [
            jnp.stack([own_low_half, jnp.minimum(own_pair[0], own_pair[1]), core.astype(jnp.int32)]),
            jnp.zeros((5,), jnp.int32),
            lax.dynamic_index_in_dim(spans, core, 1, keepdims=False).reshape(16),
            lax.dynamic_index_in_dim(spans, 1 - core, 1, keepdims=False).reshape(16),
        ]
    ).astype(jnp.int32)
    place = jnp.concatenate(
        [
            lax.dynamic_slice_in_dim(positions[0], own_pair[0] * SPAN, SPAN, 0),
            lax.dynamic_slice_in_dim(positions[0], own_pair[1] * SPAN, SPAN, 0),
        ]
    )
    half_dim = HEAD_DIM // 2
    freq = jnp.power(ROPE_BASE, -jnp.arange(half_dim, dtype=F32) / half_dim)
    angle = freq[:, None] * place.astype(F32)[None, :]
    cosine, sine = jnp.cos(angle), jnp.sin(angle)

    gain_one = pad_width(attention_norm_gain[None])
    gain_two = pad_width(feedforward_norm_gain[None])
    layer_input = pad_width(tokens).astype(F32)
    dy = pad_width(out_grad)
    dy_other = other_core(dy)

    unit_one, inverse_one, normed_one = norm_forward(layer_input, gain_one)
    small, normed_one, info, cosine, sine = lax.optimization_barrier((small, normed_one, info, cosine, sine))
    small = to_chips(jnp.broadcast_to(small, (64, BLOCK, 128)))
    small = small.reshape(2, 4, 4, 2, BLOCK, 128)
    small_other = other_core(small)
    big, _ = lax.optimization_barrier((big, small_other))
    big = lax.all_gather(big, "y", axis=0, tiled=True).reshape(4, 4, 2, 2, 480, 128)
    w_all, query, kv_local = project(info, small, small_other, normed_one, cosine, sine)

    kv = lax.all_to_all(jnp.broadcast_to(kv_local, (8, rows, 640)), SEQ, 0, 0, tiled=True)
    kv = kv.reshape(8 * rows, 640)
    kv_other = other_core(kv)

    w_out_block, kv, kv_other = lax.optimization_barrier((w_out_block, kv, kv_other))
    w_out_mine = to_chips(jnp.broadcast_to(w_out_block, (64, 64, 128)))
    attended, total = attend(info, kv, kv_other, query)
    w_out_mine, attended = lax.optimization_barrier((w_out_mine, attended))
    w_out_mine = w_out_mine.reshape(2, 4, 4, 2, 64, 128)
    hidden, normed_two, w_out_full, attended_low = project_out(
        info, attended, w_out_mine, other_core(w_out_mine), layer_input, gain_two
    )
    big, normed_two = lax.optimization_barrier((big, normed_two))
    fed, fed_other, dn_two, dn_other, g_big = feed(big, normed_two, other_core(normed_two), dy, dy_other)
    dh, dnum, delta, g_out, g_out_other, gain_two_grad = between(
        info, dn_two, other_core(dn_other), hidden, gain_two, dy, w_out_full, attended_low, attended, total
    )
    result = cut_width((hidden + (fed + other_core(fed_other).astype(F32))).astype(BF))

    g_big = lax.psum_scatter(g_big.reshape(64 * 480, 128), "y", scatter_dimension=0, tiled=True)

    dq, dkv, dkv_other = attend_back(info, kv, kv_other, query, dnum, delta, 0, KV_HEADS)
    dkv = (dkv.astype(F32) + other_core(dkv_other).astype(F32)).astype(BF)
    g_out = (g_out.astype(F32) + other_core(g_out_other).astype(F32)).astype(BF).reshape(64, 64, 128)
    dkv, g_out = lax.optimization_barrier((dkv, g_out))
    dkv = lax.all_to_all(dkv.reshape(8, rows, 640), SEQ, 0, 0, tiled=True)
    dkv, g_big = lax.optimization_barrier((dkv, g_big))
    g_big = lax.psum_scatter(g_big, "x", scatter_dimension=0, tiled=True)
    g_big = sum_line(g_big.reshape(4, 480, 128))
    dkv = jnp.sum(dkv.astype(F32), axis=0)

    dn_one, g_small, g_other = project_back(info, dq, dkv, normed_one, cosine, sine, w_all)
    back_one, gain_one_grad = norm_back(dn_one, unit_one, inverse_one, gain_one)
    input_grad = cut_width((dh + back_one).astype(BF))

    g_small = (g_small.astype(F32) + other_core(g_other).astype(F32)).astype(BF).reshape(64, BLOCK, 128)
    gain_grads = jnp.stack([gain_one_grad, gain_two_grad[0]])
    gain_grads = (gain_grads + other_core(gain_grads)).astype(BF).reshape(16, 128)
    spare = jnp.zeros((176, 128), BF)
    for n, at in enumerate((60, 84, 108, 172)):
        spare = lax.dynamic_update_slice(spare, gain_grads[4 * n : 4 * n + 4], (at, 0))
    last = jnp.concatenate([g_small, g_out], axis=1) + spare

    last, _ = lax.optimization_barrier((to_chips(last), g_big))
    last = jnp.sum(last.astype(F32), axis=0)
    gain_grads = jnp.concatenate([last[at : at + 4] for at in (60, 84, 108, 172)], axis=0)
    gain_grads = cut_width(gain_grads.reshape(2, PAD))

    def all_rows(part):
        halves = part[:, :120].reshape(part.shape[0], 2, 60)
        keep = lax.dynamic_index_in_dim(halves, core, 1, keepdims=False)
        came = other_core(lax.dynamic_index_in_dim(halves, 1 - core, 1, keepdims=False))
        first = core == 0
        return jnp.concatenate([jnp.where(first, keep, came), jnp.where(first, came, keep)], axis=0)

    return (
        result,
        input_grad,
        last[:60, :120].T,
        last[64:84, :120].T,
        last[88:108, :120].T,
        all_rows(last[112:172]),
        g_big[:160, :120].T,
        g_big[160:320, :120].T,
        all_rows(g_big[320:]),
        gain_grads[0],
        gain_grads[1],
    )


def solution(mesh):
    fine = Mesh(mesh.devices.reshape(2, 4, 4, 2, 2), ("zl", "y", "x", "zh", "c"))
    shard, ctx = ("zl", "y"), ("x", "zh", "c")
    both = shard + ctx
    return jax.shard_map(
        body,
        mesh=fine,
        in_specs=(P(both, None),)
        + (P(shard, ctx),) * 7
        + (P(), P(), P(shard, None), P(shard, None), P(both, None)),
        out_specs=(P(both, None), P(both, None)) + (P(shard, ctx),) * 7 + (P(), P()),
        check_vma=False,
    )
```

```python
import jax
import jax.numpy as jnp
from jax import lax
from jax.experimental import pallas as pl
from jax.experimental.pallas import tpu as pltpu
from jax.sharding import Mesh
from jax.sharding import PartitionSpec as P

D = 960
HEADS = 15
KV_HEADS = 5
GROUP = 3
HEAD_DIM = 64
SPAN = 128
PAD = 1024

EPS = 1e-05
ROPE_BASE = 100000.0

BF = jnp.bfloat16
F32 = jnp.float32

PLANE = ("y", "x")
LINE = ("zh", "zl")
CHIPS = ("zl", "y", "x", "zh")
SEQ = ("x", "zh")
SWAP = [(0, 1), (1, 0)]


def pad_width(value):
    rows = value.shape[0]
    blocks = value.reshape(rows, 8, 120)
    return jnp.pad(blocks, ((0, 0), (0, 0), (0, 8))).reshape(rows, PAD)


def cut_width(value):
    rows = value.shape[0]
    return value.reshape(rows, 8, 128)[:, :, :120].reshape(rows, D)


def pad_lanes(value):
    return jnp.pad(value, ((0, 0), (0, 128 - value.shape[1])))


def other_core(value):
    return lax.ppermute(value, "c", SWAP)


def sum_line(blocks):
    ring = ("zl", "zh")
    here = lax.axis_index(ring)

    def block_of(chip):
        return lax.dynamic_index_in_dim(blocks, 2 * (chip % 2) + chip // 2, 0, keepdims=False)

    total = block_of(here).astype(F32)
    for turn in range(1, 4):
        came = lax.ppermute(block_of(here ^ turn), ring, [(n, n ^ turn) for n in range(4)])
        total = total + came.astype(F32)
    return total


def to_chips(blocks):
    return lax.all_to_all(blocks, CHIPS, 0, 0, tiled=True)


def dot_last(left, right):
    return lax.dot_general(left, right, (((1,), (1,)), ((), ())), preferred_element_type=F32)


def dot_first(left, right):
    return lax.dot_general(left, right, (((0,), (0,)), ((), ())), preferred_element_type=F32)


def dot_plain(left, right):
    return jnp.dot(left, right, preferred_element_type=F32)


VMEM_LIMIT = 56 * 1024 * 1024
WIDTH = GROUP * SPAN
TILES = 8
SUB = 2
STEP = TILES * SPAN
SEQ_LEN = 4096
FEED = 640


def sort_blocks(info, sources, target):
    def one(slot, carry):
        at = pl.ds(pl.multiple_of(slot * SPAN, SPAN), SPAN)
        for n, source in enumerate(sources):
            to = pl.ds(pl.multiple_of(info[8 + 16 * n + slot] * SPAN, SPAN), SPAN)
            target[to, :] = source[at, :]
        return carry

    lax.fori_loop(0, 16, one, 0)


def unsort_blocks(info, source, targets):
    def one(slot, carry):
        at = pl.ds(pl.multiple_of(slot * SPAN, SPAN), SPAN)
        for n, target in enumerate(targets):
            to = pl.ds(pl.multiple_of(info[8 + 16 * n + slot] * SPAN, SPAN), SPAN)
            target[at, :] = source[to, :].astype(target.dtype)
        return carry

    lax.fori_loop(0, 16, one, 0)


def causal_steps(info, tile):
    low_half, low = info[0], info[1]
    high = 31 - low
    low_last = lax.div(low, TILES)
    high_last = lax.div(high, TILES)

    def whole(step, carry):
        is_low = step < low_last
        tile(
            jnp.where(is_low, low_half, 1 - low_half),
            jnp.where(is_low, step, step - low_last),
            None,
        )
        return carry

    lax.fori_loop(0, 3, whole, 0, unroll=3)
    tile(low_half, low_last, (low - low_last * TILES) * SPAN)
    tile(1 - low_half, high_last, (high - high_last * TILES) * SPAN)


def key_rows_minus_query_lanes(rows):
    row = lax.broadcasted_iota(jnp.int32, (rows, WIDTH), 0)
    lane = lax.broadcasted_iota(jnp.int32, (rows, WIDTH), 1)
    return row - lax.rem(lane, SPAN)


def attend_kernel(info, mine_ref, other_ref, q_ref, out_ref, total_ref, keys_in_order, query, numer, total):
    sort_blocks(info, (mine_ref, other_ref), keys_in_order)
    query[...] = jnp.zeros_like(query)
    for half in range(2):
        query[half, :HEAD_DIM, :] = q_ref[0, half]
    numer[...] = jnp.zeros_like(numer)
    total[...] = jnp.zeros_like(total)

    def tile(half, step, limit):
        some = STEP // SUB
        parts, sums = [], []
        for n in range(SUB):
            keys = keys_in_order[pl.ds(pl.multiple_of(step * STEP + n * some, some), some), :]
            expo = jnp.exp(dot_plain(keys, query[half]))
            if limit is not None:
                expo = jnp.where(key_rows_minus_query_lanes(some) <= limit - n * some, expo, 0.0)
            parts.append(dot_plain(keys.T[HEAD_DIM:], expo.astype(BF)))
            sums.append(jnp.sum(expo.reshape(some // 8, 8, WIDTH), axis=0))
        numer[half] += sum(parts[1:], parts[0])
        total[half] += sum(sums[1:], sums[0])

    causal_steps(info, tile)
    for half in range(2):
        summed = jnp.sum(total[half], axis=0, keepdims=True)
        total_ref[0, half] = summed
        out_ref[0, half] = numer[half] / summed


HEAD_SPEC = pl.BlockSpec((1, 2, HEAD_DIM, WIDTH), lambda g, s: (g, 0, 0, 0))
ROW_SPEC = pl.BlockSpec((1, 2, 1, WIDTH), lambda g, s: (g, 0, 0, 0))
KV_SPEC = pl.BlockSpec((SEQ_LEN // 2, 2 * HEAD_DIM), lambda g, s: (0, g))
HEAD_F32 = jax.ShapeDtypeStruct((KV_HEADS, 2, HEAD_DIM, WIDTH), F32)


def attend(info, mine, other, query):
    return pl.pallas_call(
        attend_kernel,
        grid_spec=pltpu.PrefetchScalarGridSpec(
            num_scalar_prefetch=1,
            grid=(KV_HEADS,),
            in_specs=[KV_SPEC, KV_SPEC, HEAD_SPEC],
            out_specs=[HEAD_SPEC, ROW_SPEC],
            scratch_shapes=[
                pltpu.VMEM((SEQ_LEN, 2 * HEAD_DIM), BF),
                pltpu.VMEM((2, 2 * HEAD_DIM, WIDTH), BF),
                pltpu.VMEM((2, HEAD_DIM, WIDTH), F32),
                pltpu.VMEM((2, 8, WIDTH), F32),
            ],
        ),
        out_shape=[HEAD_F32, jax.ShapeDtypeStruct((KV_HEADS, 2, 1, WIDTH), F32)],
        compiler_params=pltpu.CompilerParams(vmem_limit_bytes=VMEM_LIMIT),
        cost_estimate=pl.CostEstimate(flops=4 * 10**9, bytes_accessed=8 * 10**6, transcendentals=8 * 10**6),
    )(info, mine, other, query)


def attend_back_kernel(
    info, mine_ref, other_ref, q_ref, dnum_ref, delta_ref, dq_ref, dmine_ref, dother_ref, keys_in_order, wide, tall, dq, dkv
):
    sort_blocks(info, (mine_ref, other_ref), keys_in_order)
    for half in range(2):
        zero = jnp.zeros((HEAD_DIM, WIDTH), BF)
        both = jnp.concatenate(
            [
                jnp.concatenate([q_ref[0, half], zero], axis=1),
                jnp.concatenate([zero, dnum_ref[0, half]], axis=1),
            ],
            axis=0,
        )
        wide[half] = both
        tall[half] = both.T
    dq[...] = jnp.zeros_like(dq)
    dkv[...] = jnp.zeros_like(dkv)

    def tile(half, step, limit):
        some = STEP // SUB
        parts = []
        for n in range(SUB):
            at = pl.ds(pl.multiple_of(step * STEP + n * some, some), some)
            keys = keys_in_order[at, :]
            scores = dot_plain(keys, wide[half])
            expo = jnp.exp(scores[:, :WIDTH])
            if limit is not None:
                expo = jnp.where(key_rows_minus_query_lanes(some) <= limit - n * some, expo, 0.0)
            grads = (expo * (scores[:, WIDTH:] - delta_ref[0, half])).astype(BF)
            pair = jnp.concatenate([grads, expo.astype(BF)], axis=1)
            dkv[at, :] += dot_plain(pair, tall[half])
            parts.append(dot_plain(keys.T[:HEAD_DIM], grads))
        dq[half] += sum(parts[1:], parts[0])

    causal_steps(info, tile)
    for half in range(2):
        dq_ref[0, half] = dq[half] * (HEAD_DIM**-0.5)
    unsort_blocks(info, dkv, (dmine_ref, dother_ref))


def attend_back(info, mine, other, query, dnum, delta, first, count):
    rows = mine.shape[0]

    def at(shape, offset):
        return pl.BlockSpec(shape, lambda g, s: (g + offset, 0, 0, 0))

    def kv_at(offset):
        return pl.BlockSpec((rows, 2 * HEAD_DIM), lambda g, s: (0, g + offset))

    head, row = (1, 2, HEAD_DIM, WIDTH), (1, 2, 1, WIDTH)
    return pl.pallas_call(
        attend_back_kernel,
        grid_spec=pltpu.PrefetchScalarGridSpec(
            num_scalar_prefetch=1,
            grid=(count,),
            in_specs=[kv_at(first), kv_at(first), at(head, first), at(head, first), at(row, first)],
            out_specs=[at(head, 0), kv_at(0), kv_at(0)],
            scratch_shapes=[
                pltpu.VMEM((SEQ_LEN, 2 * HEAD_DIM), BF),
                pltpu.VMEM((2, 2 * HEAD_DIM, 2 * WIDTH), BF),
                pltpu.VMEM((2, 2 * WIDTH, 2 * HEAD_DIM), BF),
                pltpu.VMEM((2, HEAD_DIM, WIDTH), F32),
                pltpu.VMEM((SEQ_LEN, 2 * HEAD_DIM), F32),
            ],
        ),
        out_shape=[jax.ShapeDtypeStruct((count, 2, HEAD_DIM, WIDTH), F32)]
        + [jax.ShapeDtypeStruct((rows, count * 2 * HEAD_DIM), BF)] * 2,
        compiler_params=pltpu.CompilerParams(vmem_limit_bytes=VMEM_LIMIT),
        cost_estimate=pl.CostEstimate(
            flops=2 * count * 10**9, bytes_accessed=count * 3 * 10**6, transcendentals=count * 2 * 10**6
        ),
    )(info, mine, other, query, dnum, delta)


PARTS = ((0, 60), (64, 20), (88, 20))
BLOCK = 112
SLABS = 4


def project_kernel(info, mine_ref, other_ref, normed_ref, cos_ref, sin_ref, w_ref, query_ref, kv_ref, q_rows, k_rows, v_rows, pair):
    step = pl.program_id(0)
    core = info[2]
    for at in range(8):
        lanes = slice(at * 128, at * 128 + 128)
        w_ref[0, core, :, lanes] = mine_ref[at // 4, at % 4, 0, 0]
        w_ref[0, 1 - core, :, lanes] = other_ref[at // 4, at % 4, 0, 0]
    made = dot_last(w_ref[0].reshape(2 * BLOCK, PAD), normed_ref[...])
    for (start, count), rows in zip(PARTS, (q_rows, k_rows, v_rows)):
        pair[0:count] = made[start : start + count]
        pair[count : 2 * count] = made[BLOCK + start : BLOCK + start + count]
        rows[pl.ds(pl.multiple_of(step * 2 * count, 8), 2 * count), :] = pair[0 : 2 * count]

    @pl.when(step == 7)
    def _():
        cosine, sine = cos_ref[...], sin_ref[...]

        def turned(rows, head):
            first = rows[head * 64 : head * 64 + 32]
            second = rows[head * 64 + 32 : head * 64 + 64]
            return jnp.concatenate([first * cosine - second * sine, second * cosine + first * sine], axis=0)

        for g in range(KV_HEADS):
            for r in range(GROUP):
                head = turned(q_rows, GROUP * g + r).astype(BF) * BF(HEAD_DIM**-0.5)
                for half in range(2):
                    query_ref[g, half, :, r * SPAN : (r + 1) * SPAN] = head[:, half * SPAN : (half + 1) * SPAN]
            both = jnp.concatenate([turned(k_rows, g), v_rows[g * 64 : g * 64 + 64]], axis=0)
            kv_ref[:, g * 128 : (g + 1) * 128] = both.T.astype(BF)


def whole_spec(*shape):
    return pl.BlockSpec(shape, lambda j, s: (0,) * len(shape))


SMALL_SPEC = pl.BlockSpec((2, 4, 1, 1, BLOCK, 128), lambda j, s: (0, 0, j // 2, j % 2, 0, 0))
W_SPEC = pl.BlockSpec((1, 2, BLOCK, PAD), lambda j, s: (j, 0, 0, 0))


def project(info, mine, other, normed, cosine, sine):
    rows = normed.shape[0]
    return pl.pallas_call(
        project_kernel,
        grid_spec=pltpu.PrefetchScalarGridSpec(
            num_scalar_prefetch=1,
            grid=(8,),
            in_specs=[SMALL_SPEC, SMALL_SPEC, whole_spec(rows, PAD), whole_spec(32, rows), whole_spec(32, rows)],
            out_specs=[W_SPEC, whole_spec(KV_HEADS, 2, HEAD_DIM, WIDTH), whole_spec(rows, 640)],
            scratch_shapes=[
                pltpu.VMEM((D, rows), F32),
                pltpu.VMEM((320, rows), F32),
                pltpu.VMEM((320, rows), F32),
                pltpu.VMEM((120, rows), F32),
            ],
        ),
        out_shape=[
            jax.ShapeDtypeStruct((8, 2, BLOCK, PAD), BF),
            jax.ShapeDtypeStruct((KV_HEADS, 2, HEAD_DIM, WIDTH), BF),
            jax.ShapeDtypeStruct((rows, 640), BF),
        ],
        compiler_params=pltpu.CompilerParams(vmem_limit_bytes=VMEM_LIMIT),
        cost_estimate=pl.CostEstimate(flops=10**9, bytes_accessed=8 * 10**6, transcendentals=0),
    )(info, mine, other, normed, cosine, sine)


def project_back_kernel(
    info, dq_ref, dkv_ref, normed_ref, cos_ref, sin_ref, w_ref, dn_ref, mine_ref, other_ref, q_rows, k_rows, v_rows, pair, blocks, grads
):
    step = pl.program_id(0)
    core = info[2]

    @pl.when(step == 0)
    def _():
        cosine, sine = cos_ref[...], sin_ref[...]

        def turned_back(value):
            first, second = value[:32], value[32:]
            return jnp.concatenate([first * cosine + second * sine, second * cosine - first * sine], axis=0)

        for g in range(KV_HEADS):
            for r in range(GROUP):
                lanes = slice(r * SPAN, (r + 1) * SPAN)
                head = jnp.concatenate([dq_ref[g, 0, :, lanes], dq_ref[g, 1, :, lanes]], axis=1)
                at = (GROUP * g + r) * 64
                q_rows[at : at + 64] = turned_back(head)
            both = dkv_ref[:, g * 128 : (g + 1) * 128].T
            k_rows[g * 64 : g * 64 + 64] = turned_back(both[:64])
            v_rows[g * 64 : g * 64 + 64] = both[64:]
        blocks[...] = jnp.zeros_like(blocks)
        dn_ref[...] = jnp.zeros_like(dn_ref)

    for n in range(SLABS):
        base = 2 * BLOCK * n
        for (start, count), rows in zip(PARTS, (q_rows, k_rows, v_rows)):
            at = pl.multiple_of((SLABS * step + n) * 2 * count, 8)
            pair[0 : 2 * count] = rows[pl.ds(at, 2 * count), :]
            blocks[base + start : base + start + count] = pair[0:count]
            blocks[base + BLOCK + start : base + BLOCK + start + count] = pair[count : 2 * count]
    block = blocks[...].astype(BF)
    dn_ref[...] += dot_first(block, w_ref[...].reshape(2 * SLABS * BLOCK, PAD))
    grads[...] = dot_plain(block, normed_ref[...]).astype(BF).reshape(SLABS, 2, BLOCK, PAD)
    for n in range(SLABS):
        for at in range(8):
            lanes = slice(at * 128, at * 128 + 128)
            mine_ref[at // 4, at % 4, n // 2, n % 2] = grads[n, core, :, lanes]
            other_ref[at // 4, at % 4, n // 2, n % 2] = grads[n, 1 - core, :, lanes]


def project_back(info, dq, dkv, normed, cosine, sine, w_all):
    rows = normed.shape[0]
    small = jax.ShapeDtypeStruct((2, 4, 4, 2, BLOCK, 128), BF)
    return pl.pallas_call(
        project_back_kernel,
        grid_spec=pltpu.PrefetchScalarGridSpec(
            num_scalar_prefetch=1,
            grid=(8 // SLABS,),
            in_specs=[
                whole_spec(*dq.shape),
                whole_spec(rows, 640),
                whole_spec(rows, PAD),
                whole_spec(32, rows),
                whole_spec(32, rows),
                pl.BlockSpec((SLABS, 2, BLOCK, PAD), lambda j, s: (j, 0, 0, 0)),
            ],
            out_specs=[whole_spec(rows, PAD)]
            + [pl.BlockSpec((2, 4, SLABS // 2, 2, BLOCK, 128), lambda j, s: (0, 0, j, 0, 0, 0))] * 2,
            scratch_shapes=[
                pltpu.VMEM((D, rows), F32),
                pltpu.VMEM((320, rows), F32),
                pltpu.VMEM((320, rows), F32),
                pltpu.VMEM((120, rows), F32),
                pltpu.VMEM((2 * SLABS * BLOCK, rows), F32),
                pltpu.VMEM((SLABS, 2, BLOCK, PAD), BF),
            ],
        ),
        out_shape=[jax.ShapeDtypeStruct((rows, PAD), F32), small, small],
        compiler_params=pltpu.CompilerParams(vmem_limit_bytes=VMEM_LIMIT),
        cost_estimate=pl.CostEstimate(flops=2 * 10**9, bytes_accessed=10 * 10**6, transcendentals=0),
    )(info, dq, dkv, normed, cosine, sine, w_all)


def feed_kernel(
    gate_ref, up_ref, down_ref, n_mine, n_other, dy_mine, dy_other,
    fed_mine, fed_other, dn_mine, dn_other, grad_ref, normed, dy, wg, wu, wd, fed, dn
):
    step = pl.program_id(0)
    rows = n_mine.shape[0]

    @pl.when(step == 0)
    def _():
        normed[:rows] = n_mine[...]
        normed[rows:] = n_other[...]
        dy[:rows] = dy_mine[...]
        dy[rows:] = dy_other[...]
        fed[...] = jnp.zeros_like(fed)
        dn[...] = jnp.zeros_like(dn)

    for group in range(4):
        part = slice(group * 160, group * 160 + 160)
        for at in range(8):
            lanes = slice(at * 128, at * 128 + 128)
            wg[part, lanes] = gate_ref[at % 4, group // 2, group % 2, at // 4]
            wu[part, lanes] = up_ref[at % 4, group // 2, group % 2, at // 4]
            wd[part, lanes] = down_ref[group, at // 2, at % 2, 0]
    gate = dot_last(normed[...], wg[...])
    upward = dot_last(normed[...], wu[...])
    dact = dot_last(dy[...], wd[...])
    sigma = jax.nn.sigmoid(gate)
    silu_gate = gate * sigma
    active = (silu_gate * upward).astype(BF)
    dgate = (dact * upward * sigma * (1.0 + gate * (1.0 - sigma))).astype(BF)
    dup = (dact * silu_gate).astype(BF)
    fed[...] += dot_plain(active, wd[...])
    dn[...] += dot_plain(dgate, wg[...]) + dot_plain(dup, wu[...])
    g_gate = dot_first(dgate, normed[...]).astype(BF)
    g_up = dot_first(dup, normed[...]).astype(BF)
    g_down = dot_first(active, dy[...]).astype(BF)
    for group in range(4):
        part = slice(group * 160, group * 160 + 160)
        for at in range(8):
            lanes = slice(at * 128, at * 128 + 128)
            grad_ref[at % 4, 2 * step + group // 2, group % 2, at // 4, 0:160] = g_gate[part, lanes]
            grad_ref[at % 4, 2 * step + group // 2, group % 2, at // 4, 160:320] = g_up[part, lanes]
            grad_ref[group, at // 2, at % 2, step, 320:480] = g_down[part, lanes]

    @pl.when(step == 1)
    def _():
        fed_mine[...] = fed[:rows]
        fed_other[...] = fed[rows:].astype(BF)
        dn_mine[...] = dn[:rows]
        dn_other[...] = dn[rows:].astype(BF)


def feed(big, n_mine, n_other, dy_mine, dy_other):
    rows = n_mine.shape[0]
    by_plane = (4, 2, 2, 2, 160, 128)

    def flat(*shape):
        return pl.BlockSpec(shape, lambda k: (0,) * len(shape))

    return pl.pallas_call(
        feed_kernel,
        grid=(2,),
        in_specs=[
            pl.BlockSpec(by_plane, lambda k: (0, k, 0, 0, 0, 0)),
            pl.BlockSpec(by_plane, lambda k: (0, k, 0, 0, 1, 0)),
            pl.BlockSpec((4, 4, 2, 1, 160, 128), lambda k: (0, 0, 0, k, 2, 0)),
        ]
        + [flat(rows, PAD)] * 4,
        out_specs=[flat(rows, PAD)] * 4 + [flat(4, 4, 2, 2, 480, 128)],
        out_shape=[
            jax.ShapeDtypeStruct((rows, PAD), F32),
            jax.ShapeDtypeStruct((rows, PAD), BF),
            jax.ShapeDtypeStruct((rows, PAD), F32),
            jax.ShapeDtypeStruct((rows, PAD), BF),
            jax.ShapeDtypeStruct((4, 4, 2, 2, 480, 128), BF),
        ],
        scratch_shapes=[pltpu.VMEM((2 * rows, PAD), BF)] * 2
        + [pltpu.VMEM((FEED, PAD), BF)] * 3
        + [pltpu.VMEM((2 * rows, PAD), F32)] * 2,
        compiler_params=pltpu.CompilerParams(vmem_limit_bytes=VMEM_LIMIT),
        cost_estimate=pl.CostEstimate(flops=12 * 10**9, bytes_accessed=22 * 10**6, transcendentals=10**6),
    )(big, big, big, n_mine, n_other, dy_mine, dy_other)


def project_out_kernel(info, o_ref, mine_ref, other_ref, x_ref, gain_ref, hidden_ref, normed_ref, w_ref, ob_ref, rows):
    core = info[2]
    for s in range(8):
        for j in range(8):
            lanes = slice(j * 128, j * 128 + 128)
            w_ref[s, core, :, lanes] = mine_ref[s // 4, s % 4, j // 2, j % 2]
            w_ref[s, 1 - core, :, lanes] = other_ref[s // 4, s % 4, j // 2, j % 2]
    for head in range(HEADS):
        g, r = head // GROUP, head % GROUP
        for half in range(2):
            piece = o_ref[g, half, :, r * SPAN : (r + 1) * SPAN]
            rows[head * 64 : head * 64 + 64, half * SPAN : (half + 1) * SPAN] = piece
    ob_ref[...] = jnp.zeros_like(ob_ref)
    for n in range(16):
        ob_ref[n * 64 : n * 64 + 60] = rows[n * 60 : n * 60 + 60].astype(BF)
    hidden = x_ref[...] + dot_first(ob_ref[...], w_ref[...].reshape(PAD, PAD))
    hidden_ref[...] = hidden
    inverse = lax.rsqrt(jnp.sum(hidden * hidden, axis=-1, keepdims=True) / D + EPS)
    normed_ref[...] = (hidden * inverse * gain_ref[...]).astype(BF)


def one_call(kernel, info, args, outs, scratch, flops):
    return pl.pallas_call(
        kernel,
        in_specs=[pl.BlockSpec(memory_space=pltpu.SMEM)] + [pl.BlockSpec(memory_space=pltpu.VMEM)] * len(args),
        out_specs=[pl.BlockSpec(memory_space=pltpu.VMEM)] * len(outs),
        out_shape=[jax.ShapeDtypeStruct(shape, kind) for shape, kind in outs],
        scratch_shapes=scratch,
        compiler_params=pltpu.CompilerParams(vmem_limit_bytes=VMEM_LIMIT),
        cost_estimate=pl.CostEstimate(flops=flops, bytes_accessed=10 * 10**6, transcendentals=0),
    )(info, *args)


def project_out(info, attended, mine, other, layer_input, gain):
    rows = layer_input.shape[0]
    return one_call(
        project_out_kernel,
        info,
        (attended, mine, other, layer_input, gain),
        [((rows, PAD), F32), ((rows, PAD), BF), ((8, 2, 64, PAD), BF), ((PAD, rows), BF)],
        [pltpu.VMEM((D, rows), F32)],
        10**9,
    )


def between_kernel(
    info, dn_ref, dn_other_ref, hidden_ref, gain_ref, dy_ref, w_ref, ob_ref, o_ref, total_ref,
    dh_ref, dnum_ref, delta_ref, mine_ref, other_ref, gain_grad_ref, rows, grads
):
    core = info[2]
    hidden, gain = hidden_ref[...], gain_ref[...]
    inverse = lax.rsqrt(jnp.sum(hidden * hidden, axis=-1, keepdims=True) / D + EPS)
    unit = hidden * inverse
    dn = dn_ref[...] + dn_other_ref[...].astype(F32)
    back, gain_grad = norm_back(dn, unit, inverse, gain)
    gain_grad_ref[...] = gain_grad[None]
    dh = dy_ref[...].astype(F32) + back
    dh_ref[...] = dh
    dh_low = dh.astype(BF)
    dob = dot_last(w_ref[...].reshape(PAD, PAD), dh_low)
    for n in range(16):
        rows[n * 60 : n * 60 + 60] = dob[n * 64 : n * 64 + 60].astype(BF).astype(F32)
    for head in range(HEADS):
        g, r = head // GROUP, head % GROUP
        for half in range(2):
            lanes = slice(r * SPAN, (r + 1) * SPAN)
            piece = rows[head * 64 : head * 64 + 64, half * SPAN : (half + 1) * SPAN]
            total = total_ref[g, half, :, lanes]
            dnum_ref[g, half, :, lanes] = (piece / total).astype(BF)
            summed = jnp.sum(piece * o_ref[g, half, :, lanes], axis=0, keepdims=True)
            delta_ref[g, half, :, lanes] = summed / total
    grads[...] = dot_plain(ob_ref[...], dh_low).astype(BF).reshape(8, 2, 64, PAD)
    for s in range(8):
        for j in range(8):
            lanes = slice(j * 128, j * 128 + 128)
            mine_ref[s // 4, s % 4, j // 2, j % 2] = grads[s, core, :, lanes]
            other_ref[s // 4, s % 4, j // 2, j % 2] = grads[s, 1 - core, :, lanes]


def between(info, dn, dn_other, hidden, gain, dy, w_out, attended_low, attended, total):
    rows = hidden.shape[0]
    return one_call(
        between_kernel,
        info,
        (dn, dn_other, hidden, gain, dy, w_out, attended_low, attended, total),
        [
            ((rows, PAD), F32),
            ((KV_HEADS, 2, HEAD_DIM, WIDTH), BF),
            ((KV_HEADS, 2, 1, WIDTH), F32),
            ((2, 4, 4, 2, 64, 128), BF),
            ((2, 4, 4, 2, 64, 128), BF),
            ((1, PAD), F32),
        ],
        [pltpu.VMEM((D, rows), F32), pltpu.VMEM((8, 2, 64, PAD), BF)],
        2 * 10**9,
    )


def pad_rows(value, count):
    return jnp.pad(value, ((0, count - value.shape[0]), (0, 0)))


def norm_forward(value, gain):
    inverse = lax.rsqrt(jnp.sum(value * value, axis=-1, keepdims=True) / D + EPS)
    unit = value * inverse
    return unit, inverse, (unit * gain).astype(BF)


def norm_back(grad, unit, inverse, gain):
    scaled = grad * gain
    inner = jnp.sum(scaled * unit, axis=-1, keepdims=True) / D
    return inverse * (scaled - unit * inner), jnp.sum(grad * unit, axis=0)


def body(
    tokens,
    w_query,
    w_key,
    w_value,
    w_out,
    w_gate,
    w_up,
    w_down,
    attention_norm_gain,
    feedforward_norm_gain,
    span_order,
    positions,
    out_grad,
):
    rows = tokens.shape[0]
    core = lax.axis_index("c")
    me = lax.axis_index(("x", "zh", "c"))

    small = jnp.concatenate([pad_rows(w_query.T, 64), pad_rows(w_key.T, 24), pad_rows(w_value.T, 24)], axis=0)
    small = pad_lanes(small)
    mixed = jnp.concatenate([w_down.reshape(2, 160, 60), w_out.reshape(2, 60, 60)], axis=1)
    mixed = lax.all_to_all(mixed, "c", 0, 0, tiled=True)
    mixed = jnp.concatenate([mixed[0], mixed[1]], axis=1)
    big = pad_lanes(jnp.concatenate([w_gate.T, w_up.T, mixed[:160]], axis=0))
    big = lax.all_gather(big, ("x",) + LINE, axis=0, tiled=True)
    w_out_block = pad_rows(pad_lanes(mixed[160:]), 64)

    order = span_order[0]
    own_pair = lax.dynamic_slice_in_dim(order, 2 * me, 2)
    own_low_half = (own_pair[0] > own_pair[1]).astype(jnp.int32)
    spans = order.reshape(8, 2, 2)
    info = jnp.concatenate(
        [
            jnp.stack([own_low_half, jnp.minimum(own_pair[0], own_pair[1]), core.astype(jnp.int32)]),
            jnp.zeros((5,), jnp.int32),
            lax.dynamic_index_in_dim(spans, core, 1, keepdims=False).reshape(16),
            lax.dynamic_index_in_dim(spans, 1 - core, 1, keepdims=False).reshape(16),
        ]
    ).astype(jnp.int32)
    place = jnp.concatenate(
        [
            lax.dynamic_slice_in_dim(positions[0], own_pair[0] * SPAN, SPAN, 0),
            lax.dynamic_slice_in_dim(positions[0], own_pair[1] * SPAN, SPAN, 0),
        ]
    )
    half_dim = HEAD_DIM // 2
    freq = jnp.power(ROPE_BASE, -jnp.arange(half_dim, dtype=F32) / half_dim)
    angle = freq[:, None] * place.astype(F32)[None, :]
    cosine, sine = jnp.cos(angle), jnp.sin(angle)

    gain_one = pad_width(attention_norm_gain[None])
    gain_two = pad_width(feedforward_norm_gain[None])
    layer_input = pad_width(tokens).astype(F32)
    dy = pad_width(out_grad)
    dy_other = other_core(dy)

    unit_one, inverse_one, normed_one = norm_forward(layer_input, gain_one)
    small, normed_one, info, cosine, sine = lax.optimization_barrier((small, normed_one, info, cosine, sine))
    small = to_chips(jnp.broadcast_to(small, (64, BLOCK, 128)))
    small = small.reshape(2, 4, 4, 2, BLOCK, 128)
    small_other = other_core(small)
    big, _ = lax.optimization_barrier((big, small_other))
    big = lax.all_gather(big, "y", axis=0, tiled=True).reshape(4, 4, 2, 2, 480, 128)
    w_all, query, kv_local = project(info, small, small_other, normed_one, cosine, sine)

    kv = lax.all_to_all(jnp.broadcast_to(kv_local, (8, rows, 640)), SEQ, 0, 0, tiled=True)
    kv = kv.reshape(8 * rows, 640)
    kv_other = other_core(kv)

    w_out_block, kv, kv_other = lax.optimization_barrier((w_out_block, kv, kv_other))
    w_out_mine = to_chips(jnp.broadcast_to(w_out_block, (64, 64, 128)))
    attended, total = attend(info, kv, kv_other, query)
    w_out_mine, attended = lax.optimization_barrier((w_out_mine, attended))
    w_out_mine = w_out_mine.reshape(2, 4, 4, 2, 64, 128)
    hidden, normed_two, w_out_full, attended_low = project_out(
        info, attended, w_out_mine, other_core(w_out_mine), layer_input, gain_two
    )
    big, normed_two = lax.optimization_barrier((big, normed_two))
    fed, fed_other, dn_two, dn_other, g_big = feed(big, normed_two, other_core(normed_two), dy, dy_other)
    dh, dnum, delta, g_out, g_out_other, gain_two_grad = between(
        info, dn_two, other_core(dn_other), hidden, gain_two, dy, w_out_full, attended_low, attended, total
    )
    result = cut_width((hidden + (fed + other_core(fed_other).astype(F32))).astype(BF))

    g_big = lax.psum_scatter(g_big.reshape(64 * 480, 128), "y", scatter_dimension=0, tiled=True)

    dq, dkv, dkv_other = attend_back(info, kv, kv_other, query, dnum, delta, 0, KV_HEADS)
    dkv = (dkv.astype(F32) + other_core(dkv_other).astype(F32)).astype(BF)
    g_out = (g_out.astype(F32) + other_core(g_out_other).astype(F32)).astype(BF).reshape(64, 64, 128)
    dkv, g_out = lax.optimization_barrier((dkv, g_out))
    dkv = lax.all_to_all(dkv.reshape(8, rows, 640), SEQ, 0, 0, tiled=True)
    dkv, g_big = lax.optimization_barrier((dkv, g_big))
    g_big = lax.psum_scatter(g_big, "x", scatter_dimension=0, tiled=True)
    g_big = sum_line(g_big.reshape(4, 480, 128))
    dkv = jnp.sum(dkv.astype(F32), axis=0)

    dn_one, g_small, g_other = project_back(info, dq, dkv, normed_one, cosine, sine, w_all)
    back_one, gain_one_grad = norm_back(dn_one, unit_one, inverse_one, gain_one)
    input_grad = cut_width((dh + back_one).astype(BF))

    g_small = (g_small.astype(F32) + other_core(g_other).astype(F32)).astype(BF).reshape(64, BLOCK, 128)
    gain_grads = jnp.stack([gain_one_grad, gain_two_grad[0]])
    gain_grads = (gain_grads + other_core(gain_grads)).astype(BF).reshape(16, 128)
    spare = jnp.zeros((176, 128), BF)
    for n, at in enumerate((60, 84, 108, 172)):
        spare = lax.dynamic_update_slice(spare, gain_grads[4 * n : 4 * n + 4], (at, 0))
    last = jnp.concatenate([g_small, g_out], axis=1) + spare

    last, _ = lax.optimization_barrier((to_chips(last), g_big))
    last = jnp.sum(last.astype(F32), axis=0)
    gain_grads = jnp.concatenate([last[at : at + 4] for at in (60, 84, 108, 172)], axis=0)
    gain_grads = cut_width(gain_grads.reshape(2, PAD))

    def all_rows(part):
        halves = part[:, :120].reshape(part.shape[0], 2, 60)
        keep = lax.dynamic_index_in_dim(halves, core, 1, keepdims=False)
        came = other_core(lax.dynamic_index_in_dim(halves, 1 - core, 1, keepdims=False))
        first = core == 0
        return jnp.concatenate([jnp.where(first, keep, came), jnp.where(first, came, keep)], axis=0)

    return (
        result,
        input_grad,
        last[:60, :120].T,
        last[64:84, :120].T,
        last[88:108, :120].T,
        all_rows(last[112:172]),
        g_big[:160, :120].T,
        g_big[160:320, :120].T,
        all_rows(g_big[320:]),
        gain_grads[0],
        gain_grads[1],
    )


def solution(mesh):
    fine = Mesh(mesh.devices.reshape(2, 4, 4, 2, 2), ("zl", "y", "x", "zh", "c"))
    shard, ctx = ("zl", "y"), ("x", "zh", "c")
    both = shard + ctx
    return jax.shard_map(
        body,
        mesh=fine,
        in_specs=(P(both, None),)
        + (P(shard, ctx),) * 7
        + (P(), P(), P(shard, None), P(shard, None), P(both, None)),
        out_specs=(P(both, None), P(both, None)) + (P(shard, ctx),) * 7 + (P(), P()),
        check_vma=False,
    )
```
